32 devices in a mesh: tm: 4 (over y, core), patch: 8 (over z, x).
Axes of the slice: x: 2, y: 2, z: 4, core: 2. Of those that a mesh axis runs over, the one named last changes fastest.
Arguments:
- query_vectors: bfloat16 [16, 4, 64, 2048], P(None, 'tm', 'patch'), may hold values from -32 to 32
- key_vectors: bfloat16 [16, 4, 64, 2048], P(None, 'tm', 'patch'), may hold values from -32 to 32
- value_vectors: bfloat16 [16, 4, 64, 2048], P(None, 'tm', 'patch'), may hold values from -6 to 6
- grad_output: bfloat16 [16, 4, 64, 2048], P(None, 'tm', 'patch'), may hold values from -6 to 6
- time_bias: float32 [16, 4], replicated, may hold values from -26 to 2
Outputs:
- grad_queries: bfloat16 [16, 4, 64, 2048], P(None, 'tm', 'patch')
- grad_keys: bfloat16 [16, 4, 64, 2048], P(None, 'tm', 'patch')
- grad_values: bfloat16 [16, 4, 64, 2048], P(None, 'tm', 'patch')
- grad_bias: float32 [16, 4], replicated
The draws below stay inside these ranges and needn't reach their ends.
All inputs are finite; a program needn't handle non-finite values.
Results may differ from the reference program's by a relative error of at most 0.0069.
Values may be sent and summed in bfloat16 or wider, within the bound.
No kernel may reach another device: no remote copies, remote signals or barrier semaphores. Data moves between devices by JAX's collectives and lax.ppermute only.
A program may use at most 64 MiB of HBM per device.

```python
import math
import jax
import jax.numpy as jnp
from jax import lax

H = 16
HD = 128
CLIPS = 16
FRAMES = 4
PATCHES = 64


def shared_base(key):
    ground_key = jax.random.fold_in(key, 101)
    ground = jnp.clip(jax.random.normal(ground_key, (CLIPS, FRAMES, PATCHES, H * HD), jnp.float32), -5.0, 5.0)
    return ground


def draw_query_vectors(key, part):
    ground = shared_base(key)
    return ground.astype(jnp.bfloat16)


def draw_key_vectors(key, part):
    key = jax.random.fold_in(key, 5)
    fresh_draw = jnp.clip(jax.random.normal(key, (CLIPS, FRAMES, PATCHES, H * HD), jnp.float32), -5.0, 5.0)
    return fresh_draw.astype(jnp.bfloat16)


def draw_time_bias(key, part):
    key = jax.random.fold_in(key, 9)
    slope_key = jax.random.fold_in(key, 1)
    jitter_key = jax.random.fold_in(key, 2)
    unit = jax.random.uniform(slope_key, (H, 1), jnp.float32, 0.0, 1.0)
    slopes = jnp.exp(jnp.log(0.03) + unit * (jnp.log(1.5) - jnp.log(0.03)))
    jitter = jnp.clip(0.5 * jax.random.normal(jitter_key, (H, FRAMES), jnp.float32), -1.5, 1.5)
    offsets = jnp.arange(FRAMES, dtype=jnp.float32)[None, :]
    return -slopes * offsets + jitter


def level_of(stream_key, dims, cuts, least, high):
    gain, own = 1.0, jax.random.fold_in(stream_key, 6)
    for dim, blocks in cuts:
        steps = jnp.exp(jax.random.uniform(jax.random.fold_in(own, dim), (blocks,), jnp.float32, least / len(cuts), high / len(cuts)))
        gain = gain * jnp.repeat(steps, dims[dim] // blocks).reshape([-1 if axis == dim else 1 for axis in range(len(dims))])
    return gain


def normal_values(own_key, extent, spread, reach, shards=(), kind=jnp.bfloat16):
    drawn = spread * jax.random.normal(own_key, extent, jnp.float32)
    if shards:
        drawn = drawn * level_of(own_key, extent, shards, -0.22, 0.18)
    return jnp.clip(drawn, -reach, reach).astype(kind)


def setup_inputs(seed: int = 0) -> dict:
    streams_of = jax.random.split(jax.random.key(seed), 6)
    return {
        "query_vectors": draw_query_vectors(jax.random.fold_in(streams_of[5], 71), 0),
        "key_vectors": draw_key_vectors(jax.random.fold_in(streams_of[5], 71), 0),
        "value_vectors": normal_values(streams_of[2], (CLIPS, FRAMES, PATCHES, H * HD), 1.0, 6.0, ((1, 4), (2, 8))),
        "grad_output": normal_values(streams_of[3], (CLIPS, FRAMES, PATCHES, H * HD), 1.0, 6.0, ((1, 4), (2, 8))),
        "time_bias": draw_time_bias(jax.random.fold_in(streams_of[5], 71), 0),
    }


def score_table(bias_rows, frames):
    steps = jnp.arange(frames, dtype=jnp.int32)
    offsets = steps[:, None] - steps[None, :]
    onehot = (offsets[:, :, None] == steps[None, None, :]).astype(jnp.float32)
    table = jnp.einsum('hd,tud->htu', bias_rows, onehot, precision=lax.Precision.HIGHEST)
    return (table, offsets >= 0, onehot)

def attend_ref(query_heads, key_heads, value_heads, grad_heads, bias_rows):
    frames = query_heads.shape[1]
    score_scale = 1.0 / math.sqrt(query_heads.shape[4])
    table, causal, onehot = score_table(bias_rows, frames)
    query_wide = query_heads.astype(jnp.float32)
    key_wide = key_heads.astype(jnp.float32)
    value_wide = value_heads.astype(jnp.float32)
    grad_wide = grad_heads.astype(jnp.float32)
    highest = lax.Precision.HIGHEST
    scores = jnp.einsum('atxhd,auxhd->axhtu', query_wide, key_wide, precision=highest) * score_scale + table[None, None]
    scores = jnp.where(causal, scores, -jnp.inf)
    row_max = lax.optimization_barrier(jnp.max(scores, axis=-1, keepdims=True))
    expon = jnp.exp(scores - row_max)
    weights = expon / lax.optimization_barrier(jnp.sum(expon, axis=-1, keepdims=True))
    weights_wide = lax.optimization_barrier(weights.astype(jnp.bfloat16)).astype(jnp.float32)
    attended = jnp.einsum('axhtu,auxhd->atxhd', weights_wide, value_wide, precision=highest)
    rowdot = jnp.einsum('atxhd,atxhd->axht', grad_wide, attended, precision=highest)
    grad_weights = jnp.einsum('atxhd,auxhd->axhtu', grad_wide, value_wide, precision=highest)
    grad_scores = weights * (grad_weights - rowdot[..., None])
    bias_terms = jnp.einsum('axhtu,tud->axhd', grad_scores, onehot, precision=highest)
    grad_low = lax.optimization_barrier(grad_scores.astype(jnp.bfloat16)).astype(jnp.float32)
    grad_query = (jnp.einsum('axhtu,auxhd->atxhd', grad_low, key_wide, precision=highest) * score_scale).astype(jnp.bfloat16)
    grad_key = (jnp.einsum('axhtu,atxhd->auxhd', grad_low, query_wide, precision=highest) * score_scale).astype(jnp.bfloat16)
    grad_value = jnp.einsum('axhtu,atxhd->auxhd', weights_wide, grad_wide, precision=highest).astype(jnp.bfloat16)
    return (grad_query, grad_key, grad_value, bias_terms)

def reference(query_vectors, key_vectors, value_vectors, grad_output, time_bias):
    head_count = time_bias.shape[0]
    head_dim = query_vectors.shape[3] // head_count
    flat_shape = query_vectors.shape[1:]

    def per_clip(clip_block):
        split_heads = [item.reshape((1, item.shape[0], item.shape[1], head_count, head_dim)) for item in clip_block]
        grad_query, grad_key, grad_value, bias_terms = attend_ref(split_heads[0], split_heads[1], split_heads[2], split_heads[3], time_bias)
        return (grad_query.reshape(flat_shape), grad_key.reshape(flat_shape), grad_value.reshape(flat_shape), lax.optimization_barrier(jnp.sum(bias_terms, axis=(0, 1))))
    grad_query, grad_key, grad_value, bias_terms = lax.map(per_clip, (query_vectors, key_vectors, value_vectors, grad_output))
    return (grad_query, grad_key, grad_value, lax.optimization_barrier(jnp.sum(bias_terms, axis=0)))
```

```python
import functools
import math

import jax
import jax.numpy as jnp
from jax import lax
from jax.experimental import pallas as pl
from jax.experimental.pallas import tpu as pltpu
from jax.sharding import PartitionSpec as P

LANES = 128
TILE = 16
COPY_ROWS = 16
LITTLE = pl.CostEstimate(flops=1, bytes_accessed=1, transcendentals=0)
CHUNKS = 2


def score_table(bias_rows, frames):
    steps = jnp.arange(frames, dtype=jnp.int32)
    offsets = steps[:, None] - steps[None, :]
    onehot = (offsets[:, :, None] == steps[None, None, :]).astype(jnp.float32)
    table = jnp.einsum("hd,tud->htu", bias_rows, onehot, precision=lax.Precision.HIGHEST)
    return (table, offsets >= 0, onehot)


def attend_back(query_heads, key_heads, value_heads, grad_heads, bias_rows):
    frames = query_heads.shape[1]
    score_scale = 1.0 / math.sqrt(query_heads.shape[4])
    table, causal, onehot = score_table(bias_rows, frames)
    wide = jnp.float32
    scores = (
        jnp.einsum("atxhd,auxhd->axhtu", query_heads, key_heads, preferred_element_type=wide)
        * score_scale
        + table[None, None]
    )
    scores = jnp.where(causal, scores, -jnp.inf)
    row_max = jnp.max(scores, axis=-1, keepdims=True)
    expon = jnp.exp(scores - row_max)
    weights = expon / jnp.sum(expon, axis=-1, keepdims=True)
    weights_low = weights.astype(jnp.bfloat16)
    attended = jnp.einsum(
        "axhtu,auxhd->atxhd", weights_low, value_heads, preferred_element_type=wide
    )
    rowdot = jnp.einsum("atxhd,atxhd->axht", grad_heads, attended, preferred_element_type=wide)
    grad_weights = jnp.einsum(
        "atxhd,auxhd->axhtu", grad_heads, value_heads, preferred_element_type=wide
    )
    grad_scores = weights * (grad_weights - rowdot[..., None])
    bias_terms = jnp.einsum("axhtu,tud->axhd", grad_scores, onehot, precision=lax.Precision.HIGHEST)
    grad_low = grad_scores.astype(jnp.bfloat16)
    grad_query = (
        jnp.einsum("axhtu,auxhd->atxhd", grad_low, key_heads, preferred_element_type=wide)
        * score_scale
    ).astype(jnp.bfloat16)
    grad_key = (
        jnp.einsum("axhtu,atxhd->auxhd", grad_low, query_heads, preferred_element_type=wide)
        * score_scale
    ).astype(jnp.bfloat16)
    grad_value = jnp.einsum(
        "axhtu,atxhd->auxhd", weights_low, grad_heads, preferred_element_type=wide
    ).astype(jnp.bfloat16)
    return (grad_query, grad_key, grad_value, bias_terms)


def sum_everywhere(value, sizes):
    for axis, size in sizes:
        if size & (size - 1):
            value = lax.psum(value, axis)
            continue
        step = 1
        while step < size:
            other = lax.ppermute(value, axis, [(i, i ^ step) for i in range(size)])
            value = value + other
            step *= 2
    return value


def by_heads(query_vectors, key_vectors, value_vectors, grad_output, time_bias, sizes):
    head_count = time_bias.shape[0]
    frames = time_bias.shape[1]
    head_dim = query_vectors.shape[3] // head_count
    split_shape = query_vectors.shape[:3] + (head_count, head_dim)
    local_heads = head_count // lax.axis_size("tm")
    first_head = lax.axis_index("tm") * local_heads
    bias_rows = lax.dynamic_slice_in_dim(time_bias, first_head, local_heads, 0)
    spread = [
        lax.all_to_all(item.reshape(split_shape), "tm", split_axis=3, concat_axis=1, tiled=True)
        for item in (query_vectors, key_vectors, value_vectors, grad_output)
    ]
    *grads, bias_terms = attend_back(*spread, bias_rows)
    grads = [
        lax.all_to_all(item, "tm", split_axis=1, concat_axis=3, tiled=True).reshape(
            query_vectors.shape
        )
        for item in grads
    ]
    partial = lax.dynamic_update_slice_in_dim(
        jnp.zeros((head_count, frames), jnp.float32),
        jnp.sum(bias_terms, axis=(0, 1)),
        first_head,
        0,
    )
    return (*grads, sum_everywhere(partial, sizes))


def pair_dots(queries, keys, grads, values, pairs, heads):
    place = lax.broadcasted_iota(jnp.int32, (TILE, LANES), 1)
    held = [jnp.zeros((TILE, LANES), jnp.float32)] * (2 * len(pairs))
    for head in range(heads):
        at = slice(head * LANES, (head + 1) * LANES)
        here = place == head
        load = lambda refs: [ref[at].astype(jnp.float32) for ref in refs]
        q, k, o, v = load(queries), load(keys), load(grads), load(values)
        for j, (t, u) in enumerate(pairs):
            score = jnp.sum(q[t] * k[u], axis=1, keepdims=True)
            held[j] = jnp.where(here, score, held[j])
            gain = jnp.sum(o[t] * v[u], axis=1, keepdims=True)
            held[len(pairs) + j] = jnp.where(here, gain, held[len(pairs) + j])
    return held


def over_tiles(rows, body):
    pl.loop(0, rows // TILE)(lambda i: body(i * TILE))


def tile_at(start):
    return pl.ds(pl.multiple_of(start, TILE), TILE)


class Shifted:
    def __init__(self, ref, start):
        self.ref, self.start = ref, start

    def at_rows(self, row):
        return View(self.ref, tile_at(self.start + row))


class View:
    def __init__(self, ref, rows):
        self.ref, self.rows = ref, rows

    def __getitem__(self, lanes):
        return self.ref[self.rows, lanes]

    def __setitem__(self, lanes, value):
        self.ref[self.rows, lanes] = value


def tiles_of(refs, row):
    return tuple(ref.at_rows(row) for ref in refs)


def shifted(refs, start):
    return tuple(Shifted(ref, start) for ref in refs)


def soft_row(scores, gains):
    top = functools.reduce(jnp.maximum, scores)
    expon = [jnp.exp(item - top) for item in scores]
    total = functools.reduce(jnp.add, expon)
    weights = [item / total for item in expon]
    low = [item.astype(jnp.bfloat16) for item in weights]
    rowdot = functools.reduce(
        jnp.add, [a.astype(jnp.float32) * g for a, g in zip(low, gains)]
    )
    grads = [w * (g - rowdot) for w, g in zip(weights, gains)]
    return low, grads


LOCAL = ((0, 0), (1, 0), (1, 1))
CROSS = ((0, 0), (0, 1), (1, 0), (1, 1))


def unpack(packed, heads):
    return [packed if j == 0 else pltpu.roll(packed, LANES - heads * j, axis=1) for j in range(6)]


def bias_lines(terms):
    lines = []
    for items in terms:
        lines.append(
            jnp.sum(functools.reduce(jnp.add, items), axis=0, keepdims=True)
            if items
            else jnp.zeros((1, LANES), jnp.float32)
        )
    return jnp.concatenate(lines + [jnp.zeros((4, LANES), jnp.float32)], axis=0)


def early_rows(diag, scale, offset):
    score = lambda j, d: diag[j] * scale + offset[d]
    row0 = soft_row([score(0, 0)], [diag[3]])
    row1 = soft_row([score(1, 1), score(2, 0)], [diag[4], diag[5]])
    return row0, row1


def my_place():
    me = lax.axis_index("tm")
    return lax.rem(me, 2), lax.div(me, 2)


def with_frames(own, other, work):
    core, chip = my_place()
    for at_chip in range(2):
        pl.when((chip == at_chip) & (core == 0))(functools.partial(work, at_chip, own, other))
        pl.when((chip == at_chip) & (core == 1))(functools.partial(work, at_chip, other, own))


def chunk_start(chunk, size):
    return jnp.where(my_place()[1] == 0, chunk, CHUNKS - 1 - chunk) * size


def sent_start(chunk, size):
    return jnp.where(my_place()[1] == 1, chunk, CHUNKS - 1 - chunk) * size


def copy_rows(sources, start, out, sems, rows):
    copies = []
    for j, ref in enumerate(sources):
        for row in range(0, out.shape[1], rows):
            copies.append(
                pltpu.make_async_copy(
                    ref.at[pl.ds(pl.multiple_of(start + row, rows), rows)],
                    out.at[j, pl.ds(row, rows)],
                    sems.at[len(copies)],
                )
            )
    for copy in copies:
        copy.start()
    for copy in copies:
        copy.wait()


def take_far(refs, row, outs):
    chip = my_place()[1]

    def take(places):
        for out, place in zip(outs, places):
            for step in range(0, out.shape[0], TILE):
                out[step : step + TILE, : refs[place].shape[1]] = refs[place][
                    tile_at(row + step), :
                ]

    pl.when(chip == 0)(lambda: take((1, 2)))
    pl.when(chip == 1)(lambda: take((0, 3)))


def fetch_theirs_kernel(q, k, v, o, near, other, sems):
    half, size = near.shape[1], other.shape[1]
    copy_rows((q, k, v, o), (1 - my_place()[0]) * half, near, sems, COPY_ROWS)
    take_far(planes(near), sent_start(0, size), planes(other))


def fetch_mine_kernel(q, k, v, o, after, mine, sems):
    copy_rows((q, k, v, o), my_place()[0] * mine.shape[1], mine, sems, COPY_ROWS)


def split_wide(value):
    parts = []
    for _ in range(3):
        part = value.astype(jnp.bfloat16)
        value = value - part.astype(jnp.float32)
        parts.append(part)
    return parts


def local_kernel(heads, scale, table, mine, near, theirs, small, out_bias, *outs):
    others = outs[: CHUNKS - 1]
    sames = [outs[CHUNKS - 1 : CHUNKS + 1]] + [planes(out) for out in outs[CHUNKS + 1 :]]
    core, chip = my_place()
    half, size, width = mine.shape[1], sames[0][0].shape[0], mine.shape[2]
    own, other = shifted(planes(mine), 0), shifted(planes(near), 0)
    offset = [table[d : d + 1, :] for d in range(4)]
    out_bias[...] = jnp.zeros_like(out_bias)

    def run(a, b):
        def tile(row):
            at, bt = tiles_of(a, row), tiles_of(b, row)
            held = pair_dots(
                (at[0], bt[0]), (at[1], bt[1]), (at[3], bt[3]), (at[2], bt[2]), LOCAL, heads
            )
            total = held[0]
            for j in range(1, 6):
                total = total + pltpu.roll(held[j], heads * j, axis=1)
            small[tile_at(row), :] = total
            (_, d0), (_, d1) = early_rows(held, scale, offset)
            lines = bias_lines([[d0[0], d1[1]], [d1[0]], [], []])
            out_bias[...] += jnp.where(chip == 0, lines, jnp.zeros_like(lines))

        over_tiles(half, tile)

    pl.when(core == 0)(lambda: run(own, other))
    pl.when(core == 1)(lambda: run(other, own))

    for c, out in enumerate(others):
        take_far(planes(theirs), sent_start(c + 1, size), planes(out))
    for c, out in enumerate(sames):
        start = sent_start(c, size)
        take_far(planes(mine), start, out)
        for step in range(0, size, TILE):
            parts = split_wide(small[tile_at(start + step), :])
            rows = slice(step, step + TILE)
            out[0][rows, width : width + LANES] = parts[0]
            out[0][rows, width + LANES :] = parts[1]
            out[1][rows, width : width + LANES] = parts[2]
            out[1][rows, width + LANES :] = jnp.zeros((TILE, LANES), jnp.bfloat16)


EARLY, LATE = 14, 10


def score_tile(heads, scale, chip, a, b, table, small_own, small_far):
    offset = [table[d : d + 1, :] for d in range(4)]
    if chip == 0:
        queries, keys = ((a[4], a[5]), (b[4], b[5])), ((a[1], a[2]), (b[1], b[2]))
    else:
        queries, keys = ((a[0], a[3]), (b[0], b[3])), ((a[4], a[5]), (b[4], b[5]))
    held = pair_dots(
        [x[0] for x in queries], [x[0] for x in keys],
        [x[1] for x in queries], [x[1] for x in keys], CROSS, heads,
    )
    diag = unpack(small_far if chip == 0 else small_own, heads)
    score = lambda j, d: held[j] * scale + offset[d]
    p2, d2 = soft_row(
        [score(0, 2), score(1, 1), diag[0] * scale + offset[0]], [held[4], held[5], diag[3]]
    )
    p3, d3 = soft_row(
        [score(2, 3), score(3, 2), diag[1] * scale + offset[1], diag[2] * scale + offset[0]],
        [held[6], held[7], diag[4], diag[5]],
    )
    lines = bias_lines([[d2[2], d3[3]], [d2[1], d3[2]], [d2[0], d3[1]], [d3[0]]])
    if chip == 1:
        items = [d2[2], d3[2], d3[3], d2[0], d2[1], d3[0], d3[1], p2[2], p3[2], p3[3]]
    else:
        (p0, d0), (p1, d1) = early_rows(unpack(small_own, heads), scale, offset)
        items = [d0[0], d1[0], d1[1], d2[0], d2[1], d3[0], d3[1]]
        items += [p0[0], p1[0], p1[1], p2[0], p2[1], p3[0], p3[1]]
    return [item.astype(jnp.bfloat16) for item in items], lines


def gradient_tile(heads, scale, chip, a, b, items, out_a, out_b):
    width = 2 * LANES
    lines = -(-heads // TILE) * TILE
    line = lax.broadcasted_iota(jnp.int32, (lines, width), 0)
    head = lax.broadcasted_iota(jnp.int32, (lines, width), 1) // LANES
    zeros = jnp.zeros((LANES - lines, width), jnp.bfloat16)
    spread = jnp.concatenate(items, axis=0)

    for pair in range(heads // 2):
        at = slice(pair * width, (pair + 1) * width)
        pick = jnp.where(line == 2 * pair + head, 1.0, 0.0).astype(jnp.bfloat16)
        flat = jnp.dot(
            spread, jnp.concatenate([pick, zeros], axis=0), preferred_element_type=jnp.float32
        )
        w = [flat[j * TILE : (j + 1) * TILE, :] for j in range(len(items))]

        def put(ref, value):
            ref[at] = value.astype(jnp.bfloat16)

        def wide(*refs):
            return [ref[at].astype(jnp.float32) for ref in refs]

        if chip == 0:
            ka, kb = wide(a[1], b[1])
            put(out_a[0], w[0] * ka * scale)
            put(out_b[0], (w[1] * ka + w[2] * kb) * scale)
            for to, x, g, rate in ((1, 0, 0, scale), (2, 3, 7, 1.0)):
                xa, xb, x2, x3 = wide(a[x], b[x], a[3 + to], b[3 + to])
                for_a = w[g] * xa + w[g + 1] * xb + w[g + 3] * x2 + w[g + 5] * x3
                for_b = w[g + 2] * xb + w[g + 4] * x2 + w[g + 6] * x3
                put(out_a[to], for_a * rate)
                put(out_b[to], for_b * rate)
        else:
            k2, k3, k0, k1 = wide(a[1], b[1], a[4], b[4])
            put(out_a[0], (w[0] * k2 + w[3] * k0 + w[4] * k1) * scale)
            put(out_b[0], (w[1] * k2 + w[2] * k3 + w[5] * k0 + w[6] * k1) * scale)
            q2, q3, o2, o3 = wide(a[0], b[0], a[3], b[3])
            put(out_a[1], (w[0] * q2 + w[1] * q3) * scale)
            put(out_b[1], w[2] * q3 * scale)
            put(out_a[2], w[7] * o2 + w[8] * o3)
            put(out_b[2], w[9] * o3)


def planes(ref):
    return tuple(ref.at[j] for j in range(ref.shape[0]))


def frames_of(mine, near, far, start):
    *same, other = far
    return (
        shifted(planes(mine), start) + shifted(pair_of(same), 0),
        shifted(planes(near), start) + shifted(planes(other), 0),
    )


def pair_of(same):
    return tuple(same) if len(same) == 2 else planes(same[0])


def far_small(far, rows, width):
    first, second = pair_of(far[:-1])
    parts = [first[rows, width : width + LANES], first[rows, width + LANES :]]
    parts += [second[rows, width : width + LANES]]
    return functools.reduce(jnp.add, [part.astype(jnp.float32) for part in parts])


def score_kernel(heads, scale, chunk, table, small, bias, mine, near, *refs):
    *far, out_items, out_bias, lines_ref = refs
    size, width = out_items.shape[1], mine.shape[2]
    start = chunk_start(chunk, size)
    lines_ref[...] = bias[...]

    def work(chip, a, b):
        def tile(row):
            items, lines = score_tile(
                heads, scale, chip, tiles_of(a, row), tiles_of(b, row), table,
                small[tile_at(start + row), :], far_small(far, tile_at(row), width),
            )
            for j, item in enumerate(items):
                out_items[j, tile_at(row), :] = item
            lines_ref[...] += lines

        over_tiles(size, tile)

    with_frames(*frames_of(mine, near, far, start), work)
    out_bias[...] = lines_ref[: out_bias.shape[0], : out_bias.shape[1]]


def gradient_kernel(heads, scale, chunk, items_ref, mine, near, *refs):
    *far, out_own, out_other = refs
    size = out_own.shape[1]
    own, neighbour = frames_of(mine, near, far, chunk_start(chunk, size))
    own_out, other_out = shifted(planes(out_own), 0), shifted(planes(out_other), 0)

    def work(chip, a, b):
        out_a, out_b = (own_out, other_out) if a is own else (other_out, own_out)

        def tile(row):
            items = [items_ref[j, tile_at(row), :] for j in range(LATE if chip else EARLY)]
            gradient_tile(
                heads, scale, chip, tiles_of(a, row), tiles_of(b, row), items,
                tiles_of(out_a, row), tiles_of(out_b, row),
            )

        over_tiles(size, tile)

    with_frames(own, neighbour, work)


def whole_kernel(heads, scale, chunk, table, small, mine, near, *refs):
    *far, out_own = refs[:-3]
    out_others = refs[-3:]
    size, width = out_own.shape[1], mine.shape[2]
    start = chunk_start(chunk, size)
    own, neighbour = frames_of(mine, near, far, start)
    own_out, other_out = shifted(planes(out_own), 0), shifted(out_others, 0)

    def work(chip, a, b):
        out_a, out_b = (own_out, other_out) if a is own else (other_out, own_out)

        def tile(row):
            at, bt = tiles_of(a, row), tiles_of(b, row)
            items, _ = score_tile(
                heads, scale, chip, at, bt, table,
                small[tile_at(start + row), :], far_small(far, tile_at(row), width),
            )
            gradient_tile(
                heads, scale, chip, at, bt, items, tiles_of(out_a, row), tiles_of(out_b, row)
            )

        over_tiles(size, tile)

    with_frames(own, neighbour, work)


def output_kernel(*refs):
    kept, refs = refs[:CHUNKS], refs[CHUNKS:]
    *backs, left, right = refs[:-6]
    outs, (out_bias, total, sems) = refs[-6:-3], refs[-3:]
    backs = [planes(backs[0])] + [backs[j : j + 3] for j in range(1, len(backs), 3)]
    size = kept[0].shape[1]
    half = CHUNKS * size
    core = my_place()[0]
    total[...] = left[...] + right[...]
    copies = [pltpu.make_async_copy(total, out_bias, sems.at[0])]
    for c in range(CHUNKS):
        for which, piece in ((core, planes(kept[c])), (1 - core, backs[c])):
            start = pl.multiple_of(which * half + chunk_start(c, size), TILE)
            for part, out in zip(piece, outs):
                copies.append(
                    pltpu.make_async_copy(part, out.at[pl.ds(start, size)], sems.at[len(copies)])
                )
    for copy in copies:
        copy.start()
    for copy in copies:
        copy.wait()


def four_way(value, axes, masks, count):
    first, second = masks
    got = [
        lax.ppermute(value, axes, [(i, i ^ mask) for i in range(count)])
        for mask in (first, second, first ^ second)
    ]
    return (value + got[0]) + (got[1] + got[2])


def sum_group(value, sizes):
    axes = tuple(axis for axis, _ in sizes)
    (_, tm), (_, patch) = sizes
    count = tm * patch
    masks = [patch] + [1 << j for j in range(patch.bit_length() - 1)] + [2 * patch]
    while len(masks) > 2:
        value = four_way(value, axes, masks[:2], count)
        masks = masks[2:]
    if len(masks) == 2:
        value = value + lax.ppermute(value, axes, [(i, i ^ masks[0]) for i in range(count)])
    return value, lax.ppermute(value, axes, [(i, i ^ masks[-1]) for i in range(count)])


def by_chips(query_vectors, key_vectors, value_vectors, grad_output, time_bias, sizes):
    heads, frames = time_bias.shape
    clips, _, patches, width = query_vectors.shape
    rows = clips * patches
    half = rows // 2
    size = half // CHUNKS
    scale = 1.0 / math.sqrt(width // heads)
    own = [
        pltpu.with_memory_space_constraint(x.reshape(rows, width), pltpu.HBM)
        for x in (query_vectors, key_vectors, value_vectors, grad_output)
    ]
    vmem_spec = pl.BlockSpec(memory_space=pltpu.VMEM)
    any_spec = pl.BlockSpec(memory_space=pl.ANY)

    def swap(x, bits):
        return lax.ppermute(x, "tm", [(i, i ^ bits) for i in range(4)])

    def shape(*dims, dtype=jnp.bfloat16):
        return jax.ShapeDtypeStruct(dims, dtype)

    def call(kernel, name, out_shape, *args, scratch=(), hbm=0, out_spec=vmem_spec):
        return pl.pallas_call(
            kernel,
            in_specs=[any_spec] * hbm + [vmem_spec] * (len(args) - hbm),
            out_specs=[out_spec] * len(out_shape),
            out_shape=out_shape,
            scratch_shapes=scratch,
            compiler_params=pltpu.CompilerParams(vmem_limit_bytes=16 * 2**20),
            cost_estimate=LITTLE,
            name=name,
        )(*args)

    wide = jnp.float32
    copies = [pltpu.SemaphoreType.DMA((4 * half // COPY_ROWS,))]
    far_shape, same_shape = shape(2, size, width), shape(2, size, width + 2 * LANES)
    table = jnp.pad(time_bias.T, ((0, 8 - frames), (0, LANES - heads)))
    theirs, other = call(
        fetch_theirs_kernel, "fetch_theirs", [shape(4, half, width), far_shape], *own,
        scratch=copies, hbm=4,
    )
    near = swap(theirs, 1)
    others = [swap(other, 3)]
    (mine,) = call(
        fetch_mine_kernel, "fetch_mine", [shape(4, half, width)], *own, other, scratch=copies, hbm=5
    )
    small, bias, *sent = call(
        functools.partial(local_kernel, heads, scale),
        "local_scores",
        [shape(half, LANES, dtype=wide), shape(8, LANES, dtype=wide)]
        + [far_shape] * (CHUNKS - 1)
        + [shape(size, width + 2 * LANES)] * 2
        + [same_shape] * (CHUNKS - 1),
        table, mine, near, theirs,
    )
    sames = [[swap(x, 2) for x in sent[CHUNKS - 1 : CHUNKS + 1]]]
    sames += [[swap(x, 2)] for x in sent[CHUNKS + 1 :]]
    others += [swap(x, 3) for x in sent[: CHUNKS - 1]]

    kept, backs = [], []
    pieces = [shape(3, size, width)] * 2
    for c in range(CHUNKS):
        arrays = (mine, near, *sames[c], others[c])
        if c == 0:
            items, bias = call(
                functools.partial(score_kernel, heads, scale, c),
                "scores",
                [shape(EARLY, size, LANES), shape(frames, heads, dtype=wide)],
                table, small, bias, *arrays,
                scratch=[pltpu.VMEM((8, LANES), wide)],
            )
            bias = sum_group(bias, sizes)
            piece, *back = call(
                functools.partial(gradient_kernel, heads, scale, c), "gradients", pieces,
                items, *arrays,
            )
        else:
            piece, *back = call(
                functools.partial(whole_kernel, heads, scale, c), "scores_and_gradients",
                pieces[:1] + [shape(size, width)] * 3, table, small, *arrays,
            )
        kept.append(piece)
        backs.append([swap(x, 1) for x in back])
    *grads, bias = call(
        output_kernel,
        "outputs",
        [shape(rows, width)] * 3 + [shape(frames, heads, dtype=wide)],
        *kept, *(x for back in backs for x in back), *bias,
        scratch=[
            pltpu.VMEM((frames, heads), wide),
            pltpu.SemaphoreType.DMA((1 + 6 * CHUNKS,)),
        ],
        out_spec=any_spec,
    )
    return (*[x.reshape(query_vectors.shape) for x in grads], bias.T)


def solution(mesh):
    sizes = tuple((axis, mesh.shape[axis]) for axis in ("tm", "patch"))

    def per_device(*args):
        heads, frames = args[4].shape
        fits = (
            mesh.shape["tm"] == 4
            and frames == 4
            and args[0].shape[1] == 1
            and heads * LANES == args[0].shape[3]
            and heads * 6 <= LANES
            and heads % 2 == 0
            and args[0].shape[0] * args[0].shape[2] % (2 * TILE * CHUNKS) == 0
            and mesh.shape["patch"].bit_count() == 1
        )
        return (by_chips if fits else by_heads)(*args, sizes)

    vectors = P(None, "tm", "patch", None)
    return jax.shard_map(
        per_device,
        mesh=mesh,
        in_specs=(vectors,) * 4 + (P(),),
        out_specs=(vectors,) * 3 + (P(),),
        check_vma=False,
    )
```

```python
import functools
import math

import jax
import jax.numpy as jnp
from jax import lax
from jax.experimental import pallas as pl
from jax.experimental.pallas import tpu as pltpu
from jax.sharding import PartitionSpec as P

LANES = 128
TILE = 16
LITTLE = pl.CostEstimate(flops=1, bytes_accessed=1, transcendentals=0)
CHUNKS = 2


def score_table(bias_rows, frames):
    steps = jnp.arange(frames, dtype=jnp.int32)
    offsets = steps[:, None] - steps[None, :]
    onehot = (offsets[:, :, None] == steps[None, None, :]).astype(jnp.float32)
    table = jnp.einsum("hd,tud->htu", bias_rows, onehot, precision=lax.Precision.HIGHEST)
    return (table, offsets >= 0, onehot)


def attend_back(query_heads, key_heads, value_heads, grad_heads, bias_rows):
    frames = query_heads.shape[1]
    score_scale = 1.0 / math.sqrt(query_heads.shape[4])
    table, causal, onehot = score_table(bias_rows, frames)
    wide = jnp.float32
    scores = (
        jnp.einsum("atxhd,auxhd->axhtu", query_heads, key_heads, preferred_element_type=wide)
        * score_scale
        + table[None, None]
    )
    scores = jnp.where(causal, scores, -jnp.inf)
    row_max = jnp.max(scores, axis=-1, keepdims=True)
    expon = jnp.exp(scores - row_max)
    weights = expon / jnp.sum(expon, axis=-1, keepdims=True)
    weights_low = weights.astype(jnp.bfloat16)
    attended = jnp.einsum(
        "axhtu,auxhd->atxhd", weights_low, value_heads, preferred_element_type=wide
    )
    rowdot = jnp.einsum("atxhd,atxhd->axht", grad_heads, attended, preferred_element_type=wide)
    grad_weights = jnp.einsum(
        "atxhd,auxhd->axhtu", grad_heads, value_heads, preferred_element_type=wide
    )
    grad_scores = weights * (grad_weights - rowdot[..., None])
    bias_terms = jnp.einsum("axhtu,tud->axhd", grad_scores, onehot, precision=lax.Precision.HIGHEST)
    grad_low = grad_scores.astype(jnp.bfloat16)
    grad_query = (
        jnp.einsum("axhtu,auxhd->atxhd", grad_low, key_heads, preferred_element_type=wide)
        * score_scale
    ).astype(jnp.bfloat16)
    grad_key = (
        jnp.einsum("axhtu,atxhd->auxhd", grad_low, query_heads, preferred_element_type=wide)
        * score_scale
    ).astype(jnp.bfloat16)
    grad_value = jnp.einsum(
        "axhtu,atxhd->auxhd", weights_low, grad_heads, preferred_element_type=wide
    ).astype(jnp.bfloat16)
    return (grad_query, grad_key, grad_value, bias_terms)


def sum_everywhere(value, sizes):
    for axis, size in sizes:
        if size & (size - 1):
            value = lax.psum(value, axis)
            continue
        step = 1
        while step < size:
            other = lax.ppermute(value, axis, [(i, i ^ step) for i in range(size)])
            value = value + other
            step *= 2
    return value


def by_heads(query_vectors, key_vectors, value_vectors, grad_output, time_bias, sizes):
    head_count = time_bias.shape[0]
    frames = time_bias.shape[1]
    head_dim = query_vectors.shape[3] // head_count
    split_shape = query_vectors.shape[:3] + (head_count, head_dim)
    local_heads = head_count // lax.axis_size("tm")
    first_head = lax.axis_index("tm") * local_heads
    bias_rows = lax.dynamic_slice_in_dim(time_bias, first_head, local_heads, 0)
    spread = [
        lax.all_to_all(item.reshape(split_shape), "tm", split_axis=3, concat_axis=1, tiled=True)
        for item in (query_vectors, key_vectors, value_vectors, grad_output)
    ]
    *grads, bias_terms = attend_back(*spread, bias_rows)
    grads = [
        lax.all_to_all(item, "tm", split_axis=1, concat_axis=3, tiled=True).reshape(
            query_vectors.shape
        )
        for item in grads
    ]
    partial = lax.dynamic_update_slice_in_dim(
        jnp.zeros((head_count, frames), jnp.float32),
        jnp.sum(bias_terms, axis=(0, 1)),
        first_head,
        0,
    )
    return (*grads, sum_everywhere(partial, sizes))


def pair_dots(queries, keys, grads, values, pairs, heads):
    place = lax.broadcasted_iota(jnp.int32, (TILE, LANES), 1)
    held = [jnp.zeros((TILE, LANES), jnp.float32)] * (2 * len(pairs))
    for head in range(heads):
        at = slice(head * LANES, (head + 1) * LANES)
        here = place == head
        load = lambda refs: [ref[at].astype(jnp.float32) for ref in refs]
        q, k, o, v = load(queries), load(keys), load(grads), load(values)
        for j, (t, u) in enumerate(pairs):
            score = jnp.sum(q[t] * k[u], axis=1, keepdims=True)
            held[j] = jnp.where(here, score, held[j])
            gain = jnp.sum(o[t] * v[u], axis=1, keepdims=True)
            held[len(pairs) + j] = jnp.where(here, gain, held[len(pairs) + j])
    return held


def over_tiles(rows, body):
    pl.loop(0, rows // TILE)(lambda i: body(i * TILE))


def tile_at(start):
    return pl.ds(pl.multiple_of(start, TILE), TILE)


class Shifted:
    def __init__(self, ref, start):
        self.ref, self.start = ref, start

    def at_rows(self, row):
        return View(self.ref, tile_at(self.start + row))


class View:
    def __init__(self, ref, rows):
        self.ref, self.rows = ref, rows

    def __getitem__(self, lanes):
        return self.ref[self.rows, lanes]

    def __setitem__(self, lanes, value):
        self.ref[self.rows, lanes] = value


def tiles_of(refs, row):
    return tuple(ref.at_rows(row) for ref in refs)


def shifted(refs, start):
    return tuple(Shifted(ref, start) for ref in refs)


def soft_row(scores, gains):
    top = functools.reduce(jnp.maximum, scores)
    expon = [jnp.exp(item - top) for item in scores]
    total = functools.reduce(jnp.add, expon)
    weights = [item / total for item in expon]
    low = [item.astype(jnp.bfloat16) for item in weights]
    rowdot = functools.reduce(
        jnp.add, [a.astype(jnp.float32) * g for a, g in zip(low, gains)]
    )
    grads = [w * (g - rowdot) for w, g in zip(weights, gains)]
    return low, grads


LOCAL = ((0, 0), (1, 0), (1, 1))
CROSS = ((0, 0), (0, 1), (1, 0), (1, 1))


def unpack(packed, heads):
    return [packed if j == 0 else pltpu.roll(packed, LANES - heads * j, axis=1) for j in range(6)]


def bias_lines(terms):
    lines = []
    for items in terms:
        lines.append(
            jnp.sum(functools.reduce(jnp.add, items), axis=0, keepdims=True)
            if items
            else jnp.zeros((1, LANES), jnp.float32)
        )
    return jnp.concatenate(lines + [jnp.zeros((4, LANES), jnp.float32)], axis=0)


def early_rows(diag, scale, offset):
    score = lambda j, d: diag[j] * scale + offset[d]
    row0 = soft_row([score(0, 0)], [diag[3]])
    row1 = soft_row([score(1, 1), score(2, 0)], [diag[4], diag[5]])
    return row0, row1


def my_place():
    me = lax.axis_index("tm")
    return lax.rem(me, 2), lax.div(me, 2)


def with_frames(own, other, work):
    core, chip = my_place()
    for at_chip in range(2):
        pl.when((chip == at_chip) & (core == 0))(functools.partial(work, at_chip, own, other))
        pl.when((chip == at_chip) & (core == 1))(functools.partial(work, at_chip, other, own))


def chunk_start(chunk, size):
    return jnp.where(my_place()[1] == 0, chunk, CHUNKS - 1 - chunk) * size


def copy_chunks(sources, core, outs, sems):
    size = outs[0].shape[1]
    copies = []
    for c, out in enumerate(outs):
        start = pl.multiple_of(core * CHUNKS * size + chunk_start(c, size), TILE)
        for j, ref in enumerate(sources):
            copies.append(
                pltpu.make_async_copy(
                    ref.at[pl.ds(start, size)], out.at[j], sems.at[len(copies)]
                )
            )
    for copy in copies:
        copy.start()
    for copy in copies:
        copy.wait()


def take_far(refs, outs):
    chip = my_place()[1]

    def take(places):
        for out, place in zip(outs, places):
            for row in range(0, out.shape[0], TILE):
                rows = slice(row, row + TILE)
                out[rows, : refs[place].shape[1]] = refs[place][rows, :]

    pl.when(chip == 0)(lambda: take((1, 2)))
    pl.when(chip == 1)(lambda: take((0, 3)))


def fetch_theirs_kernel(q, k, v, o, *refs):
    nears, other, sems = refs[:CHUNKS], refs[CHUNKS], refs[CHUNKS + 1]
    copy_chunks((q, k, v, o), 1 - my_place()[0], nears, sems)
    take_far(planes(nears[CHUNKS - 1]), planes(other))


def fetch_mine_kernel(q, k, v, o, after, *refs):
    copy_chunks((q, k, v, o), my_place()[0], refs[:-1], refs[-1])


def packed_small(value, heads):
    used = 6 * heads
    place = lax.broadcasted_iota(jnp.int32, value.shape, 1)
    high = value.astype(jnp.bfloat16).astype(jnp.float32)
    middle = (value - high).astype(jnp.bfloat16).astype(jnp.float32)
    rest = (value - high) - middle
    first = jnp.where(place < used, high, pltpu.roll(rest, used, axis=1))
    second = jnp.where(place < used, middle, pltpu.roll(rest, 2 * used - LANES, axis=1))
    return first.astype(jnp.bfloat16), second.astype(jnp.bfloat16)


def unpacked_small(first, second, heads):
    used = 6 * heads
    first, second = first.astype(jnp.float32), second.astype(jnp.float32)
    place = lax.broadcasted_iota(jnp.int32, first.shape, 1)
    rest = jnp.where(
        place < LANES - used,
        pltpu.roll(first, LANES - used, axis=1),
        pltpu.roll(second, 2 * (LANES - used), axis=1),
    )
    return first + second + jnp.where(place < 3 * heads, rest, 0.0)


def local_kernel(heads, scale, table, *refs):
    mines, nears, theirs, refs = refs[:2], refs[2:4], refs[4], refs[5:]
    smalls, out_bias, other, sames = refs[:2], refs[2], refs[3], (refs[4:6], planes(refs[6]))
    core, chip = my_place()
    size, width = mines[0].shape[1:]
    offset = [table[d : d + 1, :] for d in range(4)]
    out_bias[...] = jnp.zeros_like(out_bias)

    def run(a, b, small):
        def tile(row):
            at, bt = tiles_of(a, row), tiles_of(b, row)
            held = pair_dots(
                (at[0], bt[0]), (at[1], bt[1]), (at[3], bt[3]), (at[2], bt[2]), LOCAL, heads
            )
            total = held[0]
            for j in range(1, 6):
                total = total + pltpu.roll(held[j], heads * j, axis=1)
            small[tile_at(row), :] = total
            (_, d0), (_, d1) = early_rows(held, scale, offset)
            lines = bias_lines([[d0[0], d1[1]], [d1[0]], [], []])
            out_bias[...] += jnp.where(chip == 0, lines, jnp.zeros_like(lines))

        over_tiles(size, tile)

    for mine, near, small in zip(mines, nears, smalls):
        own, neighbour = shifted(planes(mine), 0), shifted(planes(near), 0)
        pl.when(core == 0)(functools.partial(run, own, neighbour, small))
        pl.when(core == 1)(functools.partial(run, neighbour, own, small))

    take_far(planes(theirs), planes(other))
    for c, out in enumerate(sames):
        take_far(planes(mines[1 - c]), out)
        for row in range(0, size, TILE):
            rows = slice(row, row + TILE)
            parts = packed_small(smalls[1 - c][rows, :], heads)
            for ref, part in zip(sames[0], parts):
                ref[rows, width + c * LANES : width + (c + 1) * LANES] = part


EARLY, LATE = 14, 10


def score_tile(heads, scale, chip, a, b, table, small_own, small_far):
    offset = [table[d : d + 1, :] for d in range(4)]
    if chip == 0:
        queries, keys = ((a[4], a[5]), (b[4], b[5])), ((a[1], a[2]), (b[1], b[2]))
    else:
        queries, keys = ((a[0], a[3]), (b[0], b[3])), ((a[4], a[5]), (b[4], b[5]))
    held = pair_dots(
        [x[0] for x in queries], [x[0] for x in keys],
        [x[1] for x in queries], [x[1] for x in keys], CROSS, heads,
    )
    diag = unpack(small_far if chip == 0 else small_own, heads)
    score = lambda j, d: held[j] * scale + offset[d]
    p2, d2 = soft_row(
        [score(0, 2), score(1, 1), diag[0] * scale + offset[0]], [held[4], held[5], diag[3]]
    )
    p3, d3 = soft_row(
        [score(2, 3), score(3, 2), diag[1] * scale + offset[1], diag[2] * scale + offset[0]],
        [held[6], held[7], diag[4], diag[5]],
    )
    lines = bias_lines([[d2[2], d3[3]], [d2[1], d3[2]], [d2[0], d3[1]], [d3[0]]])
    if chip == 1:
        items = [d2[2], d3[2], d3[3], d2[0], d2[1], d3[0], d3[1], p2[2], p3[2], p3[3]]
    else:
        (p0, d0), (p1, d1) = early_rows(unpack(small_own, heads), scale, offset)
        items = [d0[0], d1[0], d1[1], d2[0], d2[1], d3[0], d3[1]]
        items += [p0[0], p1[0], p1[1], p2[0], p2[1], p3[0], p3[1]]
    return [item.astype(jnp.bfloat16) for item in items], lines


def gradient_tile(heads, scale, chip, a, b, items, out_a, out_b):
    width = 2 * LANES
    lines = -(-heads // TILE) * TILE
    line = lax.broadcasted_iota(jnp.int32, (lines, width), 0)
    head = lax.broadcasted_iota(jnp.int32, (lines, width), 1) // LANES
    zeros = jnp.zeros((LANES - lines, width), jnp.bfloat16)
    spread = jnp.concatenate(items, axis=0)

    for pair in range(heads // 2):
        at = slice(pair * width, (pair + 1) * width)
        pick = jnp.where(line == 2 * pair + head, 1.0, 0.0).astype(jnp.bfloat16)
        flat = jnp.dot(
            spread, jnp.concatenate([pick, zeros], axis=0), preferred_element_type=jnp.float32
        )
        w = [flat[j * TILE : (j + 1) * TILE, :] for j in range(len(items))]

        def put(ref, value):
            ref[at] = value.astype(jnp.bfloat16)

        def wide(*refs):
            return [ref[at].astype(jnp.float32) for ref in refs]

        if chip == 0:
            ka, kb = wide(a[1], b[1])
            put(out_a[0], w[0] * ka * scale)
            put(out_b[0], (w[1] * ka + w[2] * kb) * scale)
            for to, x, g, rate in ((1, 0, 0, scale), (2, 3, 7, 1.0)):
                xa, xb, x2, x3 = wide(a[x], b[x], a[3 + to], b[3 + to])
                for_a = w[g] * xa + w[g + 1] * xb + w[g + 3] * x2 + w[g + 5] * x3
                for_b = w[g + 2] * xb + w[g + 4] * x2 + w[g + 6] * x3
                put(out_a[to], for_a * rate)
                put(out_b[to], for_b * rate)
        else:
            k2, k3, k0, k1 = wide(a[1], b[1], a[4], b[4])
            put(out_a[0], (w[0] * k2 + w[3] * k0 + w[4] * k1) * scale)
            put(out_b[0], (w[1] * k2 + w[2] * k3 + w[5] * k0 + w[6] * k1) * scale)
            q2, q3, o2, o3 = wide(a[0], b[0], a[3], b[3])
            put(out_a[1], (w[0] * q2 + w[1] * q3) * scale)
            put(out_b[1], w[2] * q3 * scale)
            put(out_a[2], w[7] * o2 + w[8] * o3)
            put(out_b[2], w[9] * o3)


def planes(ref):
    return tuple(ref.at[j] for j in range(ref.shape[0]))


def frames_of(mine, near, far):
    *same, other = far
    return (
        shifted(planes(mine) + pair_of(same), 0),
        shifted(planes(near) + planes(other), 0),
    )


def pair_of(same):
    return tuple(same) if len(same) == 2 else planes(same[0])


def far_small(far, rows, width, heads, chunk):
    at = slice(width + chunk * LANES, width + (chunk + 1) * LANES)
    return unpacked_small(*(ref[rows, at] for ref in pair_of(far[:-1])), heads)


def score_kernel(heads, scale, table, small, bias, mine, near, *refs):
    far, (out_items, out_shares, out_small), lines_ref = refs[:3], refs[3:6], refs[6]
    size, width = mine.shape[1:]
    lines_ref[...] = bias[...]

    def work(chip, a, b):
        def tile(row):
            rows = tile_at(row)
            items, lines = score_tile(
                heads, scale, chip, tiles_of(a, row), tiles_of(b, row), table,
                small[rows, :], far_small(far, rows, width, heads, 0),
            )
            out_small[rows, :] = far_small(far, rows, width, heads, 1)
            for j, item in enumerate(items):
                out_items[j, rows, :] = item
            lines_ref[...] += lines

        over_tiles(size, tile)

    with_frames(*frames_of(mine, near, far), work)
    for j in range(out_shares.shape[0]):
        out_shares[j] = lines_ref[: out_shares.shape[1], :]


def output_copies(which, piece, outs, chunk, sems, at):
    size = piece[0].shape[0]
    start = pl.multiple_of(which * CHUNKS * size + chunk_start(chunk, size), TILE)
    return [
        pltpu.make_async_copy(part, out.at[pl.ds(start, size)], sems.at[at + j])
        for j, (part, out) in enumerate(zip(piece, outs))
    ]


def gradient_kernel(heads, scale, items_ref, mine, near, *refs):
    far, out_other, outs, kept, sems = refs[:3], refs[3], refs[4:7], refs[7], refs[8]
    own, neighbour = frames_of(mine, near, far)
    own_out, other_out = shifted(planes(kept), 0), shifted(planes(out_other), 0)

    def work(chip, a, b):
        out_a, out_b = (own_out, other_out) if a is own else (other_out, own_out)

        def tile(row):
            items = [items_ref[j, tile_at(row), :] for j in range(LATE if chip else EARLY)]
            gradient_tile(
                heads, scale, chip, tiles_of(a, row), tiles_of(b, row), items,
                tiles_of(out_a, row), tiles_of(out_b, row),
            )

        over_tiles(mine.shape[1], tile)

    with_frames(own, neighbour, work)
    copies = output_copies(my_place()[0], planes(kept), outs, 0, sems, 0)
    for copy in copies:
        copy.start()
    for copy in copies:
        copy.wait()


def whole_kernel(heads, scale, table, small, small_far, mine, near, *refs):
    far, out_own, out_others = refs[:2], refs[2], refs[3:6]
    own, neighbour = frames_of(mine, near, far)
    own_out, other_out = shifted(planes(out_own), 0), shifted(out_others, 0)

    def work(chip, a, b):
        out_a, out_b = (own_out, other_out) if a is own else (other_out, own_out)

        def tile(row):
            at, bt, rows = tiles_of(a, row), tiles_of(b, row), tile_at(row)
            items, _ = score_tile(
                heads, scale, chip, at, bt, table, small[rows, :], small_far[rows, :]
            )
            gradient_tile(
                heads, scale, chip, at, bt, items, tiles_of(out_a, row), tiles_of(out_b, row)
            )

        over_tiles(mine.shape[1], tile)

    with_frames(own, neighbour, work)


def output_kernel(*refs):
    first_back, kept, back, shares = planes(refs[0]), planes(refs[1]), refs[2:5], refs[5]
    outs, out_bias, total, sems = refs[9:12], *refs[12:]
    core = my_place()[0]
    copies = output_copies(1 - core, first_back, outs, 0, sems, 0)
    copies += output_copies(core, kept, outs, 1, sems, 3)
    copies += output_copies(1 - core, back, outs, 1, sems, 6)
    for copy in copies:
        copy.start()
    parts = [shares[j] for j in range(shares.shape[0])]
    while len(parts) > 1:
        parts = [a + b for a, b in zip(parts[::2], parts[1::2])]
    total[...] = parts[0][: total.shape[0], : total.shape[1]]
    copies.append(pltpu.make_async_copy(total, out_bias, sems.at[9]))
    copies[-1].start()
    for copy in copies:
        copy.wait()


def by_chips(query_vectors, key_vectors, value_vectors, grad_output, time_bias, sizes):
    heads, frames = time_bias.shape
    clips, _, patches, width = query_vectors.shape
    rows = clips * patches
    half = rows // 2
    size = half // CHUNKS
    scale = 1.0 / math.sqrt(width // heads)
    own = [
        pltpu.with_memory_space_constraint(x.reshape(rows, width), pltpu.HBM)
        for x in (query_vectors, key_vectors, value_vectors, grad_output)
    ]
    vmem_spec = pl.BlockSpec(memory_space=pltpu.VMEM)
    any_spec = pl.BlockSpec(memory_space=pl.ANY)

    def swap(x, bits):
        return lax.ppermute(x, "tm", [(i, i ^ bits) for i in range(4)])

    def shape(*dims, dtype=jnp.bfloat16):
        return jax.ShapeDtypeStruct(dims, dtype)

    def call(kernel, name, out_shape, *args, scratch=(), hbm=(), hbm_out=(), aliases={}):
        return pl.pallas_call(
            kernel,
            in_specs=[any_spec if j in hbm else vmem_spec for j in range(len(args))],
            out_specs=[any_spec if j in hbm_out else vmem_spec for j in range(len(out_shape))],
            out_shape=out_shape,
            scratch_shapes=scratch,
            input_output_aliases=aliases,
            compiler_params=pltpu.CompilerParams(vmem_limit_bytes=16 * 2**20),
            cost_estimate=LITTLE,
            name=name,
        )(*args)

    wide = jnp.float32
    lines = shape(8, LANES, dtype=wide)
    chunk_shape, far_shape = shape(4, size, width), shape(2, size, width)
    copies = [pltpu.SemaphoreType.DMA((4 * CHUNKS,))]
    table = jnp.pad(time_bias.T, ((0, 8 - frames), (0, LANES - heads)))

    *theirs, other = call(
        fetch_theirs_kernel, "fetch_theirs", [chunk_shape] * CHUNKS + [far_shape], *own,
        scratch=copies, hbm=range(4),
    )
    nears = [swap(x, 1) for x in theirs]
    others = [swap(other, 3)]
    mines = call(
        fetch_mine_kernel, "fetch_mine", [chunk_shape] * CHUNKS, *own, other,
        scratch=copies, hbm=range(5),
    )

    *smalls, bias, other, same_first, same_second, same = call(
        functools.partial(local_kernel, heads, scale),
        "local_scores",
        [shape(size, LANES, dtype=wide)] * CHUNKS
        + [lines, far_shape]
        + [shape(size, width + CHUNKS * LANES)] * 2
        + [far_shape],
        table, *mines, *nears, theirs[0],
    )
    sames = [[swap(same_first, 2), swap(same_second, 2)], [swap(same, 2)]]
    others.append(swap(other, 3))

    whole = pltpu.HBM((rows, width), jnp.bfloat16)
    stack, piece = shape(3, size, width), shape(size, width)
    output_sems = pltpu.SemaphoreType.DMA((10,))
    first = (mines[0], nears[0], *sames[0], others[0])
    items, shares, small_far = call(
        functools.partial(score_kernel, heads, scale),
        "scores",
        [
            shape(EARLY, size, LANES),
            shape(math.prod(count for _, count in sizes), 8, LANES, dtype=wide),
            shape(size, LANES, dtype=wide),
        ],
        table, smalls[0], bias, *first,
        scratch=[pltpu.VMEM((8, LANES), wide)],
    )
    shares = lax.all_to_all(shares, tuple(axis for axis, _ in sizes), 0, 0, tiled=True)
    back, *grads = call(
        functools.partial(gradient_kernel, heads, scale),
        "gradients",
        [stack] + [whole] * 3,
        items, *first,
        scratch=[pltpu.VMEM((3, size, width), jnp.bfloat16), output_sems],
        hbm_out=range(1, 4),
    )
    first_back = swap(back, 1)

    kept, *back = call(
        functools.partial(whole_kernel, heads, scale),
        "scores_and_gradients",
        [stack] + [piece] * 3,
        table, smalls[1], small_far, mines[1], nears[1], *sames[1], others[1],
    )
    back = [swap(x, 1) for x in back]
    grads = [pltpu.with_memory_space_constraint(x, pltpu.HBM) for x in grads]
    *grads, bias = call(
        output_kernel,
        "outputs",
        [whole] * 3 + [shape(frames, heads, dtype=wide)],
        first_back, kept, *back, shares, *grads,
        scratch=[pltpu.VMEM((frames, heads), wide), output_sems],
        hbm=range(6, 9),
        hbm_out=range(4),
        aliases={6 + j: j for j in range(3)},
    )
    return (*[x.reshape(query_vectors.shape) for x in grads], bias.T)


def solution(mesh):
    sizes = tuple((axis, mesh.shape[axis]) for axis in ("tm", "patch"))

    def per_device(*args):
        heads, frames = args[4].shape
        fits = (
            mesh.shape["tm"] == 4
            and frames == 4
            and args[0].shape[1] == 1
            and heads * LANES == args[0].shape[3]
            and 3 * heads <= 2 * (LANES - 6 * heads)
            and heads % 2 == 0
            and args[0].shape[0] * args[0].shape[2] % (2 * TILE * CHUNKS) == 0
            and mesh.shape["patch"].bit_count() == 1
        )
        return (by_chips if fits else by_heads)(*args, sizes)

    vectors = P(None, "tm", "patch", None)
    return jax.shard_map(
        per_device,
        mesh=mesh,
        in_specs=(vectors,) * 4 + (P(),),
        out_specs=(vectors,) * 3 + (P(),),
        check_vma=False,
    )
```

```python
import functools
import math

import jax
import jax.numpy as jnp
from jax import lax
from jax.experimental import pallas as pl
from jax.experimental.pallas import tpu as pltpu
from jax.sharding import PartitionSpec as P

LANES = 128
TILE = 16
LITTLE = pl.CostEstimate(flops=1, bytes_accessed=1, transcendentals=0)
CHUNKS = 2


def score_table(bias_rows, frames):
    steps = jnp.arange(frames, dtype=jnp.int32)
    offsets = steps[:, None] - steps[None, :]
    onehot = (offsets[:, :, None] == steps[None, None, :]).astype(jnp.float32)
    table = jnp.einsum("hd,tud->htu", bias_rows, onehot, precision=lax.Precision.HIGHEST)
    return (table, offsets >= 0, onehot)


def attend_back(query_heads, key_heads, value_heads, grad_heads, bias_rows):
    frames = query_heads.shape[1]
    score_scale = 1.0 / math.sqrt(query_heads.shape[4])
    table, causal, onehot = score_table(bias_rows, frames)
    wide = jnp.float32
    scores = (
        jnp.einsum("atxhd,auxhd->axhtu", query_heads, key_heads, preferred_element_type=wide)
        * score_scale
        + table[None, None]
    )
    scores = jnp.where(causal, scores, -jnp.inf)
    row_max = jnp.max(scores, axis=-1, keepdims=True)
    expon = jnp.exp(scores - row_max)
    weights = expon / jnp.sum(expon, axis=-1, keepdims=True)
    weights_low = weights.astype(jnp.bfloat16)
    attended = jnp.einsum(
        "axhtu,auxhd->atxhd", weights_low, value_heads, preferred_element_type=wide
    )
    rowdot = jnp.einsum("atxhd,atxhd->axht", grad_heads, attended, preferred_element_type=wide)
    grad_weights = jnp.einsum(
        "atxhd,auxhd->axhtu", grad_heads, value_heads, preferred_element_type=wide
    )
    grad_scores = weights * (grad_weights - rowdot[..., None])
    bias_terms = jnp.einsum("axhtu,tud->axhd", grad_scores, onehot, precision=lax.Precision.HIGHEST)
    grad_low = grad_scores.astype(jnp.bfloat16)
    grad_query = (
        jnp.einsum("axhtu,auxhd->atxhd", grad_low, key_heads, preferred_element_type=wide)
        * score_scale
    ).astype(jnp.bfloat16)
    grad_key = (
        jnp.einsum("axhtu,atxhd->auxhd", grad_low, query_heads, preferred_element_type=wide)
        * score_scale
    ).astype(jnp.bfloat16)
    grad_value = jnp.einsum(
        "axhtu,atxhd->auxhd", weights_low, grad_heads, preferred_element_type=wide
    ).astype(jnp.bfloat16)
    return (grad_query, grad_key, grad_value, bias_terms)


def sum_everywhere(value, sizes):
    for axis, size in sizes:
        if size & (size - 1):
            value = lax.psum(value, axis)
            continue
        step = 1
        while step < size:
            other = lax.ppermute(value, axis, [(i, i ^ step) for i in range(size)])
            value = value + other
            step *= 2
    return value


def by_heads(query_vectors, key_vectors, value_vectors, grad_output, time_bias, sizes):
    head_count = time_bias.shape[0]
    frames = time_bias.shape[1]
    head_dim = query_vectors.shape[3] // head_count
    split_shape = query_vectors.shape[:3] + (head_count, head_dim)
    local_heads = head_count // lax.axis_size("tm")
    first_head = lax.axis_index("tm") * local_heads
    bias_rows = lax.dynamic_slice_in_dim(time_bias, first_head, local_heads, 0)
    spread = [
        lax.all_to_all(item.reshape(split_shape), "tm", split_axis=3, concat_axis=1, tiled=True)
        for item in (query_vectors, key_vectors, value_vectors, grad_output)
    ]
    *grads, bias_terms = attend_back(*spread, bias_rows)
    grads = [
        lax.all_to_all(item, "tm", split_axis=1, concat_axis=3, tiled=True).reshape(
            query_vectors.shape
        )
        for item in grads
    ]
    partial = lax.dynamic_update_slice_in_dim(
        jnp.zeros((head_count, frames), jnp.float32),
        jnp.sum(bias_terms, axis=(0, 1)),
        first_head,
        0,
    )
    return (*grads, sum_everywhere(partial, sizes))


def pair_dots(queries, keys, grads, values, pairs, heads):
    place = lax.broadcasted_iota(jnp.int32, (TILE, LANES), 1)
    held = [jnp.zeros((TILE, LANES), jnp.float32)] * (2 * len(pairs))
    for head in range(heads):
        at = slice(head * LANES, (head + 1) * LANES)
        here = place == head
        load = lambda refs: [ref[at].astype(jnp.float32) for ref in refs]
        q, k, o, v = load(queries), load(keys), load(grads), load(values)
        for j, (t, u) in enumerate(pairs):
            score = jnp.sum(q[t] * k[u], axis=1, keepdims=True)
            held[j] = jnp.where(here, score, held[j])
            gain = jnp.sum(o[t] * v[u], axis=1, keepdims=True)
            held[len(pairs) + j] = jnp.where(here, gain, held[len(pairs) + j])
    return held


def over_tiles(rows, body):
    pl.loop(0, rows // TILE)(lambda i: body(i * TILE))


def tile_at(start):
    return pl.ds(pl.multiple_of(start, TILE), TILE)


class Shifted:
    def __init__(self, ref, start):
        self.ref, self.start = ref, start

    def at_rows(self, row):
        return View(self.ref, tile_at(self.start + row))


class View:
    def __init__(self, ref, rows):
        self.ref, self.rows = ref, rows

    def __getitem__(self, lanes):
        return self.ref[self.rows, lanes]

    def __setitem__(self, lanes, value):
        self.ref[self.rows, lanes] = value


def tiles_of(refs, row):
    return tuple(ref.at_rows(row) for ref in refs)


def shifted(refs, start):
    return tuple(Shifted(ref, start) for ref in refs)


def soft_row(scores, gains):
    top = functools.reduce(jnp.maximum, scores)
    expon = [jnp.exp(item - top) for item in scores]
    total = functools.reduce(jnp.add, expon)
    weights = [item / total for item in expon]
    low = [item.astype(jnp.bfloat16) for item in weights]
    rowdot = functools.reduce(
        jnp.add, [a.astype(jnp.float32) * g for a, g in zip(low, gains)]
    )
    grads = [w * (g - rowdot) for w, g in zip(weights, gains)]
    return low, grads


LOCAL = ((0, 0), (1, 0), (1, 1))
CROSS = ((0, 0), (0, 1), (1, 0), (1, 1))


def unpack(packed, heads):
    return [packed if j == 0 else pltpu.roll(packed, LANES - heads * j, axis=1) for j in range(6)]


def bias_lines(terms):
    lines = []
    for items in terms:
        lines.append(
            jnp.sum(functools.reduce(jnp.add, items), axis=0, keepdims=True)
            if items
            else jnp.zeros((1, LANES), jnp.float32)
        )
    return jnp.concatenate(lines + [jnp.zeros((4, LANES), jnp.float32)], axis=0)


def early_rows(diag, scale, offset):
    score = lambda j, d: diag[j] * scale + offset[d]
    row0 = soft_row([score(0, 0)], [diag[3]])
    row1 = soft_row([score(1, 1), score(2, 0)], [diag[4], diag[5]])
    return row0, row1


def my_place():
    me = lax.axis_index("tm")
    return lax.rem(me, 2), lax.div(me, 2)


def with_frames(own, other, work):
    core, chip = my_place()
    for at_chip in range(2):
        pl.when((chip == at_chip) & (core == 0))(functools.partial(work, at_chip, own, other))
        pl.when((chip == at_chip) & (core == 1))(functools.partial(work, at_chip, other, own))


def chunk_start(chunk, size):
    return jnp.where(my_place()[1] == 0, chunk, CHUNKS - 1 - chunk) * size


def copy_chunks(sources, core, outs, sems):
    size = outs[0].shape[1]
    copies = []
    for c, out in enumerate(outs):
        start = pl.multiple_of(core * CHUNKS * size + chunk_start(c, size), TILE)
        for j, ref in enumerate(sources):
            copies.append(
                pltpu.make_async_copy(
                    ref.at[pl.ds(start, size)], out.at[j], sems.at[len(copies)]
                )
            )
    for copy in copies:
        copy.start()
    for copy in copies:
        copy.wait()


def take_far(refs, outs):
    chip = my_place()[1]

    def take(places):
        for out, place in zip(outs, places):
            for row in range(0, out.shape[0], TILE):
                rows = slice(row, row + TILE)
                out[rows, : refs[place].shape[1]] = refs[place][rows, :]

    pl.when(chip == 0)(lambda: take((1, 2)))
    pl.when(chip == 1)(lambda: take((0, 3)))


def fetch_theirs_kernel(q, k, v, o, *refs):
    nears, other, sems = refs[:CHUNKS], refs[CHUNKS], refs[CHUNKS + 1]
    copy_chunks((q, k, v, o), 1 - my_place()[0], nears, sems)
    take_far(planes(nears[CHUNKS - 1]), planes(other))


def fetch_mine_kernel(q, k, v, o, after, *refs):
    copy_chunks((q, k, v, o), my_place()[0], refs[:-1], refs[-1])


def packed_small(value, heads):
    used = 6 * heads
    place = lax.broadcasted_iota(jnp.int32, value.shape, 1)
    high = value.astype(jnp.bfloat16).astype(jnp.float32)
    middle = (value - high).astype(jnp.bfloat16).astype(jnp.float32)
    rest = (value - high) - middle
    first = jnp.where(place < used, high, pltpu.roll(rest, used, axis=1))
    second = jnp.where(place < used, middle, pltpu.roll(rest, 2 * used - LANES, axis=1))
    return first.astype(jnp.bfloat16), second.astype(jnp.bfloat16)


def unpacked_small(first, second, heads):
    used = 6 * heads
    first, second = first.astype(jnp.float32), second.astype(jnp.float32)
    place = lax.broadcasted_iota(jnp.int32, first.shape, 1)
    rest = jnp.where(
        place < LANES - used,
        pltpu.roll(first, LANES - used, axis=1),
        pltpu.roll(second, 2 * (LANES - used), axis=1),
    )
    return first + second + jnp.where(place < 3 * heads, rest, 0.0)


def local_kernel(heads, scale, table, *refs):
    mines, nears, theirs, refs = refs[:2], refs[2:4], refs[4], refs[5:]
    smalls, out_bias, other, sames = refs[:2], refs[2], refs[3], (refs[4:6], planes(refs[6]))
    core, chip = my_place()
    size, width = mines[0].shape[1:]
    offset = [table[d : d + 1, :] for d in range(4)]
    out_bias[...] = jnp.zeros_like(out_bias)

    def run(a, b, small):
        def tile(row):
            at, bt = tiles_of(a, row), tiles_of(b, row)
            held = pair_dots(
                (at[0], bt[0]), (at[1], bt[1]), (at[3], bt[3]), (at[2], bt[2]), LOCAL, heads
            )
            total = held[0]
            for j in range(1, 6):
                total = total + pltpu.roll(held[j], heads * j, axis=1)
            small[tile_at(row), :] = total
            (_, d0), (_, d1) = early_rows(held, scale, offset)
            lines = bias_lines([[d0[0], d1[1]], [d1[0]], [], []])
            out_bias[...] += jnp.where(chip == 0, lines, jnp.zeros_like(lines))

        over_tiles(size, tile)

    for mine, near, small in zip(mines, nears, smalls):
        own, neighbour = shifted(planes(mine), 0), shifted(planes(near), 0)
        pl.when(core == 0)(functools.partial(run, own, neighbour, small))
        pl.when(core == 1)(functools.partial(run, neighbour, own, small))

    take_far(planes(theirs), planes(other))
    for c, out in enumerate(sames):
        take_far(planes(mines[1 - c]), out)
        for row in range(0, size, TILE):
            rows = slice(row, row + TILE)
            parts = packed_small(smalls[1 - c][rows, :], heads)
            for ref, part in zip(sames[0], parts):
                ref[rows, width + c * LANES : width + (c + 1) * LANES] = part


EARLY, LATE = 14, 10


def score_tile(heads, scale, chip, a, b, table, small_own, small_far):
    offset = [table[d : d + 1, :] for d in range(4)]
    if chip == 0:
        queries, keys = ((a[4], a[5]), (b[4], b[5])), ((a[1], a[2]), (b[1], b[2]))
    else:
        queries, keys = ((a[0], a[3]), (b[0], b[3])), ((a[4], a[5]), (b[4], b[5]))
    held = pair_dots(
        [x[0] for x in queries], [x[0] for x in keys],
        [x[1] for x in queries], [x[1] for x in keys], CROSS, heads,
    )
    diag = unpack(small_far if chip == 0 else small_own, heads)
    score = lambda j, d: held[j] * scale + offset[d]
    p2, d2 = soft_row(
        [score(0, 2), score(1, 1), diag[0] * scale + offset[0]], [held[4], held[5], diag[3]]
    )
    p3, d3 = soft_row(
        [score(2, 3), score(3, 2), diag[1] * scale + offset[1], diag[2] * scale + offset[0]],
        [held[6], held[7], diag[4], diag[5]],
    )
    lines = bias_lines([[d2[2], d3[3]], [d2[1], d3[2]], [d2[0], d3[1]], [d3[0]]])
    if chip == 1:
        items = [d2[2], d3[2], d3[3], d2[0], d2[1], d3[0], d3[1], p2[2], p3[2], p3[3]]
    else:
        (p0, d0), (p1, d1) = early_rows(unpack(small_own, heads), scale, offset)
        items = [d0[0], d1[0], d1[1], d2[0], d2[1], d3[0], d3[1]]
        items += [p0[0], p1[0], p1[1], p2[0], p2[1], p3[0], p3[1]]
    return [item.astype(jnp.bfloat16) for item in items], lines


def gradient_tile(heads, scale, chip, a, b, items, out_a, out_b):
    width = 2 * LANES
    lines = -(-heads // TILE) * TILE
    line = lax.broadcasted_iota(jnp.int32, (lines, width), 0)
    head = lax.broadcasted_iota(jnp.int32, (lines, width), 1) // LANES
    zeros = jnp.zeros((LANES - lines, width), jnp.bfloat16)
    spread = jnp.concatenate(items, axis=0)

    for pair in range(heads // 2):
        at = slice(pair * width, (pair + 1) * width)
        pick = jnp.where(line == 2 * pair + head, 1.0, 0.0).astype(jnp.bfloat16)
        flat = jnp.dot(
            spread, jnp.concatenate([pick, zeros], axis=0), preferred_element_type=jnp.float32
        )
        w = [flat[j * TILE : (j + 1) * TILE, :] for j in range(len(items))]

        def put(ref, value):
            ref[at] = value.astype(jnp.bfloat16)

        def wide(*refs):
            return [ref[at].astype(jnp.float32) for ref in refs]

        if chip == 0:
            ka, kb = wide(a[1], b[1])
            put(out_a[0], w[0] * ka * scale)
            put(out_b[0], (w[1] * ka + w[2] * kb) * scale)
            for to, x, g, rate in ((1, 0, 0, scale), (2, 3, 7, 1.0)):
                xa, xb, x2, x3 = wide(a[x], b[x], a[3 + to], b[3 + to])
                for_a = w[g] * xa + w[g + 1] * xb + w[g + 3] * x2 + w[g + 5] * x3
                for_b = w[g + 2] * xb + w[g + 4] * x2 + w[g + 6] * x3
                put(out_a[to], for_a * rate)
                put(out_b[to], for_b * rate)
        else:
            k2, k3, k0, k1 = wide(a[1], b[1], a[4], b[4])
            put(out_a[0], (w[0] * k2 + w[3] * k0 + w[4] * k1) * scale)
            put(out_b[0], (w[1] * k2 + w[2] * k3 + w[5] * k0 + w[6] * k1) * scale)
            q2, q3, o2, o3 = wide(a[0], b[0], a[3], b[3])
            put(out_a[1], (w[0] * q2 + w[1] * q3) * scale)
            put(out_b[1], w[2] * q3 * scale)
            put(out_a[2], w[7] * o2 + w[8] * o3)
            put(out_b[2], w[9] * o3)


def planes(ref):
    return tuple(ref.at[j] for j in range(ref.shape[0]))


def frames_of(mine, near, far):
    *same, other = far
    return (
        shifted(planes(mine) + pair_of(same), 0),
        shifted(planes(near) + planes(other), 0),
    )


def pair_of(same):
    return tuple(same) if len(same) == 2 else planes(same[0])


def far_small(far, rows, width, heads, chunk):
    at = slice(width + chunk * LANES, width + (chunk + 1) * LANES)
    return unpacked_small(*(ref[rows, at] for ref in pair_of(far[:-1])), heads)


def score_kernel(heads, scale, table, small, bias, mine, near, *refs):
    far, (out_items, out_shares, out_small, out_lines), lines_ref = refs[:3], refs[3:7], refs[7]
    size, width = mine.shape[1:]
    lines_ref[...] = bias[...]

    def work(chip, a, b):
        def tile(row):
            rows = tile_at(row)
            items, lines = score_tile(
                heads, scale, chip, tiles_of(a, row), tiles_of(b, row), table,
                small[rows, :], far_small(far, rows, width, heads, 0),
            )
            out_small[rows, :] = far_small(far, rows, width, heads, 1)
            for j, item in enumerate(items):
                out_items[j, rows, :] = item
            lines_ref[...] += lines

        over_tiles(size, tile)

    with_frames(*frames_of(mine, near, far), work)
    out_lines[...] = lines_ref[...]
    for j in range(out_shares.shape[0]):
        out_shares[j] = lines_ref[: out_shares.shape[1], :]


def output_copies(which, piece, outs, chunk, sems, at, offset=0):
    half = outs[0].shape[0] // 2
    start = which * half + chunk_start(chunk, half // CHUNKS) + offset
    rows = pl.ds(pl.multiple_of(start, TILE), piece[0].shape[0])
    return [
        pltpu.make_async_copy(part, out.at[rows], sems.at[at + j])
        for j, (part, out) in enumerate(zip(piece, outs))
    ]


def gradient_kernel(heads, scale, items_ref, mine, near, *refs):
    far, out_others, outs, kept, given, sems = refs[:3], refs[3:5], refs[5:8], *refs[8:]
    own, neighbour = frames_of(mine, near, far)
    own_out, other_out = shifted(planes(kept), 0), shifted(planes(given), 0)

    def work(chip, a, b):
        out_a, out_b = (own_out, other_out) if a is own else (other_out, own_out)

        def tile(row):
            items = [items_ref[j, tile_at(row), :] for j in range(LATE if chip else EARLY)]
            gradient_tile(
                heads, scale, chip, tiles_of(a, row), tiles_of(b, row), items,
                tiles_of(out_a, row), tiles_of(out_b, row),
            )

        over_tiles(mine.shape[1], tile)

    with_frames(own, neighbour, work)
    copies = output_copies(my_place()[0], planes(kept), outs, 0, sems, 0)
    for copy in copies:
        copy.start()
    start = 0
    for out in out_others:
        for row in range(0, out.shape[1], TILE):
            for j in range(3):
                out[j, row : row + TILE, :] = given[j, start + row : start + row + TILE, :]
        start += out.shape[1]
    for copy in copies:
        copy.wait()


def whole_kernel(heads, scale, after, table, small, small_far, mine, near, *refs):
    far, out_own, out_others = refs[:2], refs[2], refs[3:6]
    own, neighbour = frames_of(mine, near, far)
    own_out, other_out = shifted(planes(out_own), 0), shifted(out_others, 0)

    def work(chip, a, b):
        out_a, out_b = (own_out, other_out) if a is own else (other_out, own_out)

        def tile(row):
            at, bt, rows = tiles_of(a, row), tiles_of(b, row), tile_at(row)
            items, _ = score_tile(
                heads, scale, chip, at, bt, table, small[rows, :], small_far[rows, :]
            )
            gradient_tile(
                heads, scale, chip, at, bt, items, tiles_of(out_a, row), tiles_of(out_b, row)
            )

        over_tiles(mine.shape[1], tile)

    with_frames(own, neighbour, work)


def output_kernel(*refs):
    first_backs, kept, back, shares = refs[:2], planes(refs[2]), refs[3:6], refs[6]
    outs, out_bias, total, sems = refs[10:13], *refs[13:]
    core = my_place()[0]
    copies = output_copies(core, kept, outs, 1, sems, 0)
    copies += output_copies(1 - core, back, outs, 1, sems, 3)
    offset = 0
    for j, ref in enumerate(first_backs):
        copies += output_copies(1 - core, planes(ref), outs, 0, sems, 6 + 3 * j, offset)
        offset += ref.shape[1]
    for copy in copies:
        copy.start()
    parts = [shares[j] for j in range(shares.shape[0])]
    while len(parts) > 1:
        parts = [a + b for a, b in zip(parts[::2], parts[1::2])]
    total[...] = parts[0][: total.shape[0], : total.shape[1]]
    copies.append(pltpu.make_async_copy(total, out_bias, sems.at[12]))
    copies[-1].start()
    for copy in copies:
        copy.wait()


def by_chips(query_vectors, key_vectors, value_vectors, grad_output, time_bias, sizes):
    heads, frames = time_bias.shape
    clips, _, patches, width = query_vectors.shape
    rows = clips * patches
    half = rows // 2
    size = half // CHUNKS
    scale = 1.0 / math.sqrt(width // heads)
    own = [
        pltpu.with_memory_space_constraint(x.reshape(rows, width), pltpu.HBM)
        for x in (query_vectors, key_vectors, value_vectors, grad_output)
    ]
    vmem_spec = pl.BlockSpec(memory_space=pltpu.VMEM)
    any_spec = pl.BlockSpec(memory_space=pl.ANY)

    def swap(x, bits):
        return lax.ppermute(x, "tm", [(i, i ^ bits) for i in range(4)])

    def shape(*dims, dtype=jnp.bfloat16):
        return jax.ShapeDtypeStruct(dims, dtype)

    def call(kernel, name, out_shape, *args, scratch=(), hbm=(), hbm_out=(), aliases={}):
        return pl.pallas_call(
            kernel,
            in_specs=[any_spec if j in hbm else vmem_spec for j in range(len(args))],
            out_specs=[any_spec if j in hbm_out else vmem_spec for j in range(len(out_shape))],
            out_shape=out_shape,
            scratch_shapes=scratch,
            input_output_aliases=aliases,
            compiler_params=pltpu.CompilerParams(vmem_limit_bytes=16 * 2**20),
            cost_estimate=LITTLE,
            name=name,
        )(*args)

    wide = jnp.float32
    lines = shape(8, LANES, dtype=wide)
    chunk_shape, far_shape = shape(4, size, width), shape(2, size, width)
    copies = [pltpu.SemaphoreType.DMA((4 * CHUNKS,))]
    table = jnp.pad(time_bias.T, ((0, 8 - frames), (0, LANES - heads)))

    *theirs, other = call(
        fetch_theirs_kernel, "fetch_theirs", [chunk_shape] * CHUNKS + [far_shape], *own,
        scratch=copies, hbm=range(4),
    )
    nears = [swap(x, 1) for x in theirs]
    others = [swap(other, 3)]
    mines = call(
        fetch_mine_kernel, "fetch_mine", [chunk_shape] * CHUNKS, *own, other,
        scratch=copies, hbm=range(5),
    )

    *smalls, bias, other, same_first, same_second, same = call(
        functools.partial(local_kernel, heads, scale),
        "local_scores",
        [shape(size, LANES, dtype=wide)] * CHUNKS
        + [lines, far_shape]
        + [shape(size, width + CHUNKS * LANES)] * 2
        + [far_shape],
        table, *mines, *nears, theirs[0],
    )
    sames = [[swap(same_first, 2), swap(same_second, 2)], [swap(same, 2)]]
    others.append(swap(other, 3))

    whole = pltpu.HBM((rows, width), jnp.bfloat16)
    stack, piece = shape(3, size, width), shape(size, width)
    output_sems = pltpu.SemaphoreType.DMA((13,))
    first = (mines[0], nears[0], *sames[0], others[0])
    items, shares, small_far, token = call(
        functools.partial(score_kernel, heads, scale),
        "scores",
        [
            shape(EARLY, size, LANES),
            shape(math.prod(count for _, count in sizes), 8, LANES, dtype=wide),
            shape(size, LANES, dtype=wide),
            lines,
        ],
        table, smalls[0], bias, *first,
        scratch=[pltpu.VMEM((8, LANES), wide)],
    )
    shares = lax.all_to_all(shares, tuple(axis for axis, _ in sizes), 0, 0, tiled=True)
    *back, grad_queries, grad_keys, grad_values = call(
        functools.partial(gradient_kernel, heads, scale),
        "gradients",
        [shape(3, size // 2, width)] * 2 + [whole] * 3,
        items, *first,
        scratch=[pltpu.VMEM((3, size, width), jnp.bfloat16)] * 2 + [output_sems],
        hbm_out=range(2, 5),
    )
    grads = (grad_queries, grad_keys, grad_values)
    first_backs = [swap(x, 1) for x in back]

    kept, *back = call(
        functools.partial(whole_kernel, heads, scale),
        "scores_and_gradients",
        [stack] + [piece] * 3,
        swap(token, 1), table, smalls[1], small_far, mines[1], nears[1], *sames[1], others[1],
    )
    back = [swap(x, 1) for x in back]
    grads = [pltpu.with_memory_space_constraint(x, pltpu.HBM) for x in grads]
    *grads, bias = call(
        output_kernel,
        "outputs",
        [whole] * 3 + [shape(frames, heads, dtype=wide)],
        *first_backs, kept, *back, shares, *grads,
        scratch=[pltpu.VMEM((frames, heads), wide), output_sems],
        hbm=range(7, 10),
        hbm_out=range(4),
        aliases={7 + j: j for j in range(3)},
    )
    return (*[x.reshape(query_vectors.shape) for x in grads], bias.T)


def solution(mesh):
    sizes = tuple((axis, mesh.shape[axis]) for axis in ("tm", "patch"))

    def per_device(*args):
        heads, frames = args[4].shape
        fits = (
            mesh.shape["tm"] == 4
            and frames == 4
            and args[0].shape[1] == 1
            and heads * LANES == args[0].shape[3]
            and 3 * heads <= 2 * (LANES - 6 * heads)
            and heads % 2 == 0
            and args[0].shape[0] * args[0].shape[2] % (2 * TILE * CHUNKS) == 0
            and mesh.shape["patch"].bit_count() == 1
        )
        return (by_chips if fits else by_heads)(*args, sizes)

    vectors = P(None, "tm", "patch", None)
    return jax.shard_map(
        per_device,
        mesh=mesh,
        in_specs=(vectors,) * 4 + (P(),),
        out_specs=(vectors,) * 3 + (P(),),
        check_vma=False,
    )
```

```python
import functools
import math

import jax
import jax.numpy as jnp
from jax import lax
from jax.experimental import pallas as pl
from jax.experimental.pallas import tpu as pltpu
from jax.sharding import PartitionSpec as P

LANES = 128
TILE = 16
LITTLE = pl.CostEstimate(flops=1, bytes_accessed=1, transcendentals=0)
CHUNKS = 2


def score_table(bias_rows, frames):
    steps = jnp.arange(frames, dtype=jnp.int32)
    offsets = steps[:, None] - steps[None, :]
    onehot = (offsets[:, :, None] == steps[None, None, :]).astype(jnp.float32)
    table = jnp.einsum("hd,tud->htu", bias_rows, onehot, precision=lax.Precision.HIGHEST)
    return (table, offsets >= 0, onehot)


def attend_back(query_heads, key_heads, value_heads, grad_heads, bias_rows):
    frames = query_heads.shape[1]
    score_scale = 1.0 / math.sqrt(query_heads.shape[4])
    table, causal, onehot = score_table(bias_rows, frames)
    wide = jnp.float32
    scores = (
        jnp.einsum("atxhd,auxhd->axhtu", query_heads, key_heads, preferred_element_type=wide)
        * score_scale
        + table[None, None]
    )
    scores = jnp.where(causal, scores, -jnp.inf)
    row_max = jnp.max(scores, axis=-1, keepdims=True)
    expon = jnp.exp(scores - row_max)
    weights = expon / jnp.sum(expon, axis=-1, keepdims=True)
    weights_low = weights.astype(jnp.bfloat16)
    attended = jnp.einsum(
        "axhtu,auxhd->atxhd", weights_low, value_heads, preferred_element_type=wide
    )
    rowdot = jnp.einsum("atxhd,atxhd->axht", grad_heads, attended, preferred_element_type=wide)
    grad_weights = jnp.einsum(
        "atxhd,auxhd->axhtu", grad_heads, value_heads, preferred_element_type=wide
    )
    grad_scores = weights * (grad_weights - rowdot[..., None])
    bias_terms = jnp.einsum("axhtu,tud->axhd", grad_scores, onehot, precision=lax.Precision.HIGHEST)
    grad_low = grad_scores.astype(jnp.bfloat16)
    grad_query = (
        jnp.einsum("axhtu,auxhd->atxhd", grad_low, key_heads, preferred_element_type=wide)
        * score_scale
    ).astype(jnp.bfloat16)
    grad_key = (
        jnp.einsum("axhtu,atxhd->auxhd", grad_low, query_heads, preferred_element_type=wide)
        * score_scale
    ).astype(jnp.bfloat16)
    grad_value = jnp.einsum(
        "axhtu,atxhd->auxhd", weights_low, grad_heads, preferred_element_type=wide
    ).astype(jnp.bfloat16)
    return (grad_query, grad_key, grad_value, bias_terms)


def sum_everywhere(value, sizes):
    for axis, size in sizes:
        if size & (size - 1):
            value = lax.psum(value, axis)
            continue
        step = 1
        while step < size:
            other = lax.ppermute(value, axis, [(i, i ^ step) for i in range(size)])
            value = value + other
            step *= 2
    return value


def by_heads(query_vectors, key_vectors, value_vectors, grad_output, time_bias, sizes):
    head_count = time_bias.shape[0]
    frames = time_bias.shape[1]
    head_dim = query_vectors.shape[3] // head_count
    split_shape = query_vectors.shape[:3] + (head_count, head_dim)
    local_heads = head_count // lax.axis_size("tm")
    first_head = lax.axis_index("tm") * local_heads
    bias_rows = lax.dynamic_slice_in_dim(time_bias, first_head, local_heads, 0)
    spread = [
        lax.all_to_all(item.reshape(split_shape), "tm", split_axis=3, concat_axis=1, tiled=True)
        for item in (query_vectors, key_vectors, value_vectors, grad_output)
    ]
    *grads, bias_terms = attend_back(*spread, bias_rows)
    grads = [
        lax.all_to_all(item, "tm", split_axis=1, concat_axis=3, tiled=True).reshape(
            query_vectors.shape
        )
        for item in grads
    ]
    partial = lax.dynamic_update_slice_in_dim(
        jnp.zeros((head_count, frames), jnp.float32),
        jnp.sum(bias_terms, axis=(0, 1)),
        first_head,
        0,
    )
    return (*grads, sum_everywhere(partial, sizes))


def pair_dots(queries, keys, grads, values, pairs, heads):
    place = lax.broadcasted_iota(jnp.int32, (TILE, LANES), 1)
    held = [jnp.zeros((TILE, LANES), jnp.float32)] * (2 * len(pairs))
    for head in range(heads):
        at = slice(head * LANES, (head + 1) * LANES)
        here = place == head
        load = lambda refs: [ref[at].astype(jnp.float32) for ref in refs]
        q, k, o, v = load(queries), load(keys), load(grads), load(values)
        for j, (t, u) in enumerate(pairs):
            score = jnp.sum(q[t] * k[u], axis=1, keepdims=True)
            held[j] = jnp.where(here, score, held[j])
            gain = jnp.sum(o[t] * v[u], axis=1, keepdims=True)
            held[len(pairs) + j] = jnp.where(here, gain, held[len(pairs) + j])
    return held


def over_tiles(rows, body):
    pl.loop(0, rows // TILE)(lambda i: body(i * TILE))


def tile_at(start):
    return pl.ds(pl.multiple_of(start, TILE), TILE)


class Shifted:
    def __init__(self, ref, start):
        self.ref, self.start = ref, start

    def at_rows(self, row):
        return View(self.ref, tile_at(self.start + row))


class View:
    def __init__(self, ref, rows):
        self.ref, self.rows = ref, rows

    def __getitem__(self, lanes):
        return self.ref[self.rows, lanes]

    def __setitem__(self, lanes, value):
        self.ref[self.rows, lanes] = value


def tiles_of(refs, row):
    return tuple(ref.at_rows(row) for ref in refs)


def shifted(refs, start):
    return tuple(Shifted(ref, start) for ref in refs)


def soft_row(scores, gains):
    top = functools.reduce(jnp.maximum, scores)
    expon = [jnp.exp(item - top) for item in scores]
    total = functools.reduce(jnp.add, expon)
    weights = [item / total for item in expon]
    low = [item.astype(jnp.bfloat16) for item in weights]
    rowdot = functools.reduce(
        jnp.add, [a.astype(jnp.float32) * g for a, g in zip(low, gains)]
    )
    grads = [w * (g - rowdot) for w, g in zip(weights, gains)]
    return low, grads


LOCAL = ((0, 0), (1, 0), (1, 1))
CROSS = ((0, 0), (0, 1), (1, 0), (1, 1))


def unpack(packed, heads):
    return [packed if j == 0 else pltpu.roll(packed, LANES - heads * j, axis=1) for j in range(6)]


def bias_lines(terms):
    lines = []
    for items in terms:
        lines.append(
            jnp.sum(functools.reduce(jnp.add, items), axis=0, keepdims=True)
            if items
            else jnp.zeros((1, LANES), jnp.float32)
        )
    return jnp.concatenate(lines + [jnp.zeros((4, LANES), jnp.float32)], axis=0)


def early_rows(diag, scale, offset):
    score = lambda j, d: diag[j] * scale + offset[d]
    row0 = soft_row([score(0, 0)], [diag[3]])
    row1 = soft_row([score(1, 1), score(2, 0)], [diag[4], diag[5]])
    return row0, row1


def my_place():
    me = lax.axis_index("tm")
    return lax.rem(me, 2), lax.div(me, 2)


def with_frames(own, other, work):
    core, chip = my_place()
    for at_chip in range(2):
        pl.when((chip == at_chip) & (core == 0))(functools.partial(work, at_chip, own, other))
        pl.when((chip == at_chip) & (core == 1))(functools.partial(work, at_chip, other, own))


def chunk_start(chunk, size):
    return jnp.where(my_place()[1] == 0, chunk, CHUNKS - 1 - chunk) * size


def copy_chunks(sources, core, outs, sems):
    size = outs[0].shape[1]
    copies = []
    for c, out in enumerate(outs):
        start = pl.multiple_of(core * CHUNKS * size + chunk_start(c, size), TILE)
        for j, ref in enumerate(sources):
            copies.append(
                pltpu.make_async_copy(
                    ref.at[pl.ds(start, size)], out.at[j], sems.at[len(copies)]
                )
            )
    for copy in copies:
        copy.start()
    for copy in copies:
        copy.wait()


def take_far(refs, outs):
    chip = my_place()[1]

    def take(places):
        for out, place in zip(outs, places):
            for row in range(0, out.shape[0], TILE):
                rows = slice(row, row + TILE)
                out[rows, : refs[place].shape[1]] = refs[place][rows, :]

    pl.when(chip == 0)(lambda: take((1, 2)))
    pl.when(chip == 1)(lambda: take((0, 3)))


def fetch_theirs_kernel(q, k, v, o, *refs):
    nears, other, sems = refs[:CHUNKS], refs[CHUNKS], refs[CHUNKS + 1]
    copy_chunks((q, k, v, o), 1 - my_place()[0], nears, sems)
    take_far(planes(nears[CHUNKS - 1]), planes(other))


def fetch_mine_kernel(q, k, v, o, after, *refs):
    copy_chunks((q, k, v, o), my_place()[0], refs[:-1], refs[-1])


def packed_small(value, heads):
    used = 6 * heads
    place = lax.broadcasted_iota(jnp.int32, value.shape, 1)
    high = value.astype(jnp.bfloat16).astype(jnp.float32)
    middle = (value - high).astype(jnp.bfloat16).astype(jnp.float32)
    rest = (value - high) - middle
    first = jnp.where(place < used, high, pltpu.roll(rest, used, axis=1))
    second = jnp.where(place < used, middle, pltpu.roll(rest, 2 * used - LANES, axis=1))
    return first.astype(jnp.bfloat16), second.astype(jnp.bfloat16)


def unpacked_small(first, second, heads):
    used = 6 * heads
    first, second = first.astype(jnp.float32), second.astype(jnp.float32)
    place = lax.broadcasted_iota(jnp.int32, first.shape, 1)
    rest = jnp.where(
        place < LANES - used,
        pltpu.roll(first, LANES - used, axis=1),
        pltpu.roll(second, 2 * (LANES - used), axis=1),
    )
    return first + second + jnp.where(place < 3 * heads, rest, 0.0)


def local_kernel(heads, scale, table, *refs):
    mines, nears, theirs, refs = refs[:2], refs[2:4], refs[4], refs[5:]
    smalls, out_bias, other, sames = refs[:2], refs[2], refs[3], (refs[4:6], planes(refs[6]))
    core, chip = my_place()
    size, width = mines[0].shape[1:]
    offset = [table[d : d + 1, :] for d in range(4)]
    out_bias[...] = jnp.zeros_like(out_bias)

    def run(a, b, small):
        def tile(row):
            at, bt = tiles_of(a, row), tiles_of(b, row)
            held = pair_dots(
                (at[0], bt[0]), (at[1], bt[1]), (at[3], bt[3]), (at[2], bt[2]), LOCAL, heads
            )
            total = held[0]
            for j in range(1, 6):
                total = total + pltpu.roll(held[j], heads * j, axis=1)
            small[tile_at(row), :] = total
            (_, d0), (_, d1) = early_rows(held, scale, offset)
            lines = bias_lines([[d0[0], d1[1]], [d1[0]], [], []])
            out_bias[...] += jnp.where(chip == 0, lines, jnp.zeros_like(lines))

        over_tiles(size, tile)

    for mine, near, small in zip(mines, nears, smalls):
        own, neighbour = shifted(planes(mine), 0), shifted(planes(near), 0)
        pl.when(core == 0)(functools.partial(run, own, neighbour, small))
        pl.when(core == 1)(functools.partial(run, neighbour, own, small))

    take_far(planes(theirs), planes(other))
    for c, out in enumerate(sames):
        take_far(planes(mines[1 - c]), out)
        for row in range(0, size, TILE):
            rows = slice(row, row + TILE)
            parts = packed_small(smalls[1 - c][rows, :], heads)
            for ref, part in zip(sames[0], parts):
                ref[rows, width + c * LANES : width + (c + 1) * LANES] = part


EARLY, LATE = 14, 10


def score_tile(heads, scale, chip, a, b, table, small_own, small_far):
    offset = [table[d : d + 1, :] for d in range(4)]
    if chip == 0:
        queries, keys = ((a[4], a[5]), (b[4], b[5])), ((a[1], a[2]), (b[1], b[2]))
    else:
        queries, keys = ((a[0], a[3]), (b[0], b[3])), ((a[4], a[5]), (b[4], b[5]))
    held = pair_dots(
        [x[0] for x in queries], [x[0] for x in keys],
        [x[1] for x in queries], [x[1] for x in keys], CROSS, heads,
    )
    diag = unpack(small_far if chip == 0 else small_own, heads)
    score = lambda j, d: held[j] * scale + offset[d]
    p2, d2 = soft_row(
        [score(0, 2), score(1, 1), diag[0] * scale + offset[0]], [held[4], held[5], diag[3]]
    )
    p3, d3 = soft_row(
        [score(2, 3), score(3, 2), diag[1] * scale + offset[1], diag[2] * scale + offset[0]],
        [held[6], held[7], diag[4], diag[5]],
    )
    lines = bias_lines([[d2[2], d3[3]], [d2[1], d3[2]], [d2[0], d3[1]], [d3[0]]])
    if chip == 1:
        items = [d2[2], d3[2], d3[3], d2[0], d2[1], d3[0], d3[1], p2[2], p3[2], p3[3]]
    else:
        (p0, d0), (p1, d1) = early_rows(unpack(small_own, heads), scale, offset)
        items = [d0[0], d1[0], d1[1], d2[0], d2[1], d3[0], d3[1]]
        items += [p0[0], p1[0], p1[1], p2[0], p2[1], p3[0], p3[1]]
    return [item.astype(jnp.bfloat16) for item in items], lines


def gradient_tile(heads, scale, chip, a, b, items, out_a, out_b):
    width = 2 * LANES
    lines = -(-heads // TILE) * TILE
    line = lax.broadcasted_iota(jnp.int32, (lines, width), 0)
    head = lax.broadcasted_iota(jnp.int32, (lines, width), 1) // LANES
    zeros = jnp.zeros((LANES - lines, width), jnp.bfloat16)
    spread = jnp.concatenate(items, axis=0)

    for pair in range(heads // 2):
        at = slice(pair * width, (pair + 1) * width)
        pick = jnp.where(line == 2 * pair + head, 1.0, 0.0).astype(jnp.bfloat16)
        flat = jnp.dot(
            spread, jnp.concatenate([pick, zeros], axis=0), preferred_element_type=jnp.float32
        )
        w = [flat[j * TILE : (j + 1) * TILE, :] for j in range(len(items))]

        def put(ref, value):
            ref[at] = value.astype(jnp.bfloat16)

        def wide(*refs):
            return [ref[at].astype(jnp.float32) for ref in refs]

        if chip == 0:
            ka, kb = wide(a[1], b[1])
            put(out_a[0], w[0] * ka * scale)
            put(out_b[0], (w[1] * ka + w[2] * kb) * scale)
            for to, x, g, rate in ((1, 0, 0, scale), (2, 3, 7, 1.0)):
                xa, xb, x2, x3 = wide(a[x], b[x], a[3 + to], b[3 + to])
                for_a = w[g] * xa + w[g + 1] * xb + w[g + 3] * x2 + w[g + 5] * x3
                for_b = w[g + 2] * xb + w[g + 4] * x2 + w[g + 6] * x3
                put(out_a[to], for_a * rate)
                put(out_b[to], for_b * rate)
        else:
            k2, k3, k0, k1 = wide(a[1], b[1], a[4], b[4])
            put(out_a[0], (w[0] * k2 + w[3] * k0 + w[4] * k1) * scale)
            put(out_b[0], (w[1] * k2 + w[2] * k3 + w[5] * k0 + w[6] * k1) * scale)
            q2, q3, o2, o3 = wide(a[0], b[0], a[3], b[3])
            put(out_a[1], (w[0] * q2 + w[1] * q3) * scale)
            put(out_b[1], w[2] * q3 * scale)
            put(out_a[2], w[7] * o2 + w[8] * o3)
            put(out_b[2], w[9] * o3)


def planes(ref):
    return tuple(ref.at[j] for j in range(ref.shape[0]))


def frames_of(mine, near, far):
    *same, other = far
    return (
        shifted(planes(mine) + pair_of(same), 0),
        shifted(planes(near) + planes(other), 0),
    )


def pair_of(same):
    return tuple(same) if len(same) == 2 else planes(same[0])


def far_small(far, rows, width, heads, chunk):
    at = slice(width + chunk * LANES, width + (chunk + 1) * LANES)
    return unpacked_small(*(ref[rows, at] for ref in pair_of(far[:-1])), heads)


def first_kernel(heads, scale, table, small, bias, mine, near, *refs):
    far, kept, out_others, out_small, out_shares = refs[:3], refs[3], refs[4:6], refs[6], refs[7]
    items_ref, shares, lines_ref, given, sem = refs[8:]
    size, width = mine.shape[1:]
    own, neighbour = frames_of(mine, near, far)
    own_out, other_out = shifted(planes(kept), 0), shifted(planes(given), 0)
    lines_ref[...] = bias[...]

    def scores(chip, a, b):
        def tile(row):
            rows = tile_at(row)
            items, lines = score_tile(
                heads, scale, chip, tiles_of(a, row), tiles_of(b, row), table,
                small[rows, :], far_small(far, rows, width, heads, 0),
            )
            out_small[rows, :] = far_small(far, rows, width, heads, 1)
            for j, item in enumerate(items):
                items_ref[j, rows, :] = item
            lines_ref[...] += lines

        over_tiles(size, tile)

    def gradients(chip, a, b):
        out_a, out_b = (own_out, other_out) if a is own else (other_out, own_out)

        def tile(row):
            items = [items_ref[j, tile_at(row), :] for j in range(LATE if chip else EARLY)]
            gradient_tile(
                heads, scale, chip, tiles_of(a, row), tiles_of(b, row), items,
                tiles_of(out_a, row), tiles_of(out_b, row),
            )

        over_tiles(size, tile)

    with_frames(own, neighbour, scores)
    for j in range(shares.shape[0]):
        shares[j] = lines_ref[...]
    copy = pltpu.make_async_copy(shares, out_shares, sem)
    copy.start()
    with_frames(own, neighbour, gradients)
    start = 0
    for out in out_others:
        for row in range(0, out.shape[1], TILE):
            for j in range(3):
                out[j, row : row + TILE, :] = given[j, start + row : start + row + TILE, :]
        start += out.shape[1]
    copy.wait()


def output_copies(which, piece, outs, chunk, sems, at, offset=0):
    half = outs[0].shape[0] // 2
    start = which * half + chunk_start(chunk, half // CHUNKS) + offset
    rows = pl.ds(pl.multiple_of(start, TILE), piece[0].shape[0])
    return [
        pltpu.make_async_copy(part, out.at[rows], sems.at[at + j])
        for j, (part, out) in enumerate(zip(piece, outs))
    ]


def last_kernel(heads, scale, table, small, small_far, first_kept, mine, near, *refs):
    far, out_own, out_others, outs, sems = refs[:2], refs[2], refs[3:6], refs[6:9], refs[9]
    own, neighbour = frames_of(mine, near, far)
    own_out, other_out = shifted(planes(out_own), 0), shifted(out_others, 0)
    copies = output_copies(my_place()[0], planes(first_kept), outs, 0, sems, 0)
    for copy in copies:
        copy.start()

    def work(chip, a, b):
        out_a, out_b = (own_out, other_out) if a is own else (other_out, own_out)

        def tile(row):
            at, bt, rows = tiles_of(a, row), tiles_of(b, row), tile_at(row)
            items, _ = score_tile(
                heads, scale, chip, at, bt, table, small[rows, :], small_far[rows, :]
            )
            gradient_tile(
                heads, scale, chip, at, bt, items, tiles_of(out_a, row), tiles_of(out_b, row)
            )

        over_tiles(mine.shape[1], tile)

    with_frames(own, neighbour, work)
    for copy in copies:
        copy.wait()


def output_kernel(*refs):
    first_backs, kept, back, shares = refs[:2], planes(refs[2]), refs[3:6], refs[6]
    outs, out_bias, total, sems = refs[10:13], *refs[13:]
    core = my_place()[0]
    copies = output_copies(core, kept, outs, 1, sems, 0)
    copies += output_copies(1 - core, back, outs, 1, sems, 3)
    offset = 0
    for j, ref in enumerate(first_backs):
        copies += output_copies(1 - core, planes(ref), outs, 0, sems, 6 + 3 * j, offset)
        offset += ref.shape[1]
    for copy in copies:
        copy.start()
    parts = [shares[j] for j in range(shares.shape[0])]
    while len(parts) > 1:
        parts = [a + b for a, b in zip(parts[::2], parts[1::2])]
    total[...] = parts[0][: total.shape[0], : total.shape[1]]
    copies.append(pltpu.make_async_copy(total, out_bias, sems.at[12]))
    copies[-1].start()
    for copy in copies:
        copy.wait()


def by_chips(query_vectors, key_vectors, value_vectors, grad_output, time_bias, sizes):
    heads, frames = time_bias.shape
    clips, _, patches, width = query_vectors.shape
    rows = clips * patches
    half = rows // 2
    size = half // CHUNKS
    scale = 1.0 / math.sqrt(width // heads)
    own = [
        pltpu.with_memory_space_constraint(x.reshape(rows, width), pltpu.HBM)
        for x in (query_vectors, key_vectors, value_vectors, grad_output)
    ]
    vmem_spec = pl.BlockSpec(memory_space=pltpu.VMEM)
    any_spec = pl.BlockSpec(memory_space=pl.ANY)

    def swap(x, bits):
        return lax.ppermute(x, "tm", [(i, i ^ bits) for i in range(4)])

    def shape(*dims, dtype=jnp.bfloat16):
        return jax.ShapeDtypeStruct(dims, dtype)

    def call(kernel, name, out_shape, *args, scratch=(), hbm=(), hbm_out=(), aliases={}):
        return pl.pallas_call(
            kernel,
            in_specs=[any_spec if j in hbm else vmem_spec for j in range(len(args))],
            out_specs=[any_spec if j in hbm_out else vmem_spec for j in range(len(out_shape))],
            out_shape=out_shape,
            scratch_shapes=scratch,
            input_output_aliases=aliases,
            compiler_params=pltpu.CompilerParams(vmem_limit_bytes=16 * 2**20),
            cost_estimate=LITTLE,
            name=name,
        )(*args)

    wide = jnp.float32
    lines = shape(8, LANES, dtype=wide)
    chunk_shape, far_shape = shape(4, size, width), shape(2, size, width)
    copies = [pltpu.SemaphoreType.DMA((4 * CHUNKS,))]
    table = jnp.pad(time_bias.T, ((0, 8 - frames), (0, LANES - heads)))

    *theirs, other = call(
        fetch_theirs_kernel, "fetch_theirs", [chunk_shape] * CHUNKS + [far_shape], *own,
        scratch=copies, hbm=range(4),
    )
    nears = [swap(x, 1) for x in theirs]
    others = [swap(other, 3)]
    mines = call(
        fetch_mine_kernel, "fetch_mine", [chunk_shape] * CHUNKS, *own, other,
        scratch=copies, hbm=range(5),
    )

    *smalls, bias, other, same_first, same_second, same = call(
        functools.partial(local_kernel, heads, scale),
        "local_scores",
        [shape(size, LANES, dtype=wide)] * CHUNKS
        + [lines, far_shape]
        + [shape(size, width + CHUNKS * LANES)] * 2
        + [far_shape],
        table, *mines, *nears, theirs[0],
    )
    sames = [[swap(same_first, 2), swap(same_second, 2)], [swap(same, 2)]]
    others.append(swap(other, 3))

    whole = pltpu.HBM((rows, width), jnp.bfloat16)
    stack, piece = shape(3, size, width), shape(size, width)
    everyone = shape(math.prod(count for _, count in sizes), 8, LANES, dtype=wide)
    output_sems = pltpu.SemaphoreType.DMA((13,))
    first_kept, *back, small_far, shares = call(
        functools.partial(first_kernel, heads, scale),
        "first_chunk",
        [stack] + [shape(3, size // 2, width)] * 2 + [shape(size, LANES, dtype=wide), everyone],
        table, smalls[0], bias, mines[0], nears[0], *sames[0], others[0],
        scratch=[
            pltpu.VMEM((EARLY, size, LANES), jnp.bfloat16),
            pltpu.VMEM(everyone.shape, wide),
            pltpu.VMEM((8, LANES), wide),
            pltpu.VMEM((3, size, width), jnp.bfloat16),
            pltpu.SemaphoreType.DMA,
        ],
        hbm_out=(4,),
    )
    shares = lax.all_to_all(shares, tuple(axis for axis, _ in sizes), 0, 0, tiled=True)
    first_backs = [swap(x, 1) for x in back]

    kept, *rest = call(
        functools.partial(last_kernel, heads, scale),
        "last_chunk",
        [stack] + [piece] * 3 + [whole] * 3,
        table, smalls[1], small_far, first_kept, mines[1], nears[1], *sames[1], others[1],
        scratch=[output_sems],
        hbm_out=range(4, 7),
    )
    back = [swap(x, 1) for x in rest[:3]]
    grads = [pltpu.with_memory_space_constraint(x, pltpu.HBM) for x in rest[3:]]
    *grads, bias = call(
        output_kernel,
        "outputs",
        [whole] * 3 + [shape(frames, heads, dtype=wide)],
        *first_backs, kept, *back, shares, *grads,
        scratch=[pltpu.VMEM((frames, heads), wide), output_sems],
        hbm=range(7, 10),
        hbm_out=range(4),
        aliases={7 + j: j for j in range(3)},
    )
    return (*[x.reshape(query_vectors.shape) for x in grads], bias.T)


def solution(mesh):
    sizes = tuple((axis, mesh.shape[axis]) for axis in ("tm", "patch"))

    def per_device(*args):
        heads, frames = args[4].shape
        fits = (
            mesh.shape["tm"] == 4
            and frames == 4
            and args[0].shape[1] == 1
            and heads * LANES == args[0].shape[3]
            and 3 * heads <= 2 * (LANES - 6 * heads)
            and heads % 2 == 0
            and args[0].shape[0] * args[0].shape[2] % (2 * TILE * CHUNKS) == 0
            and mesh.shape["patch"].bit_count() == 1
        )
        return (by_chips if fits else by_heads)(*args, sizes)

    vectors = P(None, "tm", "patch", None)
    return jax.shard_map(
        per_device,
        mesh=mesh,
        in_specs=(vectors,) * 4 + (P(),),
        out_specs=(vectors,) * 3 + (P(),),
        check_vma=False,
    )
```

```python
import functools
import math

import jax
import jax.numpy as jnp
from jax import lax
from jax.experimental import pallas as pl
from jax.experimental.pallas import tpu as pltpu
from jax.sharding import PartitionSpec as P

LANES = 128
TILE = 16
LITTLE = pl.CostEstimate(flops=1, bytes_accessed=1, transcendentals=0)
CHUNKS = 2


def score_table(bias_rows, frames):
    steps = jnp.arange(frames, dtype=jnp.int32)
    offsets = steps[:, None] - steps[None, :]
    onehot = (offsets[:, :, None] == steps[None, None, :]).astype(jnp.float32)
    table = jnp.einsum("hd,tud->htu", bias_rows, onehot, precision=lax.Precision.HIGHEST)
    return (table, offsets >= 0, onehot)


def attend_back(query_heads, key_heads, value_heads, grad_heads, bias_rows):
    frames = query_heads.shape[1]
    score_scale = 1.0 / math.sqrt(query_heads.shape[4])
    table, causal, onehot = score_table(bias_rows, frames)
    wide = jnp.float32
    scores = (
        jnp.einsum("atxhd,auxhd->axhtu", query_heads, key_heads, preferred_element_type=wide)
        * score_scale
        + table[None, None]
    )
    scores = jnp.where(causal, scores, -jnp.inf)
    row_max = jnp.max(scores, axis=-1, keepdims=True)
    expon = jnp.exp(scores - row_max)
    weights = expon / jnp.sum(expon, axis=-1, keepdims=True)
    weights_low = weights.astype(jnp.bfloat16)
    attended = jnp.einsum(
        "axhtu,auxhd->atxhd", weights_low, value_heads, preferred_element_type=wide
    )
    rowdot = jnp.einsum("atxhd,atxhd->axht", grad_heads, attended, preferred_element_type=wide)
    grad_weights = jnp.einsum(
        "atxhd,auxhd->axhtu", grad_heads, value_heads, preferred_element_type=wide
    )
    grad_scores = weights * (grad_weights - rowdot[..., None])
    bias_terms = jnp.einsum("axhtu,tud->axhd", grad_scores, onehot, precision=lax.Precision.HIGHEST)
    grad_low = grad_scores.astype(jnp.bfloat16)
    grad_query = (
        jnp.einsum("axhtu,auxhd->atxhd", grad_low, key_heads, preferred_element_type=wide)
        * score_scale
    ).astype(jnp.bfloat16)
    grad_key = (
        jnp.einsum("axhtu,atxhd->auxhd", grad_low, query_heads, preferred_element_type=wide)
        * score_scale
    ).astype(jnp.bfloat16)
    grad_value = jnp.einsum(
        "axhtu,atxhd->auxhd", weights_low, grad_heads, preferred_element_type=wide
    ).astype(jnp.bfloat16)
    return (grad_query, grad_key, grad_value, bias_terms)


def sum_everywhere(value, sizes):
    for axis, size in sizes:
        if size & (size - 1):
            value = lax.psum(value, axis)
            continue
        step = 1
        while step < size:
            other = lax.ppermute(value, axis, [(i, i ^ step) for i in range(size)])
            value = value + other
            step *= 2
    return value


def by_heads(query_vectors, key_vectors, value_vectors, grad_output, time_bias, sizes):
    head_count = time_bias.shape[0]
    frames = time_bias.shape[1]
    head_dim = query_vectors.shape[3] // head_count
    split_shape = query_vectors.shape[:3] + (head_count, head_dim)
    local_heads = head_count // lax.axis_size("tm")
    first_head = lax.axis_index("tm") * local_heads
    bias_rows = lax.dynamic_slice_in_dim(time_bias, first_head, local_heads, 0)
    spread = [
        lax.all_to_all(item.reshape(split_shape), "tm", split_axis=3, concat_axis=1, tiled=True)
        for item in (query_vectors, key_vectors, value_vectors, grad_output)
    ]
    *grads, bias_terms = attend_back(*spread, bias_rows)
    grads = [
        lax.all_to_all(item, "tm", split_axis=1, concat_axis=3, tiled=True).reshape(
            query_vectors.shape
        )
        for item in grads
    ]
    partial = lax.dynamic_update_slice_in_dim(
        jnp.zeros((head_count, frames), jnp.float32),
        jnp.sum(bias_terms, axis=(0, 1)),
        first_head,
        0,
    )
    return (*grads, sum_everywhere(partial, sizes))


def pair_dots(queries, keys, grads, values, pairs, heads):
    place = lax.broadcasted_iota(jnp.int32, (TILE, LANES), 1)
    held = [jnp.zeros((TILE, LANES), jnp.float32)] * (2 * len(pairs))
    for head in range(heads):
        at = slice(head * LANES, (head + 1) * LANES)
        here = place == head
        load = lambda refs, used: {j: refs[j][at].astype(jnp.float32) for j in used}
        late, early = {t for t, _ in pairs}, {u for _, u in pairs}
        q, k = load(queries, sorted(late)), load(keys, sorted(early))
        o, v = load(grads, sorted(late)), load(values, sorted(early))
        for j, (t, u) in enumerate(pairs):
            score = jnp.sum(q[t] * k[u], axis=1, keepdims=True)
            held[j] = jnp.where(here, score, held[j])
            gain = jnp.sum(o[t] * v[u], axis=1, keepdims=True)
            held[len(pairs) + j] = jnp.where(here, gain, held[len(pairs) + j])
    return held


def over_tiles(rows, body):
    pl.loop(0, rows // TILE)(lambda i: body(i * TILE))


def tile_at(start):
    return pl.ds(pl.multiple_of(start, TILE), TILE)


class Shifted:
    def __init__(self, ref, start):
        self.ref, self.start = ref, start

    def at_rows(self, row):
        return View(self.ref, tile_at(self.start + row))


class View:
    def __init__(self, ref, rows):
        self.ref, self.rows = ref, rows

    def __getitem__(self, lanes):
        return self.ref[self.rows, lanes]

    def __setitem__(self, lanes, value):
        self.ref[self.rows, lanes] = value


def tiles_of(refs, row):
    return tuple(ref if ref is None else ref.at_rows(row) for ref in refs)


def shifted(refs, start):
    return tuple(ref if ref is None else Shifted(ref, start) for ref in refs)


def soft_row(scores, gains):
    top = functools.reduce(jnp.maximum, scores)
    expon = [jnp.exp(item - top) for item in scores]
    total = functools.reduce(jnp.add, expon)
    weights = [item / total for item in expon]
    low = [item.astype(jnp.bfloat16) for item in weights]
    rowdot = functools.reduce(
        jnp.add, [a.astype(jnp.float32) * g for a, g in zip(low, gains)]
    )
    grads = [w * (g - rowdot) for w, g in zip(weights, gains)]
    return low, grads


LOCAL = ((0, 0), (1, 0), (1, 1))
CROSS = ((0, 0), (0, 1), (1, 0), (1, 1))


def unpack(packed, heads, count=6):
    return [
        packed if j == 0 else pltpu.roll(packed, LANES - heads * j, axis=1) for j in range(count)
    ]


def bias_lines(terms):
    lines = []
    for items in terms:
        lines.append(
            jnp.sum(functools.reduce(jnp.add, items), axis=0, keepdims=True)
            if items
            else jnp.zeros((1, LANES), jnp.float32)
        )
    return jnp.concatenate(lines + [jnp.zeros((4, LANES), jnp.float32)], axis=0)


def early_rows(diag, scale, offset):
    score = lambda j, d: diag[j] * scale + offset[d]
    row0 = soft_row([score(0, 0)], [diag[3]])
    row1 = soft_row([score(1, 1), score(2, 0)], [diag[4], diag[5]])
    return row0, row1


def my_place():
    me = lax.axis_index("tm")
    return lax.rem(me, 2), lax.div(me, 2)


def with_frames(own, other, work):
    core, chip = my_place()
    for at_chip in range(2):
        pl.when((chip == at_chip) & (core == 0))(functools.partial(work, at_chip, own, other))
        pl.when((chip == at_chip) & (core == 1))(functools.partial(work, at_chip, other, own))


def chunk_start(chunk, size):
    return jnp.where(my_place()[1] == 0, chunk, CHUNKS - 1 - chunk) * size


def copy_chunks(sources, core, outs, sems):
    size = outs[0].shape[1]
    copies = []
    for c, out in enumerate(outs):
        start = pl.multiple_of(core * CHUNKS * size + chunk_start(c, size), TILE)
        for j, ref in enumerate(sources):
            copies.append(
                pltpu.make_async_copy(
                    ref.at[pl.ds(start, size)], out.at[j], sems.at[len(copies)]
                )
            )
    for copy in copies:
        copy.start()
    for copy in copies:
        copy.wait()


def take_far(refs, outs):
    chip = my_place()[1]

    def take(places):
        for out, place in zip(outs, places):
            for row in range(0, out.shape[0], TILE):
                rows = slice(row, row + TILE)
                out[rows, : refs[place].shape[1]] = refs[place][rows, :]

    pl.when(chip == 0)(lambda: take((1, 2)))
    pl.when(chip == 1)(lambda: take((0, 3)))


def fetch_theirs_kernel(q, k, v, o, *refs):
    nears, other, sems = refs[:CHUNKS], refs[CHUNKS], refs[CHUNKS + 1]
    copy_chunks((q, k, v, o), 1 - my_place()[0], nears, sems)
    take_far(planes(nears[CHUNKS - 1]), planes(other))


def fetch_mine_kernel(q, k, v, o, after, *refs):
    copy_chunks((q, k, v, o), my_place()[0], refs[:-1], refs[-1])


def packed_small(value, heads):
    used = 6 * heads
    place = lax.broadcasted_iota(jnp.int32, value.shape, 1)
    high = value.astype(jnp.bfloat16).astype(jnp.float32)
    middle = (value - high).astype(jnp.bfloat16).astype(jnp.float32)
    rest = (value - high) - middle
    first = jnp.where(place < used, high, pltpu.roll(rest, used, axis=1))
    second = jnp.where(place < used, middle, pltpu.roll(rest, 2 * used - LANES, axis=1))
    return first.astype(jnp.bfloat16), second.astype(jnp.bfloat16)


def unpacked_small(first, second, heads):
    used = 6 * heads
    first, second = first.astype(jnp.float32), second.astype(jnp.float32)
    place = lax.broadcasted_iota(jnp.int32, first.shape, 1)
    rest = jnp.where(
        place < LANES - used,
        pltpu.roll(first, LANES - used, axis=1),
        pltpu.roll(second, 2 * (LANES - used), axis=1),
    )
    return first + second + jnp.where(place < 3 * heads, rest, 0.0)


def local_kernel(heads, scale, table, *refs):
    mines, nears, theirs, refs = refs[:2], refs[2:4], refs[4], refs[5:]
    smalls, out_bias, other, sames = refs[:2], refs[2], refs[3], (refs[4:6], planes(refs[6]))
    core, chip = my_place()
    size, width = mines[0].shape[1:]
    offset = [table[d : d + 1, :] for d in range(4)]
    out_bias[...] = jnp.zeros_like(out_bias)

    def run(a, b, small):
        def tile(row):
            at, bt = tiles_of(a, row), tiles_of(b, row)
            held = pair_dots(
                (at[0], bt[0]), (at[1], bt[1]), (at[3], bt[3]), (at[2], bt[2]), LOCAL, heads
            )
            total = held[0]
            for j in range(1, 6):
                total = total + pltpu.roll(held[j], heads * j, axis=1)
            small[tile_at(row), :] = total
            (_, d0), (_, d1) = early_rows(held, scale, offset)
            lines = bias_lines([[d0[0], d1[1]], [d1[0]], [], []])
            out_bias[...] += jnp.where(chip == 0, lines, jnp.zeros_like(lines))

        over_tiles(size, tile)

    for mine, near, small in zip(mines, nears, smalls):
        own, neighbour = shifted(planes(mine), 0), shifted(planes(near), 0)
        pl.when(core == 0)(functools.partial(run, own, neighbour, small))
        pl.when(core == 1)(functools.partial(run, neighbour, own, small))

    take_far(planes(theirs), planes(other))
    for c, out in enumerate(sames):
        take_far(planes(mines[1 - c]), out)
        for row in range(0, size, TILE):
            rows = slice(row, row + TILE)
            parts = packed_small(smalls[1 - c][rows, :], heads)
            for ref, part in zip(sames[0], parts):
                ref[rows, width + c * LANES : width + (c + 1) * LANES] = part


EARLY, LATE = 14, 10


def cross_sides(chip, a, b):
    if chip == 0:
        return ((a[4], a[5]), (b[4], b[5])), ((a[1], a[2]), (b[1], b[2]))
    return ((a[0], a[3]), (b[0], b[3])), ((a[4], a[5]), (b[4], b[5]))


def far_pairs(chip, parity):
    return [pair for pair in CROSS if pair[chip] == parity]


def cross_dots(queries, keys, pairs, heads):
    return pair_dots(
        [x[0] for x in queries], [x[0] for x in keys],
        [x[1] for x in queries], [x[1] for x in keys], pairs, heads,
    )


def piece_kernel(heads, same, mine, near, *refs):
    far, out = refs[:-1], refs[-1]
    piece = far if len(far) == 2 else planes(far[0])
    own, other = planes(mine), planes(near)
    if same:
        own, other = own + piece, other + (None, None)
    else:
        own, other = own + (None, None), other + piece
    own, other = shifted(own, 0), shifted(other, 0)

    def work(chip, a, b):
        parity = int((a is own) != same)

        def tile(row):
            queries, keys = cross_sides(chip, tiles_of(a, row), tiles_of(b, row))
            held = cross_dots(queries, keys, far_pairs(chip, parity), heads)
            total = held[0]
            for j in range(1, 4):
                total = total + pltpu.roll(held[j], heads * j, axis=1)
            out[tile_at(row), :] = total

        over_tiles(out.shape[0], tile)

    with_frames(own, other, work)


def score_tile(heads, scale, chip, a, b, table, small_own, small_far, known, parity):
    offset = [table[d : d + 1, :] for d in range(4)]
    queries, keys = cross_sides(chip, a, b)
    held = [None] * 8
    for pairs, values in (
        (far_pairs(chip, parity), known),
        (far_pairs(chip, 1 - parity), None),
    ):
        if values is None:
            values = cross_dots(queries, keys, pairs, heads)
        for j, pair in enumerate(pairs):
            held[CROSS.index(pair)] = values[j]
            held[4 + CROSS.index(pair)] = values[2 + j]
    diag = unpack(small_far if chip == 0 else small_own, heads)
    score = lambda j, d: held[j] * scale + offset[d]
    p2, d2 = soft_row(
        [score(0, 2), score(1, 1), diag[0] * scale + offset[0]], [held[4], held[5], diag[3]]
    )
    p3, d3 = soft_row(
        [score(2, 3), score(3, 2), diag[1] * scale + offset[1], diag[2] * scale + offset[0]],
        [held[6], held[7], diag[4], diag[5]],
    )
    lines = bias_lines([[d2[2], d3[3]], [d2[1], d3[2]], [d2[0], d3[1]], [d3[0]]])
    if chip == 1:
        items = [d2[2], d3[2], d3[3], d2[0], d2[1], d3[0], d3[1], p2[2], p3[2], p3[3]]
    else:
        (p0, d0), (p1, d1) = early_rows(unpack(small_own, heads), scale, offset)
        items = [d0[0], d1[0], d1[1], d2[0], d2[1], d3[0], d3[1]]
        items += [p0[0], p1[0], p1[1], p2[0], p2[1], p3[0], p3[1]]
    return [item.astype(jnp.bfloat16) for item in items], lines


def gradient_tile(heads, scale, chip, a, b, items, out_a, out_b):
    width = 2 * LANES
    lines = -(-heads // TILE) * TILE
    line = lax.broadcasted_iota(jnp.int32, (lines, width), 0)
    head = lax.broadcasted_iota(jnp.int32, (lines, width), 1) // LANES
    zeros = jnp.zeros((LANES - lines, width), jnp.bfloat16)
    spread = jnp.concatenate(items, axis=0)

    for pair in range(heads // 2):
        at = slice(pair * width, (pair + 1) * width)
        pick = jnp.where(line == 2 * pair + head, 1.0, 0.0).astype(jnp.bfloat16)
        flat = jnp.dot(
            spread, jnp.concatenate([pick, zeros], axis=0), preferred_element_type=jnp.float32
        )
        w = [flat[j * TILE : (j + 1) * TILE, :] for j in range(len(items))]

        def put(ref, value):
            ref[at] = value.astype(jnp.bfloat16)

        def wide(*refs):
            return [ref[at].astype(jnp.float32) for ref in refs]

        if chip == 0:
            ka, kb = wide(a[1], b[1])
            put(out_a[0], w[0] * ka * scale)
            put(out_b[0], (w[1] * ka + w[2] * kb) * scale)
            for to, x, g, rate in ((1, 0, 0, scale), (2, 3, 7, 1.0)):
                xa, xb, x2, x3 = wide(a[x], b[x], a[3 + to], b[3 + to])
                for_a = w[g] * xa + w[g + 1] * xb + w[g + 3] * x2 + w[g + 5] * x3
                for_b = w[g + 2] * xb + w[g + 4] * x2 + w[g + 6] * x3
                put(out_a[to], for_a * rate)
                put(out_b[to], for_b * rate)
        else:
            k2, k3, k0, k1 = wide(a[1], b[1], a[4], b[4])
            put(out_a[0], (w[0] * k2 + w[3] * k0 + w[4] * k1) * scale)
            put(out_b[0], (w[1] * k2 + w[2] * k3 + w[5] * k0 + w[6] * k1) * scale)
            q2, q3, o2, o3 = wide(a[0], b[0], a[3], b[3])
            put(out_a[1], (w[0] * q2 + w[1] * q3) * scale)
            put(out_b[1], w[2] * q3 * scale)
            put(out_a[2], w[7] * o2 + w[8] * o3)
            put(out_b[2], w[9] * o3)


def planes(ref):
    return tuple(ref.at[j] for j in range(ref.shape[0]))


def frames_of(mine, near, far):
    *same, other = far
    return (
        shifted(planes(mine) + pair_of(same), 0),
        shifted(planes(near) + planes(other), 0),
    )


def pair_of(same):
    return tuple(same) if len(same) == 2 else planes(same[0])


def far_small(far, rows, width, heads, chunk):
    at = slice(width + chunk * LANES, width + (chunk + 1) * LANES)
    return unpacked_small(*(ref[rows, at] for ref in pair_of(far[:-1])), heads)


def score_kernel(heads, scale, known, table, small, bias, mine, near, *refs):
    far, (out_items, out_shares, out_small), lines_ref = refs[:3], refs[3:6], refs[6]
    size, width = mine.shape[1:]
    lines_ref[...] = bias[...]
    own, neighbour = frames_of(mine, near, far)

    def work(chip, a, b):
        def tile(row):
            rows = tile_at(row)
            items, lines = score_tile(
                heads, scale, chip, tiles_of(a, row), tiles_of(b, row), table,
                small[rows, :], far_small(far, rows, width, heads, 0),
                unpack(known[rows, :], heads, 4), int(a is own),
            )
            out_small[rows, :] = far_small(far, rows, width, heads, 1)
            for j, item in enumerate(items):
                out_items[j, rows, :] = item
            lines_ref[...] += lines

        over_tiles(size, tile)

    with_frames(own, neighbour, work)
    for j in range(out_shares.shape[0]):
        out_shares[j] = lines_ref[: out_shares.shape[1], :]


def output_copies(which, piece, outs, chunk, sems, at, offset=0):
    half = outs[0].shape[0] // 2
    start = which * half + chunk_start(chunk, half // CHUNKS) + offset
    rows = pl.ds(pl.multiple_of(start, TILE), piece[0].shape[0])
    return [
        pltpu.make_async_copy(part, out.at[rows], sems.at[at + j])
        for j, (part, out) in enumerate(zip(piece, outs))
    ]


def gradient_kernel(heads, scale, items_ref, mine, near, *refs):
    far, out_others, outs, kept, given, sems = refs[:3], refs[3:5], refs[5:8], *refs[8:]
    own, neighbour = frames_of(mine, near, far)
    own_out, other_out = shifted(planes(kept), 0), shifted(planes(given), 0)

    def work(chip, a, b):
        out_a, out_b = (own_out, other_out) if a is own else (other_out, own_out)

        def tile(row):
            items = [items_ref[j, tile_at(row), :] for j in range(LATE if chip else EARLY)]
            gradient_tile(
                heads, scale, chip, tiles_of(a, row), tiles_of(b, row), items,
                tiles_of(out_a, row), tiles_of(out_b, row),
            )

        over_tiles(mine.shape[1], tile)

    with_frames(own, neighbour, work)
    copies = output_copies(my_place()[0], planes(kept), outs, 0, sems, 0)
    for copy in copies:
        copy.start()
    start = 0
    for out in out_others:
        for row in range(0, out.shape[1], TILE):
            for j in range(3):
                out[j, row : row + TILE, :] = given[j, start + row : start + row + TILE, :]
        start += out.shape[1]
    for copy in copies:
        copy.wait()


def whole_kernel(heads, scale, known, table, small, small_far, mine, near, *refs):
    far, out_own, out_others = refs[:2], refs[2], refs[3:6]
    own, neighbour = frames_of(mine, near, far)
    own_out, other_out = shifted(planes(out_own), 0), shifted(out_others, 0)

    def work(chip, a, b):
        out_a, out_b = (own_out, other_out) if a is own else (other_out, own_out)

        def tile(row):
            at, bt, rows = tiles_of(a, row), tiles_of(b, row), tile_at(row)
            items, _ = score_tile(
                heads, scale, chip, at, bt, table, small[rows, :], small_far[rows, :],
                unpack(known[rows, :], heads, 4), int(a is not own),
            )
            gradient_tile(
                heads, scale, chip, at, bt, items, tiles_of(out_a, row), tiles_of(out_b, row)
            )

        over_tiles(mine.shape[1], tile)

    with_frames(own, neighbour, work)


def output_kernel(*refs):
    first_backs, kept, back, shares = refs[:2], planes(refs[2]), refs[3:6], refs[6]
    outs, out_bias, total, sems = refs[10:13], *refs[13:]
    core = my_place()[0]
    copies = output_copies(core, kept, outs, 1, sems, 0)
    copies += output_copies(1 - core, back, outs, 1, sems, 3)
    offset = 0
    for j, ref in enumerate(first_backs):
        copies += output_copies(1 - core, planes(ref), outs, 0, sems, 6 + 3 * j, offset)
        offset += ref.shape[1]
    for copy in copies:
        copy.start()
    parts = [shares[j] for j in range(shares.shape[0])]
    while len(parts) > 1:
        parts = [a + b for a, b in zip(parts[::2], parts[1::2])]
    total[...] = parts[0][: total.shape[0], : total.shape[1]]
    copies.append(pltpu.make_async_copy(total, out_bias, sems.at[12]))
    copies[-1].start()
    for copy in copies:
        copy.wait()


def by_chips(query_vectors, key_vectors, value_vectors, grad_output, time_bias, sizes):
    heads, frames = time_bias.shape
    clips, _, patches, width = query_vectors.shape
    rows = clips * patches
    half = rows // 2
    size = half // CHUNKS
    scale = 1.0 / math.sqrt(width // heads)
    own = [
        pltpu.with_memory_space_constraint(x.reshape(rows, width), pltpu.HBM)
        for x in (query_vectors, key_vectors, value_vectors, grad_output)
    ]
    vmem_spec = pl.BlockSpec(memory_space=pltpu.VMEM)
    any_spec = pl.BlockSpec(memory_space=pl.ANY)

    def swap(x, bits):
        return lax.ppermute(x, "tm", [(i, i ^ bits) for i in range(4)])

    def shape(*dims, dtype=jnp.bfloat16):
        return jax.ShapeDtypeStruct(dims, dtype)

    def call(kernel, name, out_shape, *args, scratch=(), hbm=(), hbm_out=(), aliases={}):
        return pl.pallas_call(
            kernel,
            in_specs=[any_spec if j in hbm else vmem_spec for j in range(len(args))],
            out_specs=[any_spec if j in hbm_out else vmem_spec for j in range(len(out_shape))],
            out_shape=out_shape,
            scratch_shapes=scratch,
            input_output_aliases=aliases,
            compiler_params=pltpu.CompilerParams(vmem_limit_bytes=16 * 2**20),
            cost_estimate=LITTLE,
            name=name,
        )(*args)

    wide = jnp.float32
    lines = shape(8, LANES, dtype=wide)
    chunk_shape, far_shape = shape(4, size, width), shape(2, size, width)
    copies = [pltpu.SemaphoreType.DMA((4 * CHUNKS,))]
    table = jnp.pad(time_bias.T, ((0, 8 - frames), (0, LANES - heads)))

    *theirs, other = call(
        fetch_theirs_kernel, "fetch_theirs", [chunk_shape] * CHUNKS + [far_shape], *own,
        scratch=copies, hbm=range(4),
    )
    nears = [swap(x, 1) for x in theirs]
    others = [swap(other, 3)]
    mines = call(
        fetch_mine_kernel, "fetch_mine", [chunk_shape] * CHUNKS, *own, other,
        scratch=copies, hbm=range(5),
    )

    *smalls, bias, other, same_first, same_second, same = call(
        functools.partial(local_kernel, heads, scale),
        "local_scores",
        [shape(size, LANES, dtype=wide)] * CHUNKS
        + [lines, far_shape]
        + [shape(size, width + CHUNKS * LANES)] * 2
        + [far_shape],
        table, *mines, *nears, theirs[0],
    )
    sames = [[swap(same_first, 2), swap(same_second, 2)], [swap(same, 2)]]
    others.append(swap(other, 3))

    whole = pltpu.HBM((rows, width), jnp.bfloat16)
    stack, piece = shape(3, size, width), shape(size, width)
    output_sems = pltpu.SemaphoreType.DMA((13,))
    first = (mines[0], nears[0], *sames[0], others[0])
    (known,) = call(
        functools.partial(piece_kernel, heads, False),
        "first_dots",
        [shape(size, LANES, dtype=wide)],
        mines[0], nears[0], others[0],
    )
    items, shares, small_far = call(
        functools.partial(score_kernel, heads, scale),
        "scores",
        [
            shape(EARLY, size, LANES),
            shape(math.prod(count for _, count in sizes), 8, LANES, dtype=wide),
            shape(size, LANES, dtype=wide),
        ],
        known, table, smalls[0], bias, *first,
        scratch=[pltpu.VMEM((8, LANES), wide)],
    )
    shares = lax.all_to_all(shares, tuple(axis for axis, _ in sizes), 0, 0, tiled=True)
    *back, grad_queries, grad_keys, grad_values = call(
        functools.partial(gradient_kernel, heads, scale),
        "gradients",
        [shape(3, size // 2, width)] * 2 + [whole] * 3,
        items, *first,
        scratch=[pltpu.VMEM((3, size, width), jnp.bfloat16)] * 2 + [output_sems],
        hbm_out=range(2, 5),
    )
    grads = (grad_queries, grad_keys, grad_values)
    first_backs = [swap(x, 1) for x in back]

    (known_last,) = call(
        functools.partial(piece_kernel, heads, True),
        "last_dots",
        [shape(size, LANES, dtype=wide)],
        mines[1], nears[1], *sames[1],
    )
    kept, *back = call(
        functools.partial(whole_kernel, heads, scale),
        "scores_and_gradients",
        [stack] + [piece] * 3,
        known_last, table, smalls[1], small_far, mines[1], nears[1], *sames[1], others[1],
    )
    back = [swap(x, 1) for x in back]
    grads = [pltpu.with_memory_space_constraint(x, pltpu.HBM) for x in grads]
    *grads, bias = call(
        output_kernel,
        "outputs",
        [whole] * 3 + [shape(frames, heads, dtype=wide)],
        *first_backs, kept, *back, shares, *grads,
        scratch=[pltpu.VMEM((frames, heads), wide), output_sems],
        hbm=range(7, 10),
        hbm_out=range(4),
        aliases={7 + j: j for j in range(3)},
    )
    return (*[x.reshape(query_vectors.shape) for x in grads], bias.T)


def solution(mesh):
    sizes = tuple((axis, mesh.shape[axis]) for axis in ("tm", "patch"))

    def per_device(*args):
        heads, frames = args[4].shape
        fits = (
            mesh.shape["tm"] == 4
            and frames == 4
            and args[0].shape[1] == 1
            and heads * LANES == args[0].shape[3]
            and 3 * heads <= 2 * (LANES - 6 * heads)
            and heads % 2 == 0
            and args[0].shape[0] * args[0].shape[2] % (2 * TILE * CHUNKS) == 0
            and mesh.shape["patch"].bit_count() == 1
        )
        return (by_chips if fits else by_heads)(*args, sizes)

    vectors = P(None, "tm", "patch", None)
    return jax.shard_map(
        per_device,
        mesh=mesh,
        in_specs=(vectors,) * 4 + (P(),),
        out_specs=(vectors,) * 3 + (P(),),
        check_vma=False,
    )
```

```python
import functools
import math

import jax
import jax.numpy as jnp
from jax import lax
from jax.experimental import pallas as pl
from jax.experimental.pallas import tpu as pltpu
from jax.sharding import PartitionSpec as P

LANES = 128
TILE = 16
LITTLE = pl.CostEstimate(flops=1, bytes_accessed=1, transcendentals=0)
CHUNKS = 2


def score_table(bias_rows, frames):
    steps = jnp.arange(frames, dtype=jnp.int32)
    offsets = steps[:, None] - steps[None, :]
    onehot = (offsets[:, :, None] == steps[None, None, :]).astype(jnp.float32)
    table = jnp.einsum("hd,tud->htu", bias_rows, onehot, precision=lax.Precision.HIGHEST)
    return (table, offsets >= 0, onehot)


def attend_back(query_heads, key_heads, value_heads, grad_heads, bias_rows):
    frames = query_heads.shape[1]
    score_scale = 1.0 / math.sqrt(query_heads.shape[4])
    table, causal, onehot = score_table(bias_rows, frames)
    wide = jnp.float32
    scores = (
        jnp.einsum("atxhd,auxhd->axhtu", query_heads, key_heads, preferred_element_type=wide)
        * score_scale
        + table[None, None]
    )
    scores = jnp.where(causal, scores, -jnp.inf)
    row_max = jnp.max(scores, axis=-1, keepdims=True)
    expon = jnp.exp(scores - row_max)
    weights = expon / jnp.sum(expon, axis=-1, keepdims=True)
    weights_low = weights.astype(jnp.bfloat16)
    attended = jnp.einsum(
        "axhtu,auxhd->atxhd", weights_low, value_heads, preferred_element_type=wide
    )
    rowdot = jnp.einsum("atxhd,atxhd->axht", grad_heads, attended, preferred_element_type=wide)
    grad_weights = jnp.einsum(
        "atxhd,auxhd->axhtu", grad_heads, value_heads, preferred_element_type=wide
    )
    grad_scores = weights * (grad_weights - rowdot[..., None])
    bias_terms = jnp.einsum("axhtu,tud->axhd", grad_scores, onehot, precision=lax.Precision.HIGHEST)
    grad_low = grad_scores.astype(jnp.bfloat16)
    grad_query = (
        jnp.einsum("axhtu,auxhd->atxhd", grad_low, key_heads, preferred_element_type=wide)
        * score_scale
    ).astype(jnp.bfloat16)
    grad_key = (
        jnp.einsum("axhtu,atxhd->auxhd", grad_low, query_heads, preferred_element_type=wide)
        * score_scale
    ).astype(jnp.bfloat16)
    grad_value = jnp.einsum(
        "axhtu,atxhd->auxhd", weights_low, grad_heads, preferred_element_type=wide
    ).astype(jnp.bfloat16)
    return (grad_query, grad_key, grad_value, bias_terms)


def sum_everywhere(value, sizes):
    for axis, size in sizes:
        if size & (size - 1):
            value = lax.psum(value, axis)
            continue
        step = 1
        while step < size:
            other = lax.ppermute(value, axis, [(i, i ^ step) for i in range(size)])
            value = value + other
            step *= 2
    return value


def by_heads(query_vectors, key_vectors, value_vectors, grad_output, time_bias, sizes):
    head_count = time_bias.shape[0]
    frames = time_bias.shape[1]
    head_dim = query_vectors.shape[3] // head_count
    split_shape = query_vectors.shape[:3] + (head_count, head_dim)
    local_heads = head_count // lax.axis_size("tm")
    first_head = lax.axis_index("tm") * local_heads
    bias_rows = lax.dynamic_slice_in_dim(time_bias, first_head, local_heads, 0)
    spread = [
        lax.all_to_all(item.reshape(split_shape), "tm", split_axis=3, concat_axis=1, tiled=True)
        for item in (query_vectors, key_vectors, value_vectors, grad_output)
    ]
    *grads, bias_terms = attend_back(*spread, bias_rows)
    grads = [
        lax.all_to_all(item, "tm", split_axis=1, concat_axis=3, tiled=True).reshape(
            query_vectors.shape
        )
        for item in grads
    ]
    partial = lax.dynamic_update_slice_in_dim(
        jnp.zeros((head_count, frames), jnp.float32),
        jnp.sum(bias_terms, axis=(0, 1)),
        first_head,
        0,
    )
    return (*grads, sum_everywhere(partial, sizes))


def pair_dots(queries, keys, grads, values, pairs, heads):
    place = lax.broadcasted_iota(jnp.int32, (TILE, LANES), 1)
    held = [jnp.zeros((TILE, LANES), jnp.float32)] * (2 * len(pairs))
    for head in range(heads):
        at = slice(head * LANES, (head + 1) * LANES)
        here = place == head
        load = lambda refs, used: {j: refs[j][at].astype(jnp.float32) for j in used}
        late, early = {t for t, _ in pairs}, {u for _, u in pairs}
        q, k = load(queries, sorted(late)), load(keys, sorted(early))
        o, v = load(grads, sorted(late)), load(values, sorted(early))
        for j, (t, u) in enumerate(pairs):
            score = jnp.sum(q[t] * k[u], axis=1, keepdims=True)
            held[j] = jnp.where(here, score, held[j])
            gain = jnp.sum(o[t] * v[u], axis=1, keepdims=True)
            held[len(pairs) + j] = jnp.where(here, gain, held[len(pairs) + j])
    return held


def over_tiles(rows, body):
    pl.loop(0, rows // TILE)(lambda i: body(i * TILE))


def tile_at(start):
    return pl.ds(pl.multiple_of(start, TILE), TILE)


class Shifted:
    def __init__(self, ref, start):
        self.ref, self.start = ref, start

    def at_rows(self, row):
        return View(self.ref, tile_at(self.start + row))


class View:
    def __init__(self, ref, rows):
        self.ref, self.rows = ref, rows

    def __getitem__(self, lanes):
        return self.ref[self.rows, lanes]

    def __setitem__(self, lanes, value):
        self.ref[self.rows, lanes] = value


def tiles_of(refs, row):
    return tuple(ref if ref is None else ref.at_rows(row) for ref in refs)


def shifted(refs, start):
    return tuple(ref if ref is None else Shifted(ref, start) for ref in refs)


def soft_row(scores, gains):
    top = functools.reduce(jnp.maximum, scores)
    expon = [jnp.exp(item - top) for item in scores]
    total = functools.reduce(jnp.add, expon)
    weights = [item / total for item in expon]
    low = [item.astype(jnp.bfloat16) for item in weights]
    rowdot = functools.reduce(
        jnp.add, [a.astype(jnp.float32) * g for a, g in zip(low, gains)]
    )
    grads = [w * (g - rowdot) for w, g in zip(weights, gains)]
    return low, grads


LOCAL = ((0, 0), (1, 0), (1, 1))
CROSS = ((0, 0), (0, 1), (1, 0), (1, 1))


def unpack(packed, heads, count=6):
    return [
        packed if j == 0 else pltpu.roll(packed, LANES - heads * j, axis=1) for j in range(count)
    ]


def bias_lines(terms):
    lines = []
    for items in terms:
        lines.append(
            jnp.sum(functools.reduce(jnp.add, items), axis=0, keepdims=True)
            if items
            else jnp.zeros((1, LANES), jnp.float32)
        )
    return jnp.concatenate(lines + [jnp.zeros((4, LANES), jnp.float32)], axis=0)


def early_rows(diag, scale, offset):
    score = lambda j, d: diag[j] * scale + offset[d]
    row0 = soft_row([score(0, 0)], [diag[3]])
    row1 = soft_row([score(1, 1), score(2, 0)], [diag[4], diag[5]])
    return row0, row1


def my_place():
    me = lax.axis_index("tm")
    return lax.rem(me, 2), lax.div(me, 2)


def with_frames(own, other, work):
    core, chip = my_place()
    for at_chip in range(2):
        pl.when((chip == at_chip) & (core == 0))(functools.partial(work, at_chip, own, other))
        pl.when((chip == at_chip) & (core == 1))(functools.partial(work, at_chip, other, own))


def chunk_start(chunk, size):
    return jnp.where(my_place()[1] == 0, chunk, CHUNKS - 1 - chunk) * size


def copy_chunks(sources, core, outs, sems):
    size = outs[0].shape[1]
    copies = []
    for c, out in enumerate(outs):
        start = pl.multiple_of(core * CHUNKS * size + chunk_start(c, size), TILE)
        for j, ref in enumerate(sources):
            copies.append(
                pltpu.make_async_copy(
                    ref.at[pl.ds(start, size)], out.at[j], sems.at[len(copies)]
                )
            )
    for copy in copies:
        copy.start()
    for copy in copies:
        copy.wait()


def take_far(refs, outs):
    chip = my_place()[1]

    def take(places):
        for out, place in zip(outs, places):
            for row in range(0, out.shape[0], TILE):
                rows = slice(row, row + TILE)
                out[rows, : refs[place].shape[1]] = refs[place][rows, :]

    pl.when(chip == 0)(lambda: take((1, 2)))
    pl.when(chip == 1)(lambda: take((0, 3)))


def fetch_theirs_kernel(q, k, v, o, *refs):
    nears, other, sems = refs[:CHUNKS], refs[CHUNKS], refs[CHUNKS + 1]
    copy_chunks((q, k, v, o), 1 - my_place()[0], nears, sems)
    take_far(planes(nears[CHUNKS - 1]), planes(other))


def fetch_mine_kernel(q, k, v, o, after, *refs):
    copy_chunks((q, k, v, o), my_place()[0], refs[:-1], refs[-1])


def packed_small(value, heads):
    used = 6 * heads
    place = lax.broadcasted_iota(jnp.int32, value.shape, 1)
    high = value.astype(jnp.bfloat16).astype(jnp.float32)
    middle = (value - high).astype(jnp.bfloat16).astype(jnp.float32)
    rest = (value - high) - middle
    first = jnp.where(place < used, high, pltpu.roll(rest, used, axis=1))
    second = jnp.where(place < used, middle, pltpu.roll(rest, 2 * used - LANES, axis=1))
    return first.astype(jnp.bfloat16), second.astype(jnp.bfloat16)


def unpacked_small(first, second, heads):
    used = 6 * heads
    first, second = first.astype(jnp.float32), second.astype(jnp.float32)
    place = lax.broadcasted_iota(jnp.int32, first.shape, 1)
    rest = jnp.where(
        place < LANES - used,
        pltpu.roll(first, LANES - used, axis=1),
        pltpu.roll(second, 2 * (LANES - used), axis=1),
    )
    return first + second + jnp.where(place < 3 * heads, rest, 0.0)


def local_kernel(heads, scale, table, *refs):
    mines, nears, theirs, refs = refs[:2], refs[2:4], refs[4], refs[5:]
    smalls, out_bias, other, sames = refs[:2], refs[2], refs[3], (refs[4:6], planes(refs[6]))
    core, chip = my_place()
    size, width = mines[0].shape[1:]
    offset = [table[d : d + 1, :] for d in range(4)]
    out_bias[...] = jnp.zeros_like(out_bias)

    def run(a, b, small):
        def tile(row):
            at, bt = tiles_of(a, row), tiles_of(b, row)
            held = pair_dots(
                (at[0], bt[0]), (at[1], bt[1]), (at[3], bt[3]), (at[2], bt[2]), LOCAL, heads
            )
            total = held[0]
            for j in range(1, 6):
                total = total + pltpu.roll(held[j], heads * j, axis=1)
            small[tile_at(row), :] = total
            (_, d0), (_, d1) = early_rows(held, scale, offset)
            lines = bias_lines([[d0[0], d1[1]], [d1[0]], [], []])
            out_bias[...] += jnp.where(chip == 0, lines, jnp.zeros_like(lines))

        over_tiles(size, tile)

    for mine, near, small in zip(mines, nears, smalls):
        own, neighbour = shifted(planes(mine), 0), shifted(planes(near), 0)
        pl.when(core == 0)(functools.partial(run, own, neighbour, small))
        pl.when(core == 1)(functools.partial(run, neighbour, own, small))

    take_far(planes(theirs), planes(other))
    for c, out in enumerate(sames):
        take_far(planes(mines[1 - c]), out)
        for row in range(0, size, TILE):
            rows = slice(row, row + TILE)
            parts = packed_small(smalls[1 - c][rows, :], heads)
            for ref, part in zip(sames[0], parts):
                ref[rows, width + c * LANES : width + (c + 1) * LANES] = part


EARLY, LATE = 14, 10


def cross_sides(chip, a, b):
    if chip == 0:
        return ((a[4], a[5]), (b[4], b[5])), ((a[1], a[2]), (b[1], b[2]))
    return ((a[0], a[3]), (b[0], b[3])), ((a[4], a[5]), (b[4], b[5]))


def far_pairs(chip, parity):
    return [pair for pair in CROSS if pair[chip] == parity]


def cross_dots(queries, keys, pairs, heads):
    return pair_dots(
        [x[0] for x in queries], [x[0] for x in keys],
        [x[1] for x in queries], [x[1] for x in keys], pairs, heads,
    )


def piece_kernel(heads, same, mine, near, *refs):
    far, out = refs[:-1], refs[-1]
    piece = far if len(far) == 2 else planes(far[0])
    own, other = planes(mine), planes(near)
    if same:
        own, other = own + piece, other + (None, None)
    else:
        own, other = own + (None, None), other + piece
    own, other = shifted(own, 0), shifted(other, 0)

    def work(chip, a, b):
        parity = int((a is own) != same)

        def tile(row):
            queries, keys = cross_sides(chip, tiles_of(a, row), tiles_of(b, row))
            held = cross_dots(queries, keys, far_pairs(chip, parity), heads)
            total = held[0]
            for j in range(1, 4):
                total = total + pltpu.roll(held[j], heads * j, axis=1)
            out[tile_at(row), :] = total

        over_tiles(out.shape[0], tile)

    with_frames(own, other, work)


def score_tile(heads, scale, chip, a, b, table, small_own, small_far, known, parity):
    offset = [table[d : d + 1, :] for d in range(4)]
    queries, keys = cross_sides(chip, a, b)
    held = [None] * 8
    for pairs, values in (
        (far_pairs(chip, parity), known),
        (far_pairs(chip, 1 - parity), None),
    ):
        if values is None:
            values = cross_dots(queries, keys, pairs, heads)
        for j, pair in enumerate(pairs):
            held[CROSS.index(pair)] = values[j]
            held[4 + CROSS.index(pair)] = values[2 + j]
    diag = unpack(small_far if chip == 0 else small_own, heads)
    score = lambda j, d: held[j] * scale + offset[d]
    p2, d2 = soft_row(
        [score(0, 2), score(1, 1), diag[0] * scale + offset[0]], [held[4], held[5], diag[3]]
    )
    p3, d3 = soft_row(
        [score(2, 3), score(3, 2), diag[1] * scale + offset[1], diag[2] * scale + offset[0]],
        [held[6], held[7], diag[4], diag[5]],
    )
    lines = bias_lines([[d2[2], d3[3]], [d2[1], d3[2]], [d2[0], d3[1]], [d3[0]]])
    if chip == 1:
        items = [d2[2], d3[2], d3[3], d2[0], d2[1], d3[0], d3[1], p2[2], p3[2], p3[3]]
    else:
        (p0, d0), (p1, d1) = early_rows(unpack(small_own, heads), scale, offset)
        items = [d0[0], d1[0], d1[1], d2[0], d2[1], d3[0], d3[1]]
        items += [p0[0], p1[0], p1[1], p2[0], p2[1], p3[0], p3[1]]
    return [item.astype(jnp.bfloat16) for item in items], lines


def gradient_tile(heads, scale, chip, a, b, items, out_a, out_b):
    width = 2 * LANES
    lines = -(-heads // TILE) * TILE
    line = lax.broadcasted_iota(jnp.int32, (lines, width), 0)
    head = lax.broadcasted_iota(jnp.int32, (lines, width), 1) // LANES
    zeros = jnp.zeros((LANES - lines, width), jnp.bfloat16)
    spread = jnp.concatenate(items, axis=0)

    for pair in range(heads // 2):
        at = slice(pair * width, (pair + 1) * width)
        pick = jnp.where(line == 2 * pair + head, 1.0, 0.0).astype(jnp.bfloat16)
        flat = jnp.dot(
            spread, jnp.concatenate([pick, zeros], axis=0), preferred_element_type=jnp.float32
        )
        w = [flat[j * TILE : (j + 1) * TILE, :] for j in range(len(items))]

        def put(ref, value):
            ref[at] = value.astype(jnp.bfloat16)

        def wide(*refs):
            return [ref[at].astype(jnp.float32) for ref in refs]

        if chip == 0:
            ka, kb = wide(a[1], b[1])
            put(out_a[0], w[0] * ka * scale)
            put(out_b[0], (w[1] * ka + w[2] * kb) * scale)
            for to, x, g, rate in ((1, 0, 0, scale), (2, 3, 7, 1.0)):
                xa, xb, x2, x3 = wide(a[x], b[x], a[3 + to], b[3 + to])
                for_a = w[g] * xa + w[g + 1] * xb + w[g + 3] * x2 + w[g + 5] * x3
                for_b = w[g + 2] * xb + w[g + 4] * x2 + w[g + 6] * x3
                put(out_a[to], for_a * rate)
                put(out_b[to], for_b * rate)
        else:
            k2, k3, k0, k1 = wide(a[1], b[1], a[4], b[4])
            put(out_a[0], (w[0] * k2 + w[3] * k0 + w[4] * k1) * scale)
            put(out_b[0], (w[1] * k2 + w[2] * k3 + w[5] * k0 + w[6] * k1) * scale)
            q2, q3, o2, o3 = wide(a[0], b[0], a[3], b[3])
            put(out_a[1], (w[0] * q2 + w[1] * q3) * scale)
            put(out_b[1], w[2] * q3 * scale)
            put(out_a[2], w[7] * o2 + w[8] * o3)
            put(out_b[2], w[9] * o3)


def planes(ref):
    return tuple(ref.at[j] for j in range(ref.shape[0]))


def frames_of(mine, near, far):
    *same, other = far
    return (
        shifted(planes(mine) + pair_of(same), 0),
        shifted(planes(near) + planes(other), 0),
    )


def pair_of(same):
    return tuple(same) if len(same) == 2 else planes(same[0])


def far_small(far, rows, width, heads, chunk):
    at = slice(width + chunk * LANES, width + (chunk + 1) * LANES)
    return unpacked_small(*(ref[rows, at] for ref in pair_of(far[:-1])), heads)


def score_kernel(heads, scale, known, table, small, bias, mine, near, *refs):
    far, (out_items, out_shares, out_small), lines_ref = refs[:3], refs[3:6], refs[6]
    size, width = mine.shape[1:]
    lines_ref[...] = bias[...]
    own, neighbour = frames_of(mine, near, far)

    def work(chip, a, b):
        def tile(row):
            rows = tile_at(row)
            items, lines = score_tile(
                heads, scale, chip, tiles_of(a, row), tiles_of(b, row), table,
                small[rows, :], far_small(far, rows, width, heads, 0),
                unpack(known[rows, :], heads, 4), int(a is own),
            )
            out_small[rows, :] = far_small(far, rows, width, heads, 1)
            for j, item in enumerate(items):
                out_items[j, rows, :] = item
            lines_ref[...] += lines

        over_tiles(size, tile)

    with_frames(own, neighbour, work)
    for j in range(out_shares.shape[0]):
        out_shares[j] = lines_ref[: out_shares.shape[1], :]


def output_copies(which, piece, outs, chunk, sems, at, offset=0):
    half = outs[0].shape[0] // 2
    start = which * half + chunk_start(chunk, half // CHUNKS) + offset
    rows = pl.ds(pl.multiple_of(start, TILE), piece[0].shape[0])
    return [
        pltpu.make_async_copy(part, out.at[rows], sems.at[at + j])
        for j, (part, out) in enumerate(zip(piece, outs))
    ]


def gradient_kernel(heads, scale, items_ref, mine, near, *refs):
    far, out_others, outs, kept, given, sems = refs[:3], refs[3:5], refs[5:8], *refs[8:]
    own, neighbour = frames_of(mine, near, far)
    own_out, other_out = shifted(planes(kept), 0), shifted(planes(given), 0)

    def work(chip, a, b):
        out_a, out_b = (own_out, other_out) if a is own else (other_out, own_out)

        def tile(row):
            items = [items_ref[j, tile_at(row), :] for j in range(LATE if chip else EARLY)]
            gradient_tile(
                heads, scale, chip, tiles_of(a, row), tiles_of(b, row), items,
                tiles_of(out_a, row), tiles_of(out_b, row),
            )

        over_tiles(mine.shape[1], tile)

    with_frames(own, neighbour, work)
    copies = output_copies(my_place()[0], planes(kept), outs, 0, sems, 0)
    for copy in copies:
        copy.start()
    start = 0
    for out in out_others:
        for row in range(0, out.shape[1], TILE):
            for j in range(3):
                out[j, row : row + TILE, :] = given[j, start + row : start + row + TILE, :]
        start += out.shape[1]
    for copy in copies:
        copy.wait()


def whole_kernel(heads, scale, known, table, small, small_far, mine, near, *refs):
    far, out_own, out_others = refs[:2], refs[2], refs[3:6]
    own, neighbour = frames_of(mine, near, far)
    own_out, other_out = shifted(planes(out_own), 0), shifted(out_others, 0)

    def work(chip, a, b):
        out_a, out_b = (own_out, other_out) if a is own else (other_out, own_out)

        def tile(row):
            at, bt, rows = tiles_of(a, row), tiles_of(b, row), tile_at(row)
            items, _ = score_tile(
                heads, scale, chip, at, bt, table, small[rows, :], small_far[rows, :],
                unpack(known[rows, :], heads, 4), int(a is not own),
            )
            gradient_tile(
                heads, scale, chip, at, bt, items, tiles_of(out_a, row), tiles_of(out_b, row)
            )

        over_tiles(mine.shape[1], tile)

    with_frames(own, neighbour, work)


def early_output_kernel(*refs):
    first_backs, kept, outs, sems = refs[:2], planes(refs[2]), refs[6:9], refs[9]
    core = my_place()[0]
    copies = output_copies(core, kept, outs, 1, sems, 0)
    offset = 0
    for j, ref in enumerate(first_backs):
        copies += output_copies(1 - core, planes(ref), outs, 0, sems, 3 + 3 * j, offset)
        offset += ref.shape[1]
    for copy in copies:
        copy.start()
    for copy in copies:
        copy.wait()


def output_kernel(*refs):
    back, shares, outs, out_bias, total, sems = refs[:3], refs[3], refs[7:10], *refs[10:]
    copies = output_copies(1 - my_place()[0], back, outs, 1, sems, 0)
    for copy in copies:
        copy.start()
    parts = [shares[j] for j in range(shares.shape[0])]
    while len(parts) > 1:
        parts = [a + b for a, b in zip(parts[::2], parts[1::2])]
    total[...] = parts[0][: total.shape[0], : total.shape[1]]
    copies.append(pltpu.make_async_copy(total, out_bias, sems.at[len(copies)]))
    copies[-1].start()
    for copy in copies:
        copy.wait()


def by_chips(query_vectors, key_vectors, value_vectors, grad_output, time_bias, sizes):
    heads, frames = time_bias.shape
    clips, _, patches, width = query_vectors.shape
    rows = clips * patches
    half = rows // 2
    size = half // CHUNKS
    scale = 1.0 / math.sqrt(width // heads)
    own = [
        pltpu.with_memory_space_constraint(x.reshape(rows, width), pltpu.HBM)
        for x in (query_vectors, key_vectors, value_vectors, grad_output)
    ]
    vmem_spec = pl.BlockSpec(memory_space=pltpu.VMEM)
    any_spec = pl.BlockSpec(memory_space=pl.ANY)

    def swap(x, bits):
        return lax.ppermute(x, "tm", [(i, i ^ bits) for i in range(4)])

    def shape(*dims, dtype=jnp.bfloat16):
        return jax.ShapeDtypeStruct(dims, dtype)

    def call(kernel, name, out_shape, *args, scratch=(), hbm=(), hbm_out=(), aliases={}):
        return pl.pallas_call(
            kernel,
            in_specs=[any_spec if j in hbm else vmem_spec for j in range(len(args))],
            out_specs=[any_spec if j in hbm_out else vmem_spec for j in range(len(out_shape))],
            out_shape=out_shape,
            scratch_shapes=scratch,
            input_output_aliases=aliases,
            compiler_params=pltpu.CompilerParams(vmem_limit_bytes=16 * 2**20),
            cost_estimate=LITTLE,
            name=name,
        )(*args)

    wide = jnp.float32
    lines = shape(8, LANES, dtype=wide)
    chunk_shape, far_shape = shape(4, size, width), shape(2, size, width)
    copies = [pltpu.SemaphoreType.DMA((4 * CHUNKS,))]
    table = jnp.pad(time_bias.T, ((0, 8 - frames), (0, LANES - heads)))

    *theirs, other = call(
        fetch_theirs_kernel, "fetch_theirs", [chunk_shape] * CHUNKS + [far_shape], *own,
        scratch=copies, hbm=range(4),
    )
    nears = [swap(x, 1) for x in theirs]
    others = [swap(other, 3)]
    mines = call(
        fetch_mine_kernel, "fetch_mine", [chunk_shape] * CHUNKS, *own, other,
        scratch=copies, hbm=range(5),
    )

    *smalls, bias, other, same_first, same_second, same = call(
        functools.partial(local_kernel, heads, scale),
        "local_scores",
        [shape(size, LANES, dtype=wide)] * CHUNKS
        + [lines, far_shape]
        + [shape(size, width + CHUNKS * LANES)] * 2
        + [far_shape],
        table, *mines, *nears, theirs[0],
    )
    sames = [[swap(same_first, 2), swap(same_second, 2)], [swap(same, 2)]]
    others.append(swap(other, 3))

    whole = pltpu.HBM((rows, width), jnp.bfloat16)
    stack, piece = shape(3, size, width), shape(size, width)
    output_sems = pltpu.SemaphoreType.DMA((13,))
    first = (mines[0], nears[0], *sames[0], others[0])
    (known,) = call(
        functools.partial(piece_kernel, heads, False),
        "first_dots",
        [shape(size, LANES, dtype=wide)],
        mines[0], nears[0], others[0],
    )
    items, shares, small_far = call(
        functools.partial(score_kernel, heads, scale),
        "scores",
        [
            shape(EARLY, size, LANES),
            shape(math.prod(count for _, count in sizes), 8, LANES, dtype=wide),
            shape(size, LANES, dtype=wide),
        ],
        known, table, smalls[0], bias, *first,
        scratch=[pltpu.VMEM((8, LANES), wide)],
    )
    shares = lax.all_to_all(shares, tuple(axis for axis, _ in sizes), 0, 0, tiled=True)
    *back, grad_queries, grad_keys, grad_values = call(
        functools.partial(gradient_kernel, heads, scale),
        "gradients",
        [shape(3, size // 2, width)] * 2 + [whole] * 3,
        items, *first,
        scratch=[pltpu.VMEM((3, size, width), jnp.bfloat16)] * 2 + [output_sems],
        hbm_out=range(2, 5),
    )
    grads = (grad_queries, grad_keys, grad_values)
    first_backs = [swap(x, 1) for x in back]

    (known_last,) = call(
        functools.partial(piece_kernel, heads, True),
        "last_dots",
        [shape(size, LANES, dtype=wide)],
        mines[1], nears[1], *sames[1],
    )
    kept, *back = call(
        functools.partial(whole_kernel, heads, scale),
        "scores_and_gradients",
        [stack] + [piece] * 3,
        known_last, table, smalls[1], small_far, mines[1], nears[1], *sames[1], others[1],
    )
    back = [swap(x, 1) for x in back]
    in_hbm = lambda arrays: [pltpu.with_memory_space_constraint(x, pltpu.HBM) for x in arrays]
    grads = call(
        early_output_kernel,
        "early_outputs",
        [whole] * 3,
        *first_backs, kept, *in_hbm(grads),
        scratch=[output_sems],
        hbm=range(3, 6),
        hbm_out=range(3),
        aliases={3 + j: j for j in range(3)},
    )
    *grads, bias = call(
        output_kernel,
        "outputs",
        [whole] * 3 + [shape(frames, heads, dtype=wide)],
        *back, shares, *in_hbm(grads),
        scratch=[pltpu.VMEM((frames, heads), wide), output_sems],
        hbm=range(4, 7),
        hbm_out=range(4),
        aliases={4 + j: j for j in range(3)},
    )
    return (*[x.reshape(query_vectors.shape) for x in grads], bias.T)


def solution(mesh):
    sizes = tuple((axis, mesh.shape[axis]) for axis in ("tm", "patch"))

    def per_device(*args):
        heads, frames = args[4].shape
        fits = (
            mesh.shape["tm"] == 4
            and frames == 4
            and args[0].shape[1] == 1
            and heads * LANES == args[0].shape[3]
            and 3 * heads <= 2 * (LANES - 6 * heads)
            and heads % 2 == 0
            and args[0].shape[0] * args[0].shape[2] % (2 * TILE * CHUNKS) == 0
            and mesh.shape["patch"].bit_count() == 1
        )
        return (by_chips if fits else by_heads)(*args, sizes)

    vectors = P(None, "tm", "patch", None)
    return jax.shard_map(
        per_device,
        mesh=mesh,
        in_specs=(vectors,) * 4 + (P(),),
        out_specs=(vectors,) * 3 + (P(),),
        check_vma=False,
    )
```

```python
import functools
import math

import jax
import jax.numpy as jnp
from jax import lax
from jax.experimental import pallas as pl
from jax.experimental.pallas import tpu as pltpu
from jax.sharding import PartitionSpec as P

LANES = 128
TILE = 16
LITTLE = pl.CostEstimate(flops=1, bytes_accessed=1, transcendentals=0)
CHUNKS = 2


def score_table(bias_rows, frames):
    steps = jnp.arange(frames, dtype=jnp.int32)
    offsets = steps[:, None] - steps[None, :]
    onehot = (offsets[:, :, None] == steps[None, None, :]).astype(jnp.float32)
    table = jnp.einsum("hd,tud->htu", bias_rows, onehot, precision=lax.Precision.HIGHEST)
    return (table, offsets >= 0, onehot)


def attend_back(query_heads, key_heads, value_heads, grad_heads, bias_rows):
    frames = query_heads.shape[1]
    score_scale = 1.0 / math.sqrt(query_heads.shape[4])
    table, causal, onehot = score_table(bias_rows, frames)
    wide = jnp.float32
    scores = (
        jnp.einsum("atxhd,auxhd->axhtu", query_heads, key_heads, preferred_element_type=wide)
        * score_scale
        + table[None, None]
    )
    scores = jnp.where(causal, scores, -jnp.inf)
    row_max = jnp.max(scores, axis=-1, keepdims=True)
    expon = jnp.exp(scores - row_max)
    weights = expon / jnp.sum(expon, axis=-1, keepdims=True)
    weights_low = weights.astype(jnp.bfloat16)
    attended = jnp.einsum(
        "axhtu,auxhd->atxhd", weights_low, value_heads, preferred_element_type=wide
    )
    rowdot = jnp.einsum("atxhd,atxhd->axht", grad_heads, attended, preferred_element_type=wide)
    grad_weights = jnp.einsum(
        "atxhd,auxhd->axhtu", grad_heads, value_heads, preferred_element_type=wide
    )
    grad_scores = weights * (grad_weights - rowdot[..., None])
    bias_terms = jnp.einsum("axhtu,tud->axhd", grad_scores, onehot, precision=lax.Precision.HIGHEST)
    grad_low = grad_scores.astype(jnp.bfloat16)
    grad_query = (
        jnp.einsum("axhtu,auxhd->atxhd", grad_low, key_heads, preferred_element_type=wide)
        * score_scale
    ).astype(jnp.bfloat16)
    grad_key = (
        jnp.einsum("axhtu,atxhd->auxhd", grad_low, query_heads, preferred_element_type=wide)
        * score_scale
    ).astype(jnp.bfloat16)
    grad_value = jnp.einsum(
        "axhtu,atxhd->auxhd", weights_low, grad_heads, preferred_element_type=wide
    ).astype(jnp.bfloat16)
    return (grad_query, grad_key, grad_value, bias_terms)


def sum_everywhere(value, sizes):
    for axis, size in sizes:
        if size & (size - 1):
            value = lax.psum(value, axis)
            continue
        step = 1
        while step < size:
            other = lax.ppermute(value, axis, [(i, i ^ step) for i in range(size)])
            value = value + other
            step *= 2
    return value


def by_heads(query_vectors, key_vectors, value_vectors, grad_output, time_bias, sizes):
    head_count = time_bias.shape[0]
    frames = time_bias.shape[1]
    head_dim = query_vectors.shape[3] // head_count
    split_shape = query_vectors.shape[:3] + (head_count, head_dim)
    local_heads = head_count // lax.axis_size("tm")
    first_head = lax.axis_index("tm") * local_heads
    bias_rows = lax.dynamic_slice_in_dim(time_bias, first_head, local_heads, 0)
    spread = [
        lax.all_to_all(item.reshape(split_shape), "tm", split_axis=3, concat_axis=1, tiled=True)
        for item in (query_vectors, key_vectors, value_vectors, grad_output)
    ]
    *grads, bias_terms = attend_back(*spread, bias_rows)
    grads = [
        lax.all_to_all(item, "tm", split_axis=1, concat_axis=3, tiled=True).reshape(
            query_vectors.shape
        )
        for item in grads
    ]
    partial = lax.dynamic_update_slice_in_dim(
        jnp.zeros((head_count, frames), jnp.float32),
        jnp.sum(bias_terms, axis=(0, 1)),
        first_head,
        0,
    )
    return (*grads, sum_everywhere(partial, sizes))


def pair_dots(queries, keys, grads, values, pairs, heads):
    place = lax.broadcasted_iota(jnp.int32, (TILE, LANES), 1)
    held = [jnp.zeros((TILE, LANES), jnp.float32)] * (2 * len(pairs))
    for head in range(heads):
        at = slice(head * LANES, (head + 1) * LANES)
        here = place == head
        load = lambda refs, used: {j: refs[j][at].astype(jnp.float32) for j in used}
        late, early = {t for t, _ in pairs}, {u for _, u in pairs}
        q, k = load(queries, sorted(late)), load(keys, sorted(early))
        o, v = load(grads, sorted(late)), load(values, sorted(early))
        for j, (t, u) in enumerate(pairs):
            score = jnp.sum(q[t] * k[u], axis=1, keepdims=True)
            held[j] = jnp.where(here, score, held[j])
            gain = jnp.sum(o[t] * v[u], axis=1, keepdims=True)
            held[len(pairs) + j] = jnp.where(here, gain, held[len(pairs) + j])
    return held


def over_tiles(rows, body):
    pl.loop(0, rows // TILE)(lambda i: body(i * TILE))


def tile_at(start):
    return pl.ds(pl.multiple_of(start, TILE), TILE)


class Shifted:
    def __init__(self, ref, start):
        self.ref, self.start = ref, start

    def at_rows(self, row):
        return View(self.ref, tile_at(self.start + row))


class View:
    def __init__(self, ref, rows):
        self.ref, self.rows = ref, rows

    def __getitem__(self, lanes):
        return self.ref[self.rows, lanes]

    def __setitem__(self, lanes, value):
        self.ref[self.rows, lanes] = value


def tiles_of(refs, row):
    return tuple(ref if ref is None else ref.at_rows(row) for ref in refs)


def shifted(refs, start):
    return tuple(ref if ref is None else Shifted(ref, start) for ref in refs)


def soft_row(scores, gains):
    top = functools.reduce(jnp.maximum, scores)
    expon = [jnp.exp(item - top) for item in scores]
    total = functools.reduce(jnp.add, expon)
    weights = [item / total for item in expon]
    low = [item.astype(jnp.bfloat16) for item in weights]
    rowdot = functools.reduce(
        jnp.add, [a.astype(jnp.float32) * g for a, g in zip(low, gains)]
    )
    grads = [w * (g - rowdot) for w, g in zip(weights, gains)]
    return low, grads


LOCAL = ((0, 0), (1, 0), (1, 1))
CROSS = ((0, 0), (0, 1), (1, 0), (1, 1))


def unpack(packed, heads, count=6):
    return [
        packed if j == 0 else pltpu.roll(packed, LANES - heads * j, axis=1) for j in range(count)
    ]


def bias_lines(terms):
    lines = []
    for items in terms:
        lines.append(
            jnp.sum(functools.reduce(jnp.add, items), axis=0, keepdims=True)
            if items
            else jnp.zeros((1, LANES), jnp.float32)
        )
    return jnp.concatenate(lines + [jnp.zeros((4, LANES), jnp.float32)], axis=0)


def early_rows(diag, scale, offset):
    score = lambda j, d: diag[j] * scale + offset[d]
    row0 = soft_row([score(0, 0)], [diag[3]])
    row1 = soft_row([score(1, 1), score(2, 0)], [diag[4], diag[5]])
    return row0, row1


def my_place():
    me = lax.axis_index("tm")
    return lax.rem(me, 2), lax.div(me, 2)


def with_frames(own, other, work):
    core, chip = my_place()
    for at_chip in range(2):
        pl.when((chip == at_chip) & (core == 0))(functools.partial(work, at_chip, own, other))
        pl.when((chip == at_chip) & (core == 1))(functools.partial(work, at_chip, other, own))


def chunk_start(chunk, size):
    return jnp.where(my_place()[1] == 0, chunk, CHUNKS - 1 - chunk) * size


def copy_chunks(sources, core, outs, sems):
    size = outs[0].shape[1]
    copies = []
    for c, out in enumerate(outs):
        start = pl.multiple_of(core * CHUNKS * size + chunk_start(c, size), TILE)
        for j, ref in enumerate(sources):
            copies.append(
                pltpu.make_async_copy(
                    ref.at[pl.ds(start, size)], out.at[j], sems.at[len(copies)]
                )
            )
    for copy in copies:
        copy.start()
    for copy in copies:
        copy.wait()


def take_far(refs, outs):
    chip = my_place()[1]

    def take(places):
        for out, place in zip(outs, places):
            for row in range(0, out.shape[0], TILE):
                rows = slice(row, row + TILE)
                out[rows, : refs[place].shape[1]] = refs[place][rows, :]

    pl.when(chip == 0)(lambda: take((1, 2)))
    pl.when(chip == 1)(lambda: take((0, 3)))


def fetch_theirs_kernel(q, k, v, o, *refs):
    nears, other, sems = refs[:CHUNKS], refs[CHUNKS], refs[CHUNKS + 1]
    copy_chunks((q, k, v, o), 1 - my_place()[0], nears, sems)
    take_far(planes(nears[CHUNKS - 1]), planes(other))


def fetch_mine_kernel(q, k, v, o, after, *refs):
    copy_chunks((q, k, v, o), my_place()[0], refs[:-1], refs[-1])


def packed_small(value, heads):
    used = 6 * heads
    place = lax.broadcasted_iota(jnp.int32, value.shape, 1)
    high = value.astype(jnp.bfloat16).astype(jnp.float32)
    middle = (value - high).astype(jnp.bfloat16).astype(jnp.float32)
    rest = (value - high) - middle
    first = jnp.where(place < used, high, pltpu.roll(rest, used, axis=1))
    second = jnp.where(place < used, middle, pltpu.roll(rest, 2 * used - LANES, axis=1))
    return first.astype(jnp.bfloat16), second.astype(jnp.bfloat16)


def unpacked_small(first, second, heads):
    used = 6 * heads
    first, second = first.astype(jnp.float32), second.astype(jnp.float32)
    place = lax.broadcasted_iota(jnp.int32, first.shape, 1)
    rest = jnp.where(
        place < LANES - used,
        pltpu.roll(first, LANES - used, axis=1),
        pltpu.roll(second, 2 * (LANES - used), axis=1),
    )
    return first + second + jnp.where(place < 3 * heads, rest, 0.0)


def local_kernel(heads, scale, table, *refs):
    mines, nears, theirs, refs = refs[:2], refs[2:4], refs[4], refs[5:]
    smalls, out_bias, other, sames = refs[:2], refs[2], refs[3], (refs[4:6], planes(refs[6]))
    core, chip = my_place()
    size, width = mines[0].shape[1:]
    offset = [table[d : d + 1, :] for d in range(4)]
    out_bias[...] = jnp.zeros_like(out_bias)

    def run(a, b, small):
        def tile(row):
            at, bt = tiles_of(a, row), tiles_of(b, row)
            held = pair_dots(
                (at[0], bt[0]), (at[1], bt[1]), (at[3], bt[3]), (at[2], bt[2]), LOCAL, heads
            )
            total = held[0]
            for j in range(1, 6):
                total = total + pltpu.roll(held[j], heads * j, axis=1)
            small[tile_at(row), :] = total
            (_, d0), (_, d1) = early_rows(held, scale, offset)
            lines = bias_lines([[d0[0], d1[1]], [d1[0]], [], []])
            out_bias[...] += jnp.where(chip == 0, lines, jnp.zeros_like(lines))

        over_tiles(size, tile)

    for mine, near, small in zip(mines, nears, smalls):
        own, neighbour = shifted(planes(mine), 0), shifted(planes(near), 0)
        pl.when(core == 0)(functools.partial(run, own, neighbour, small))
        pl.when(core == 1)(functools.partial(run, neighbour, own, small))

    take_far(planes(theirs), planes(other))
    for c, out in enumerate(sames):
        take_far(planes(mines[1 - c]), out)
        for row in range(0, size, TILE):
            rows = slice(row, row + TILE)
            parts = packed_small(smalls[1 - c][rows, :], heads)
            for ref, part in zip(sames[0], parts):
                ref[rows, width + c * LANES : width + (c + 1) * LANES] = part


EARLY, LATE = 14, 10


def cross_sides(chip, a, b):
    if chip == 0:
        return ((a[4], a[5]), (b[4], b[5])), ((a[1], a[2]), (b[1], b[2]))
    return ((a[0], a[3]), (b[0], b[3])), ((a[4], a[5]), (b[4], b[5]))


def far_pairs(chip, parity):
    return [pair for pair in CROSS if pair[chip] == parity]


def cross_dots(queries, keys, pairs, heads):
    return pair_dots(
        [x[0] for x in queries], [x[0] for x in keys],
        [x[1] for x in queries], [x[1] for x in keys], pairs, heads,
    )


def piece_kernel(heads, same, mine, near, *refs):
    far, out = refs[:-1], refs[-1]
    piece = far if len(far) == 2 else planes(far[0])
    own, other = planes(mine), planes(near)
    if same:
        own, other = own + piece, other + (None, None)
    else:
        own, other = own + (None, None), other + piece
    own, other = shifted(own, 0), shifted(other, 0)

    def work(chip, a, b):
        parity = int((a is own) != same)

        def tile(row):
            queries, keys = cross_sides(chip, tiles_of(a, row), tiles_of(b, row))
            held = cross_dots(queries, keys, far_pairs(chip, parity), heads)
            total = held[0]
            for j in range(1, 4):
                total = total + pltpu.roll(held[j], heads * j, axis=1)
            out[tile_at(row), :] = total

        over_tiles(out.shape[0], tile)

    with_frames(own, other, work)


def score_tile(heads, scale, chip, a, b, table, small_own, small_far, known, parity):
    offset = [table[d : d + 1, :] for d in range(4)]
    queries, keys = cross_sides(chip, a, b)
    held = [None] * 8
    for pairs, values in (
        (far_pairs(chip, parity), known),
        (far_pairs(chip, 1 - parity), None),
    ):
        if values is None:
            values = cross_dots(queries, keys, pairs, heads)
        for j, pair in enumerate(pairs):
            held[CROSS.index(pair)] = values[j]
            held[4 + CROSS.index(pair)] = values[2 + j]
    diag = unpack(small_far if chip == 0 else small_own, heads)
    score = lambda j, d: held[j] * scale + offset[d]
    p2, d2 = soft_row(
        [score(0, 2), score(1, 1), diag[0] * scale + offset[0]], [held[4], held[5], diag[3]]
    )
    p3, d3 = soft_row(
        [score(2, 3), score(3, 2), diag[1] * scale + offset[1], diag[2] * scale + offset[0]],
        [held[6], held[7], diag[4], diag[5]],
    )
    lines = bias_lines([[d2[2], d3[3]], [d2[1], d3[2]], [d2[0], d3[1]], [d3[0]]])
    if chip == 1:
        items = [d2[2], d3[2], d3[3], d2[0], d2[1], d3[0], d3[1], p2[2], p3[2], p3[3]]
    else:
        (p0, d0), (p1, d1) = early_rows(unpack(small_own, heads), scale, offset)
        items = [d0[0], d1[0], d1[1], d2[0], d2[1], d3[0], d3[1]]
        items += [p0[0], p1[0], p1[1], p2[0], p2[1], p3[0], p3[1]]
    return [item.astype(jnp.bfloat16) for item in items], lines


def gradient_tile(heads, scale, chip, a, b, items, out_a, out_b):
    width = 2 * LANES
    lines = -(-heads // TILE) * TILE
    line = lax.broadcasted_iota(jnp.int32, (lines, width), 0)
    head = lax.broadcasted_iota(jnp.int32, (lines, width), 1) // LANES
    zeros = jnp.zeros((LANES - lines, width), jnp.bfloat16)
    spread = jnp.concatenate(items, axis=0)

    for pair in range(heads // 2):
        at = slice(pair * width, (pair + 1) * width)
        pick = jnp.where(line == 2 * pair + head, 1.0, 0.0).astype(jnp.bfloat16)
        flat = jnp.dot(
            spread, jnp.concatenate([pick, zeros], axis=0), preferred_element_type=jnp.float32
        )
        w = [flat[j * TILE : (j + 1) * TILE, :] for j in range(len(items))]

        def put(ref, value):
            ref[at] = value.astype(jnp.bfloat16)

        def wide(*refs):
            return [ref[at].astype(jnp.float32) for ref in refs]

        if chip == 0:
            ka, kb = wide(a[1], b[1])
            put(out_a[0], w[0] * ka * scale)
            put(out_b[0], (w[1] * ka + w[2] * kb) * scale)
            for to, x, g, rate in ((1, 0, 0, scale), (2, 3, 7, 1.0)):
                xa, xb, x2, x3 = wide(a[x], b[x], a[3 + to], b[3 + to])
                for_a = w[g] * xa + w[g + 1] * xb + w[g + 3] * x2 + w[g + 5] * x3
                for_b = w[g + 2] * xb + w[g + 4] * x2 + w[g + 6] * x3
                put(out_a[to], for_a * rate)
                put(out_b[to], for_b * rate)
        else:
            k2, k3, k0, k1 = wide(a[1], b[1], a[4], b[4])
            put(out_a[0], (w[0] * k2 + w[3] * k0 + w[4] * k1) * scale)
            put(out_b[0], (w[1] * k2 + w[2] * k3 + w[5] * k0 + w[6] * k1) * scale)
            q2, q3, o2, o3 = wide(a[0], b[0], a[3], b[3])
            put(out_a[1], (w[0] * q2 + w[1] * q3) * scale)
            put(out_b[1], w[2] * q3 * scale)
            put(out_a[2], w[7] * o2 + w[8] * o3)
            put(out_b[2], w[9] * o3)


def planes(ref):
    return tuple(ref.at[j] for j in range(ref.shape[0]))


def frames_of(mine, near, far):
    *same, other = far
    return (
        shifted(planes(mine) + pair_of(same), 0),
        shifted(planes(near) + planes(other), 0),
    )


def pair_of(same):
    return tuple(same) if len(same) == 2 else planes(same[0])


def far_small(far, rows, width, heads, chunk):
    at = slice(width + chunk * LANES, width + (chunk + 1) * LANES)
    return unpacked_small(*(ref[rows, at] for ref in pair_of(far[:-1])), heads)


def score_kernel(heads, scale, known, table, small, bias, mine, near, *refs):
    far, (out_items, out_shares, out_small), lines_ref = refs[:3], refs[3:6], refs[6]
    size, width = mine.shape[1:]
    lines_ref[...] = bias[...]
    own, neighbour = frames_of(mine, near, far)

    def work(chip, a, b):
        def tile(row):
            rows = tile_at(row)
            items, lines = score_tile(
                heads, scale, chip, tiles_of(a, row), tiles_of(b, row), table,
                small[rows, :], far_small(far, rows, width, heads, 0),
                unpack(known[rows, :], heads, 4), int(a is own),
            )
            out_small[rows, :] = far_small(far, rows, width, heads, 1)
            for j, item in enumerate(items):
                out_items[j, rows, :] = item
            lines_ref[...] += lines

        over_tiles(size, tile)

    with_frames(own, neighbour, work)
    for j in range(out_shares.shape[0]):
        out_shares[j] = lines_ref[: out_shares.shape[1], :]


def output_copies(which, piece, outs, chunk, sems, at, offset=0):
    half = outs[0].shape[0] // 2
    start = which * half + chunk_start(chunk, half // CHUNKS) + offset
    rows = pl.ds(pl.multiple_of(start, TILE), piece[0].shape[0])
    return [
        pltpu.make_async_copy(part, out.at[rows], sems.at[at + j])
        for j, (part, out) in enumerate(zip(piece, outs))
    ]


def gradient_kernel(heads, scale, items_ref, mine, near, *refs):
    far, out_others, outs, kept, given, sems = refs[:3], refs[3:5], refs[5:8], *refs[8:]
    own, neighbour = frames_of(mine, near, far)
    own_out, other_out = shifted(planes(kept), 0), shifted(planes(given), 0)

    def work(chip, a, b):
        out_a, out_b = (own_out, other_out) if a is own else (other_out, own_out)

        def tile(row):
            items = [items_ref[j, tile_at(row), :] for j in range(LATE if chip else EARLY)]
            gradient_tile(
                heads, scale, chip, tiles_of(a, row), tiles_of(b, row), items,
                tiles_of(out_a, row), tiles_of(out_b, row),
            )

        over_tiles(mine.shape[1], tile)

    with_frames(own, neighbour, work)
    copies = output_copies(my_place()[0], planes(kept), outs, 0, sems, 0)
    for copy in copies:
        copy.start()
    start = 0
    for out in out_others:
        for row in range(0, out.shape[1], TILE):
            for j in range(3):
                out[j, row : row + TILE, :] = given[j, start + row : start + row + TILE, :]
        start += out.shape[1]
    for copy in copies:
        copy.wait()


def whole_kernel(heads, scale, known, table, small, small_far, mine, near, *refs):
    far, out_own, out_others = refs[:2], refs[2], refs[3:6]
    own, neighbour = frames_of(mine, near, far)
    own_out, other_out = shifted(planes(out_own), 0), shifted(out_others, 0)

    def work(chip, a, b):
        out_a, out_b = (own_out, other_out) if a is own else (other_out, own_out)

        def tile(row):
            at, bt, rows = tiles_of(a, row), tiles_of(b, row), tile_at(row)
            items, _ = score_tile(
                heads, scale, chip, at, bt, table, small[rows, :], small_far[rows, :],
                unpack(known[rows, :], heads, 4), int(a is not own),
            )
            gradient_tile(
                heads, scale, chip, at, bt, items, tiles_of(out_a, row), tiles_of(out_b, row)
            )

        over_tiles(mine.shape[1], tile)

    with_frames(own, neighbour, work)


def early_output_kernel(*refs):
    first_backs, kept, outs, sems = refs[:2], planes(refs[2]), refs[6:9], refs[9]
    core = my_place()[0]
    copies = output_copies(core, kept, outs, 1, sems, 0)
    offset = 0
    for j, ref in enumerate(first_backs):
        copies += output_copies(1 - core, planes(ref), outs, 0, sems, 3 + 3 * j, offset)
        offset += ref.shape[1]
    for copy in copies:
        copy.start()
    for copy in copies:
        copy.wait()


def late_output_kernel(*refs):
    back, outs, sems = refs[:3], refs[6:9], refs[9]
    copies = output_copies(1 - my_place()[0], back, outs, 1, sems, 0)
    for copy in copies:
        copy.start()
    for copy in copies:
        copy.wait()


def bias_kernel(shares, after, out_bias, total, sem):
    parts = [shares[j] for j in range(shares.shape[0])]
    while len(parts) > 1:
        parts = [a + b for a, b in zip(parts[::2], parts[1::2])]
    total[...] = parts[0][: total.shape[0], : total.shape[1]]
    copy = pltpu.make_async_copy(total, out_bias, sem)
    copy.start()
    copy.wait()


def by_chips(query_vectors, key_vectors, value_vectors, grad_output, time_bias, sizes):
    heads, frames = time_bias.shape
    clips, _, patches, width = query_vectors.shape
    rows = clips * patches
    half = rows // 2
    size = half // CHUNKS
    scale = 1.0 / math.sqrt(width // heads)
    own = [
        pltpu.with_memory_space_constraint(x.reshape(rows, width), pltpu.HBM)
        for x in (query_vectors, key_vectors, value_vectors, grad_output)
    ]
    vmem_spec = pl.BlockSpec(memory_space=pltpu.VMEM)
    any_spec = pl.BlockSpec(memory_space=pl.ANY)

    def swap(x, bits):
        return lax.ppermute(x, "tm", [(i, i ^ bits) for i in range(4)])

    def shape(*dims, dtype=jnp.bfloat16):
        return jax.ShapeDtypeStruct(dims, dtype)

    def call(kernel, name, out_shape, *args, scratch=(), hbm=(), hbm_out=(), aliases={}):
        return pl.pallas_call(
            kernel,
            in_specs=[any_spec if j in hbm else vmem_spec for j in range(len(args))],
            out_specs=[any_spec if j in hbm_out else vmem_spec for j in range(len(out_shape))],
            out_shape=out_shape,
            scratch_shapes=scratch,
            input_output_aliases=aliases,
            compiler_params=pltpu.CompilerParams(vmem_limit_bytes=16 * 2**20),
            cost_estimate=LITTLE,
            name=name,
        )(*args)

    wide = jnp.float32
    lines = shape(8, LANES, dtype=wide)
    chunk_shape, far_shape = shape(4, size, width), shape(2, size, width)
    copies = [pltpu.SemaphoreType.DMA((4 * CHUNKS,))]
    table = jnp.pad(time_bias.T, ((0, 8 - frames), (0, LANES - heads)))

    *theirs, other = call(
        fetch_theirs_kernel, "fetch_theirs", [chunk_shape] * CHUNKS + [far_shape], *own,
        scratch=copies, hbm=range(4),
    )
    nears = [swap(x, 1) for x in theirs]
    others = [swap(other, 3)]
    mines = call(
        fetch_mine_kernel, "fetch_mine", [chunk_shape] * CHUNKS, *own, other,
        scratch=copies, hbm=range(5),
    )

    *smalls, bias, other, same_first, same_second, same = call(
        functools.partial(local_kernel, heads, scale),
        "local_scores",
        [shape(size, LANES, dtype=wide)] * CHUNKS
        + [lines, far_shape]
        + [shape(size, width + CHUNKS * LANES)] * 2
        + [far_shape],
        table, *mines, *nears, theirs[0],
    )
    sames = [[swap(same_first, 2), swap(same_second, 2)], [swap(same, 2)]]
    others.append(swap(other, 3))

    whole = pltpu.HBM((rows, width), jnp.bfloat16)
    stack, piece = shape(3, size, width), shape(size, width)
    output_sems = pltpu.SemaphoreType.DMA((13,))
    first = (mines[0], nears[0], *sames[0], others[0])
    (known,) = call(
        functools.partial(piece_kernel, heads, False),
        "first_dots",
        [shape(size, LANES, dtype=wide)],
        mines[0], nears[0], others[0],
    )
    items, shares, small_far = call(
        functools.partial(score_kernel, heads, scale),
        "scores",
        [
            shape(EARLY, size, LANES),
            shape(math.prod(count for _, count in sizes), 8, LANES, dtype=wide),
            shape(size, LANES, dtype=wide),
        ],
        known, table, smalls[0], bias, *first,
        scratch=[pltpu.VMEM((8, LANES), wide)],
    )
    shares = lax.all_to_all(shares, tuple(axis for axis, _ in sizes), 0, 0, tiled=True)
    *back, grad_queries, grad_keys, grad_values = call(
        functools.partial(gradient_kernel, heads, scale),
        "gradients",
        [shape(3, size // 2, width)] * 2 + [whole] * 3,
        items, *first,
        scratch=[pltpu.VMEM((3, size, width), jnp.bfloat16)] * 2 + [output_sems],
        hbm_out=range(2, 5),
    )
    grads = (grad_queries, grad_keys, grad_values)
    first_backs = [swap(x, 1) for x in back]

    (known_last,) = call(
        functools.partial(piece_kernel, heads, True),
        "last_dots",
        [shape(size, LANES, dtype=wide)],
        mines[1], nears[1], *sames[1],
    )
    kept, *back = call(
        functools.partial(whole_kernel, heads, scale),
        "scores_and_gradients",
        [stack] + [piece] * 3,
        known_last, table, smalls[1], small_far, mines[1], nears[1], *sames[1], others[1],
    )
    back = [swap(x, 1) for x in back]
    in_hbm = lambda arrays: [pltpu.with_memory_space_constraint(x, pltpu.HBM) for x in arrays]
    grads = call(
        early_output_kernel,
        "early_outputs",
        [whole] * 3,
        *first_backs, kept, *in_hbm(grads),
        scratch=[output_sems],
        hbm=range(3, 6),
        hbm_out=range(3),
        aliases={3 + j: j for j in range(3)},
    )
    grads = call(
        late_output_kernel,
        "late_outputs",
        [whole] * 3,
        *back, *in_hbm(grads),
        scratch=[output_sems],
        hbm=range(3, 6),
        hbm_out=range(3),
        aliases={3 + j: j for j in range(3)},
    )
    (bias,) = call(
        bias_kernel,
        "bias",
        [shape(frames, heads, dtype=wide)],
        shares, *in_hbm(grads[:1]),
        scratch=[pltpu.VMEM((frames, heads), wide), pltpu.SemaphoreType.DMA],
        hbm=(1,),
        hbm_out=(0,),
    )
    return (*[x.reshape(query_vectors.shape) for x in grads], bias.T)


def solution(mesh):
    sizes = tuple((axis, mesh.shape[axis]) for axis in ("tm", "patch"))

    def per_device(*args):
        heads, frames = args[4].shape
        fits = (
            mesh.shape["tm"] == 4
            and frames == 4
            and args[0].shape[1] == 1
            and heads * LANES == args[0].shape[3]
            and 3 * heads <= 2 * (LANES - 6 * heads)
            and heads % 2 == 0
            and args[0].shape[0] * args[0].shape[2] % (2 * TILE * CHUNKS) == 0
            and mesh.shape["patch"].bit_count() == 1
        )
        return (by_chips if fits else by_heads)(*args, sizes)

    vectors = P(None, "tm", "patch", None)
    return jax.shard_map(
        per_device,
        mesh=mesh,
        in_specs=(vectors,) * 4 + (P(),),
        out_specs=(vectors,) * 3 + (P(),),
        check_vma=False,
    )
```

```python
import functools
import math

import jax
import jax.numpy as jnp
from jax import lax
from jax.experimental import pallas as pl
from jax.experimental.pallas import tpu as pltpu
from jax.sharding import PartitionSpec as P

LANES = 128
TILE = 32
ALIGN = 16
LITTLE = pl.CostEstimate(flops=1, bytes_accessed=1, transcendentals=0)
CHUNKS = 2


def score_table(bias_rows, frames):
    steps = jnp.arange(frames, dtype=jnp.int32)
    offsets = steps[:, None] - steps[None, :]
    onehot = (offsets[:, :, None] == steps[None, None, :]).astype(jnp.float32)
    table = jnp.einsum("hd,tud->htu", bias_rows, onehot, precision=lax.Precision.HIGHEST)
    return (table, offsets >= 0, onehot)


def attend_back(query_heads, key_heads, value_heads, grad_heads, bias_rows):
    frames = query_heads.shape[1]
    score_scale = 1.0 / math.sqrt(query_heads.shape[4])
    table, causal, onehot = score_table(bias_rows, frames)
    wide = jnp.float32
    scores = (
        jnp.einsum("atxhd,auxhd->axhtu", query_heads, key_heads, preferred_element_type=wide)
        * score_scale
        + table[None, None]
    )
    scores = jnp.where(causal, scores, -jnp.inf)
    row_max = jnp.max(scores, axis=-1, keepdims=True)
    expon = jnp.exp(scores - row_max)
    weights = expon / jnp.sum(expon, axis=-1, keepdims=True)
    weights_low = weights.astype(jnp.bfloat16)
    attended = jnp.einsum(
        "axhtu,auxhd->atxhd", weights_low, value_heads, preferred_element_type=wide
    )
    rowdot = jnp.einsum("atxhd,atxhd->axht", grad_heads, attended, preferred_element_type=wide)
    grad_weights = jnp.einsum(
        "atxhd,auxhd->axhtu", grad_heads, value_heads, preferred_element_type=wide
    )
    grad_scores = weights * (grad_weights - rowdot[..., None])
    bias_terms = jnp.einsum("axhtu,tud->axhd", grad_scores, onehot, precision=lax.Precision.HIGHEST)
    grad_low = grad_scores.astype(jnp.bfloat16)
    grad_query = (
        jnp.einsum("axhtu,auxhd->atxhd", grad_low, key_heads, preferred_element_type=wide)
        * score_scale
    ).astype(jnp.bfloat16)
    grad_key = (
        jnp.einsum("axhtu,atxhd->auxhd", grad_low, query_heads, preferred_element_type=wide)
        * score_scale
    ).astype(jnp.bfloat16)
    grad_value = jnp.einsum(
        "axhtu,atxhd->auxhd", weights_low, grad_heads, preferred_element_type=wide
    ).astype(jnp.bfloat16)
    return (grad_query, grad_key, grad_value, bias_terms)


def sum_everywhere(value, sizes):
    for axis, size in sizes:
        if size & (size - 1):
            value = lax.psum(value, axis)
            continue
        step = 1
        while step < size:
            other = lax.ppermute(value, axis, [(i, i ^ step) for i in range(size)])
            value = value + other
            step *= 2
    return value


def by_heads(query_vectors, key_vectors, value_vectors, grad_output, time_bias, sizes):
    head_count = time_bias.shape[0]
    frames = time_bias.shape[1]
    head_dim = query_vectors.shape[3] // head_count
    split_shape = query_vectors.shape[:3] + (head_count, head_dim)
    local_heads = head_count // lax.axis_size("tm")
    first_head = lax.axis_index("tm") * local_heads
    bias_rows = lax.dynamic_slice_in_dim(time_bias, first_head, local_heads, 0)
    spread = [
        lax.all_to_all(item.reshape(split_shape), "tm", split_axis=3, concat_axis=1, tiled=True)
        for item in (query_vectors, key_vectors, value_vectors, grad_output)
    ]
    *grads, bias_terms = attend_back(*spread, bias_rows)
    grads = [
        lax.all_to_all(item, "tm", split_axis=1, concat_axis=3, tiled=True).reshape(
            query_vectors.shape
        )
        for item in grads
    ]
    partial = lax.dynamic_update_slice_in_dim(
        jnp.zeros((head_count, frames), jnp.float32),
        jnp.sum(bias_terms, axis=(0, 1)),
        first_head,
        0,
    )
    return (*grads, sum_everywhere(partial, sizes))


def pair_dots(queries, keys, grads, values, pairs, heads):
    place = lax.broadcasted_iota(jnp.int32, (TILE, LANES), 1)
    held = [jnp.zeros((TILE, LANES), jnp.float32)] * (2 * len(pairs))
    for head in range(heads):
        at = slice(head * LANES, (head + 1) * LANES)
        here = place == head
        load = lambda refs, used: {j: refs[j][at].astype(jnp.float32) for j in used}
        late, early = {t for t, _ in pairs}, {u for _, u in pairs}
        q, k = load(queries, sorted(late)), load(keys, sorted(early))
        o, v = load(grads, sorted(late)), load(values, sorted(early))
        for j, (t, u) in enumerate(pairs):
            score = jnp.sum(q[t] * k[u], axis=1, keepdims=True)
            held[j] = jnp.where(here, score, held[j])
            gain = jnp.sum(o[t] * v[u], axis=1, keepdims=True)
            held[len(pairs) + j] = jnp.where(here, gain, held[len(pairs) + j])
    return held


def over_tiles(rows, body):
    pl.loop(0, rows // TILE)(lambda i: body(i * TILE))


def tile_at(start):
    return pl.ds(pl.multiple_of(start, TILE), TILE)


class Shifted:
    def __init__(self, ref, start):
        self.ref, self.start = ref, start

    def at_rows(self, row):
        return View(self.ref, tile_at(self.start + row))


class View:
    def __init__(self, ref, rows):
        self.ref, self.rows = ref, rows

    def __getitem__(self, lanes):
        return self.ref[self.rows, lanes]

    def __setitem__(self, lanes, value):
        self.ref[self.rows, lanes] = value


def tiles_of(refs, row):
    return tuple(ref if ref is None else ref.at_rows(row) for ref in refs)


def shifted(refs, start):
    return tuple(ref if ref is None else Shifted(ref, start) for ref in refs)


def soft_row(scores, gains):
    top = functools.reduce(jnp.maximum, scores)
    expon = [jnp.exp(item - top) for item in scores]
    total = functools.reduce(jnp.add, expon)
    weights = [item / total for item in expon]
    low = [item.astype(jnp.bfloat16) for item in weights]
    rowdot = functools.reduce(
        jnp.add, [a.astype(jnp.float32) * g for a, g in zip(low, gains)]
    )
    grads = [w * (g - rowdot) for w, g in zip(weights, gains)]
    return low, grads


LOCAL = ((0, 0), (1, 0), (1, 1))
CROSS = ((0, 0), (0, 1), (1, 0), (1, 1))


def unpack(packed, heads, count=6):
    return [
        packed if j == 0 else pltpu.roll(packed, LANES - heads * j, axis=1) for j in range(count)
    ]


def bias_lines(terms):
    lines = []
    for items in terms:
        lines.append(
            jnp.sum(functools.reduce(jnp.add, items), axis=0, keepdims=True)
            if items
            else jnp.zeros((1, LANES), jnp.float32)
        )
    return jnp.concatenate(lines + [jnp.zeros((4, LANES), jnp.float32)], axis=0)


def early_rows(diag, scale, offset):
    score = lambda j, d: diag[j] * scale + offset[d]
    row0 = soft_row([score(0, 0)], [diag[3]])
    row1 = soft_row([score(1, 1), score(2, 0)], [diag[4], diag[5]])
    return row0, row1


def my_place():
    me = lax.axis_index("tm")
    return lax.rem(me, 2), lax.div(me, 2)


def with_frames(own, other, work):
    core, chip = my_place()
    for at_chip in range(2):
        pl.when((chip == at_chip) & (core == 0))(functools.partial(work, at_chip, own, other))
        pl.when((chip == at_chip) & (core == 1))(functools.partial(work, at_chip, other, own))


def chunk_start(chunk, size):
    return jnp.where(my_place()[1] == 0, chunk, CHUNKS - 1 - chunk) * size


def copy_chunks(sources, core, outs, sems):
    size = outs[0].shape[1]
    copies = []
    for c, out in enumerate(outs):
        start = pl.multiple_of(core * CHUNKS * size + chunk_start(c, size), TILE)
        for j, ref in enumerate(sources):
            copies.append(
                pltpu.make_async_copy(
                    ref.at[pl.ds(start, size)], out.at[j], sems.at[len(copies)]
                )
            )
    for copy in copies:
        copy.start()
    for copy in copies:
        copy.wait()


def take_far(refs, outs):
    chip = my_place()[1]

    def take(places):
        for out, place in zip(outs, places):
            for row in range(0, out.shape[0], TILE):
                rows = slice(row, row + TILE)
                out[rows, : refs[place].shape[1]] = refs[place][rows, :]

    pl.when(chip == 0)(lambda: take((1, 2)))
    pl.when(chip == 1)(lambda: take((0, 3)))


def fetch_theirs_kernel(q, k, v, o, *refs):
    nears, other, sems = refs[:CHUNKS], refs[CHUNKS], refs[CHUNKS + 1]
    copy_chunks((q, k, v, o), 1 - my_place()[0], nears, sems)
    take_far(planes(nears[CHUNKS - 1]), planes(other))


def fetch_mine_kernel(q, k, v, o, after, *refs):
    copy_chunks((q, k, v, o), my_place()[0], refs[:-1], refs[-1])


def packed_small(value, heads):
    used = 6 * heads
    place = lax.broadcasted_iota(jnp.int32, value.shape, 1)
    high = value.astype(jnp.bfloat16).astype(jnp.float32)
    middle = (value - high).astype(jnp.bfloat16).astype(jnp.float32)
    rest = (value - high) - middle
    first = jnp.where(place < used, high, pltpu.roll(rest, used, axis=1))
    second = jnp.where(place < used, middle, pltpu.roll(rest, 2 * used - LANES, axis=1))
    return first.astype(jnp.bfloat16), second.astype(jnp.bfloat16)


def unpacked_small(first, second, heads):
    used = 6 * heads
    first, second = first.astype(jnp.float32), second.astype(jnp.float32)
    place = lax.broadcasted_iota(jnp.int32, first.shape, 1)
    rest = jnp.where(
        place < LANES - used,
        pltpu.roll(first, LANES - used, axis=1),
        pltpu.roll(second, 2 * (LANES - used), axis=1),
    )
    return first + second + jnp.where(place < 3 * heads, rest, 0.0)


def local_kernel(heads, scale, table, *refs):
    mines, nears, theirs, refs = refs[:2], refs[2:4], refs[4], refs[5:]
    smalls, out_bias, other, sames = refs[:2], refs[2], refs[3], (refs[4:6], planes(refs[6]))
    core, chip = my_place()
    size, width = mines[0].shape[1:]
    offset = [table[d : d + 1, :] for d in range(4)]
    out_bias[...] = jnp.zeros_like(out_bias)

    def run(a, b, small):
        def tile(row):
            at, bt = tiles_of(a, row), tiles_of(b, row)
            held = pair_dots(
                (at[0], bt[0]), (at[1], bt[1]), (at[3], bt[3]), (at[2], bt[2]), LOCAL, heads
            )
            total = held[0]
            for j in range(1, 6):
                total = total + pltpu.roll(held[j], heads * j, axis=1)
            small[tile_at(row), :] = total
            (_, d0), (_, d1) = early_rows(held, scale, offset)
            lines = bias_lines([[d0[0], d1[1]], [d1[0]], [], []])
            out_bias[...] += jnp.where(chip == 0, lines, jnp.zeros_like(lines))

        over_tiles(size, tile)

    for mine, near, small in zip(mines, nears, smalls):
        own, neighbour = shifted(planes(mine), 0), shifted(planes(near), 0)
        pl.when(core == 0)(functools.partial(run, own, neighbour, small))
        pl.when(core == 1)(functools.partial(run, neighbour, own, small))

    take_far(planes(theirs), planes(other))
    for c, out in enumerate(sames):
        take_far(planes(mines[1 - c]), out)
        for row in range(0, size, TILE):
            rows = slice(row, row + TILE)
            parts = packed_small(smalls[1 - c][rows, :], heads)
            for ref, part in zip(sames[0], parts):
                ref[rows, width + c * LANES : width + (c + 1) * LANES] = part


EARLY, LATE = 14, 10


def cross_sides(chip, a, b):
    if chip == 0:
        return ((a[4], a[5]), (b[4], b[5])), ((a[1], a[2]), (b[1], b[2]))
    return ((a[0], a[3]), (b[0], b[3])), ((a[4], a[5]), (b[4], b[5]))


def far_pairs(chip, parity):
    return [pair for pair in CROSS if pair[chip] == parity]


def cross_dots(queries, keys, pairs, heads):
    return pair_dots(
        [x[0] for x in queries], [x[0] for x in keys],
        [x[1] for x in queries], [x[1] for x in keys], pairs, heads,
    )


def piece_kernel(heads, same, mine, near, *refs):
    far, out = refs[:-1], refs[-1]
    piece = far if len(far) == 2 else planes(far[0])
    own, other = planes(mine), planes(near)
    if same:
        own, other = own + piece, other + (None, None)
    else:
        own, other = own + (None, None), other + piece
    own, other = shifted(own, 0), shifted(other, 0)

    def work(chip, a, b):
        parity = int((a is own) != same)

        def tile(row):
            queries, keys = cross_sides(chip, tiles_of(a, row), tiles_of(b, row))
            held = cross_dots(queries, keys, far_pairs(chip, parity), heads)
            total = held[0]
            for j in range(1, 4):
                total = total + pltpu.roll(held[j], heads * j, axis=1)
            out[tile_at(row), :] = total

        over_tiles(out.shape[0], tile)

    with_frames(own, other, work)


def score_tile(heads, scale, chip, a, b, table, small_own, small_far, known, parity):
    offset = [table[d : d + 1, :] for d in range(4)]
    queries, keys = cross_sides(chip, a, b)
    held = [None] * 8
    for pairs, values in (
        (far_pairs(chip, parity), known),
        (far_pairs(chip, 1 - parity), None),
    ):
        if values is None:
            values = cross_dots(queries, keys, pairs, heads)
        for j, pair in enumerate(pairs):
            held[CROSS.index(pair)] = values[j]
            held[4 + CROSS.index(pair)] = values[2 + j]
    diag = unpack(small_far if chip == 0 else small_own, heads)
    score = lambda j, d: held[j] * scale + offset[d]
    p2, d2 = soft_row(
        [score(0, 2), score(1, 1), diag[0] * scale + offset[0]], [held[4], held[5], diag[3]]
    )
    p3, d3 = soft_row(
        [score(2, 3), score(3, 2), diag[1] * scale + offset[1], diag[2] * scale + offset[0]],
        [held[6], held[7], diag[4], diag[5]],
    )
    lines = bias_lines([[d2[2], d3[3]], [d2[1], d3[2]], [d2[0], d3[1]], [d3[0]]])
    if chip == 1:
        items = [d2[2], d3[2], d3[3], d2[0], d2[1], d3[0], d3[1], p2[2], p3[2], p3[3]]
    else:
        (p0, d0), (p1, d1) = early_rows(unpack(small_own, heads), scale, offset)
        items = [d0[0], d1[0], d1[1], d2[0], d2[1], d3[0], d3[1]]
        items += [p0[0], p1[0], p1[1], p2[0], p2[1], p3[0], p3[1]]
    return [item.astype(jnp.bfloat16) for item in items], lines


def gradient_tile(heads, scale, chip, a, b, items, out_a, out_b):
    width = 2 * LANES
    lines = -(-heads // TILE) * TILE
    line = lax.broadcasted_iota(jnp.int32, (lines, width), 0)
    head = lax.broadcasted_iota(jnp.int32, (lines, width), 1) // LANES
    zeros = jnp.zeros((LANES - lines, width), jnp.bfloat16)
    spread = jnp.concatenate(items, axis=0)

    for pair in range(heads // 2):
        at = slice(pair * width, (pair + 1) * width)
        pick = jnp.where(line == 2 * pair + head, 1.0, 0.0).astype(jnp.bfloat16)
        flat = jnp.dot(
            spread, jnp.concatenate([pick, zeros], axis=0), preferred_element_type=jnp.float32
        )
        w = [flat[j * TILE : (j + 1) * TILE, :] for j in range(len(items))]

        def put(ref, value):
            ref[at] = value.astype(jnp.bfloat16)

        def wide(*refs):
            return [ref[at].astype(jnp.float32) for ref in refs]

        if chip == 0:
            ka, kb = wide(a[1], b[1])
            put(out_a[0], w[0] * ka * scale)
            put(out_b[0], (w[1] * ka + w[2] * kb) * scale)
            for to, x, g, rate in ((1, 0, 0, scale), (2, 3, 7, 1.0)):
                xa, xb, x2, x3 = wide(a[x], b[x], a[3 + to], b[3 + to])
                for_a = w[g] * xa + w[g + 1] * xb + w[g + 3] * x2 + w[g + 5] * x3
                for_b = w[g + 2] * xb + w[g + 4] * x2 + w[g + 6] * x3
                put(out_a[to], for_a * rate)
                put(out_b[to], for_b * rate)
        else:
            k2, k3, k0, k1 = wide(a[1], b[1], a[4], b[4])
            put(out_a[0], (w[0] * k2 + w[3] * k0 + w[4] * k1) * scale)
            put(out_b[0], (w[1] * k2 + w[2] * k3 + w[5] * k0 + w[6] * k1) * scale)
            q2, q3, o2, o3 = wide(a[0], b[0], a[3], b[3])
            put(out_a[1], (w[0] * q2 + w[1] * q3) * scale)
            put(out_b[1], w[2] * q3 * scale)
            put(out_a[2], w[7] * o2 + w[8] * o3)
            put(out_b[2], w[9] * o3)


def planes(ref):
    return tuple(ref.at[j] for j in range(ref.shape[0]))


def frames_of(mine, near, far):
    *same, other = far
    return (
        shifted(planes(mine) + pair_of(same), 0),
        shifted(planes(near) + planes(other), 0),
    )


def pair_of(same):
    return tuple(same) if len(same) == 2 else planes(same[0])


def far_small(far, rows, width, heads, chunk):
    at = slice(width + chunk * LANES, width + (chunk + 1) * LANES)
    return unpacked_small(*(ref[rows, at] for ref in pair_of(far[:-1])), heads)


def score_kernel(heads, scale, known, table, small, bias, mine, near, *refs):
    far, (out_items, out_shares, out_small), lines_ref = refs[:3], refs[3:6], refs[6]
    size, width = mine.shape[1:]
    lines_ref[...] = bias[...]
    own, neighbour = frames_of(mine, near, far)

    def work(chip, a, b):
        def tile(row):
            rows = tile_at(row)
            items, lines = score_tile(
                heads, scale, chip, tiles_of(a, row), tiles_of(b, row), table,
                small[rows, :], far_small(far, rows, width, heads, 0),
                unpack(known[rows, :], heads, 4), int(a is own),
            )
            out_small[rows, :] = far_small(far, rows, width, heads, 1)
            for j, item in enumerate(items):
                out_items[j, rows, :] = item
            lines_ref[...] += lines

        over_tiles(size, tile)

    with_frames(own, neighbour, work)
    for j in range(out_shares.shape[0]):
        out_shares[j] = lines_ref[: out_shares.shape[1], :]


def output_copies(which, piece, outs, chunk, sems, at, offset=0):
    half = outs[0].shape[0] // 2
    start = which * half + chunk_start(chunk, half // CHUNKS) + offset
    rows = pl.ds(pl.multiple_of(start, ALIGN), piece[0].shape[0])
    return [
        pltpu.make_async_copy(part, out.at[rows], sems.at[at + j])
        for j, (part, out) in enumerate(zip(piece, outs))
    ]


def gradient_kernel(heads, scale, items_ref, mine, near, *refs):
    far, out_others, outs, kept, given, sems = refs[:3], refs[3:5], refs[5:8], *refs[8:]
    own, neighbour = frames_of(mine, near, far)
    own_out, other_out = shifted(planes(kept), 0), shifted(planes(given), 0)

    def work(chip, a, b):
        out_a, out_b = (own_out, other_out) if a is own else (other_out, own_out)

        def tile(row):
            items = [items_ref[j, tile_at(row), :] for j in range(LATE if chip else EARLY)]
            gradient_tile(
                heads, scale, chip, tiles_of(a, row), tiles_of(b, row), items,
                tiles_of(out_a, row), tiles_of(out_b, row),
            )

        over_tiles(mine.shape[1], tile)

    with_frames(own, neighbour, work)
    copies = output_copies(my_place()[0], planes(kept), outs, 0, sems, 0)
    for copy in copies:
        copy.start()
    start = 0
    for out in out_others:
        for j in range(3):
            out[j] = given[j, start : start + out.shape[1], :]
        start += out.shape[1]
    for copy in copies:
        copy.wait()


def whole_kernel(heads, scale, known, table, small, small_far, mine, near, *refs):
    far, out_own, out_others = refs[:2], refs[2], refs[3:6]
    own, neighbour = frames_of(mine, near, far)
    own_out, other_out = shifted(planes(out_own), 0), shifted(out_others, 0)

    def work(chip, a, b):
        out_a, out_b = (own_out, other_out) if a is own else (other_out, own_out)

        def tile(row):
            at, bt, rows = tiles_of(a, row), tiles_of(b, row), tile_at(row)
            items, _ = score_tile(
                heads, scale, chip, at, bt, table, small[rows, :], small_far[rows, :],
                unpack(known[rows, :], heads, 4), int(a is not own),
            )
            gradient_tile(
                heads, scale, chip, at, bt, items, tiles_of(out_a, row), tiles_of(out_b, row)
            )

        over_tiles(mine.shape[1], tile)

    with_frames(own, neighbour, work)


def early_output_kernel(*refs):
    first_backs, kept, outs, sems = refs[:2], planes(refs[2]), refs[6:9], refs[9]
    core = my_place()[0]
    copies = output_copies(core, kept, outs, 1, sems, 0)
    offset = 0
    for j, ref in enumerate(first_backs):
        copies += output_copies(1 - core, planes(ref), outs, 0, sems, 3 + 3 * j, offset)
        offset += ref.shape[1]
    for copy in copies:
        copy.start()
    for copy in copies:
        copy.wait()


def output_kernel(*refs):
    back, shares, outs, out_bias, total, sems = refs[:3], refs[3], refs[7:10], *refs[10:]
    copies = output_copies(1 - my_place()[0], back, outs, 1, sems, 0)
    for copy in copies:
        copy.start()
    parts = [shares[j] for j in range(shares.shape[0])]
    while len(parts) > 1:
        parts = [a + b for a, b in zip(parts[::2], parts[1::2])]
    total[...] = parts[0][: total.shape[0], : total.shape[1]]
    copies.append(pltpu.make_async_copy(total, out_bias, sems.at[len(copies)]))
    copies[-1].start()
    for copy in copies:
        copy.wait()


def by_chips(query_vectors, key_vectors, value_vectors, grad_output, time_bias, sizes):
    heads, frames = time_bias.shape
    clips, _, patches, width = query_vectors.shape
    rows = clips * patches
    half = rows // 2
    size = half // CHUNKS
    scale = 1.0 / math.sqrt(width // heads)
    own = [
        pltpu.with_memory_space_constraint(x.reshape(rows, width), pltpu.HBM)
        for x in (query_vectors, key_vectors, value_vectors, grad_output)
    ]
    vmem_spec = pl.BlockSpec(memory_space=pltpu.VMEM)
    any_spec = pl.BlockSpec(memory_space=pl.ANY)

    def swap(x, bits):
        return lax.ppermute(x, "tm", [(i, i ^ bits) for i in range(4)])

    def shape(*dims, dtype=jnp.bfloat16):
        return jax.ShapeDtypeStruct(dims, dtype)

    def call(kernel, name, out_shape, *args, scratch=(), hbm=(), hbm_out=(), aliases={}):
        return pl.pallas_call(
            kernel,
            in_specs=[any_spec if j in hbm else vmem_spec for j in range(len(args))],
            out_specs=[any_spec if j in hbm_out else vmem_spec for j in range(len(out_shape))],
            out_shape=out_shape,
            scratch_shapes=scratch,
            input_output_aliases=aliases,
            compiler_params=pltpu.CompilerParams(vmem_limit_bytes=16 * 2**20),
            cost_estimate=LITTLE,
            name=name,
        )(*args)

    wide = jnp.float32
    lines = shape(8, LANES, dtype=wide)
    chunk_shape, far_shape = shape(4, size, width), shape(2, size, width)
    copies = [pltpu.SemaphoreType.DMA((4 * CHUNKS,))]
    table = jnp.pad(time_bias.T, ((0, 8 - frames), (0, LANES - heads)))

    *theirs, other = call(
        fetch_theirs_kernel, "fetch_theirs", [chunk_shape] * CHUNKS + [far_shape], *own,
        scratch=copies, hbm=range(4),
    )
    nears = [swap(x, 1) for x in theirs]
    others = [swap(other, 3)]
    mines = call(
        fetch_mine_kernel, "fetch_mine", [chunk_shape] * CHUNKS, *own, other,
        scratch=copies, hbm=range(5),
    )

    *smalls, bias, other, same_first, same_second, same = call(
        functools.partial(local_kernel, heads, scale),
        "local_scores",
        [shape(size, LANES, dtype=wide)] * CHUNKS
        + [lines, far_shape]
        + [shape(size, width + CHUNKS * LANES)] * 2
        + [far_shape],
        table, *mines, *nears, theirs[0],
    )
    sames = [[swap(same_first, 2), swap(same_second, 2)], [swap(same, 2)]]
    others.append(swap(other, 3))

    whole = pltpu.HBM((rows, width), jnp.bfloat16)
    stack, piece = shape(3, size, width), shape(size, width)
    output_sems = pltpu.SemaphoreType.DMA((13,))
    first = (mines[0], nears[0], *sames[0], others[0])
    (known,) = call(
        functools.partial(piece_kernel, heads, False),
        "first_dots",
        [shape(size, LANES, dtype=wide)],
        mines[0], nears[0], others[0],
    )
    items, shares, small_far = call(
        functools.partial(score_kernel, heads, scale),
        "scores",
        [
            shape(EARLY, size, LANES),
            shape(math.prod(count for _, count in sizes), 8, LANES, dtype=wide),
            shape(size, LANES, dtype=wide),
        ],
        known, table, smalls[0], bias, *first,
        scratch=[pltpu.VMEM((8, LANES), wide)],
    )
    shares = lax.all_to_all(shares, tuple(axis for axis, _ in sizes), 0, 0, tiled=True)
    *back, grad_queries, grad_keys, grad_values = call(
        functools.partial(gradient_kernel, heads, scale),
        "gradients",
        [shape(3, size // 2, width)] * 2 + [whole] * 3,
        items, *first,
        scratch=[pltpu.VMEM((3, size, width), jnp.bfloat16)] * 2 + [output_sems],
        hbm_out=range(2, 5),
    )
    grads = (grad_queries, grad_keys, grad_values)
    first_backs = [swap(x, 1) for x in back]

    (known_last,) = call(
        functools.partial(piece_kernel, heads, True),
        "last_dots",
        [shape(size, LANES, dtype=wide)],
        mines[1], nears[1], *sames[1],
    )
    kept, *back = call(
        functools.partial(whole_kernel, heads, scale),
        "scores_and_gradients",
        [stack] + [piece] * 3,
        known_last, table, smalls[1], small_far, mines[1], nears[1], *sames[1], others[1],
    )
    back = [swap(x, 1) for x in back]
    in_hbm = lambda arrays: [pltpu.with_memory_space_constraint(x, pltpu.HBM) for x in arrays]
    grads = call(
        early_output_kernel,
        "early_outputs",
        [whole] * 3,
        *first_backs, kept, *in_hbm(grads),
        scratch=[output_sems],
        hbm=range(3, 6),
        hbm_out=range(3),
        aliases={3 + j: j for j in range(3)},
    )
    *grads, bias = call(
        output_kernel,
        "outputs",
        [whole] * 3 + [shape(frames, heads, dtype=wide)],
        *back, shares, *in_hbm(grads),
        scratch=[pltpu.VMEM((frames, heads), wide), output_sems],
        hbm=range(4, 7),
        hbm_out=range(4),
        aliases={4 + j: j for j in range(3)},
    )
    return (*[x.reshape(query_vectors.shape) for x in grads], bias.T)


def solution(mesh):
    sizes = tuple((axis, mesh.shape[axis]) for axis in ("tm", "patch"))

    def per_device(*args):
        heads, frames = args[4].shape
        fits = (
            mesh.shape["tm"] == 4
            and frames == 4
            and args[0].shape[1] == 1
            and heads * LANES == args[0].shape[3]
            and 3 * heads <= 2 * (LANES - 6 * heads)
            and heads % 2 == 0
            and args[0].shape[0] * args[0].shape[2] % (2 * TILE * CHUNKS) == 0
            and mesh.shape["patch"].bit_count() == 1
        )
        return (by_chips if fits else by_heads)(*args, sizes)

    vectors = P(None, "tm", "patch", None)
    return jax.shard_map(
        per_device,
        mesh=mesh,
        in_specs=(vectors,) * 4 + (P(),),
        out_specs=(vectors,) * 3 + (P(),),
        check_vma=False,
    )
```

```python
import functools
import math

import jax
import jax.numpy as jnp
from jax import lax
from jax.experimental import pallas as pl
from jax.experimental.pallas import tpu as pltpu
from jax.sharding import PartitionSpec as P

LANES = 128
TILE = 32
ALIGN = 16
LITTLE = pl.CostEstimate(flops=1, bytes_accessed=1, transcendentals=0)
CHUNKS = 2
FORWARD_MORE = 6


def score_table(bias_rows, frames):
    steps = jnp.arange(frames, dtype=jnp.int32)
    offsets = steps[:, None] - steps[None, :]
    onehot = (offsets[:, :, None] == steps[None, None, :]).astype(jnp.float32)
    table = jnp.einsum("hd,tud->htu", bias_rows, onehot, precision=lax.Precision.HIGHEST)
    return (table, offsets >= 0, onehot)


def attend_back(query_heads, key_heads, value_heads, grad_heads, bias_rows):
    frames = query_heads.shape[1]
    score_scale = 1.0 / math.sqrt(query_heads.shape[4])
    table, causal, onehot = score_table(bias_rows, frames)
    wide = jnp.float32
    scores = (
        jnp.einsum("atxhd,auxhd->axhtu", query_heads, key_heads, preferred_element_type=wide)
        * score_scale
        + table[None, None]
    )
    scores = jnp.where(causal, scores, -jnp.inf)
    row_max = jnp.max(scores, axis=-1, keepdims=True)
    expon = jnp.exp(scores - row_max)
    weights = expon / jnp.sum(expon, axis=-1, keepdims=True)
    weights_low = weights.astype(jnp.bfloat16)
    attended = jnp.einsum(
        "axhtu,auxhd->atxhd", weights_low, value_heads, preferred_element_type=wide
    )
    rowdot = jnp.einsum("atxhd,atxhd->axht", grad_heads, attended, preferred_element_type=wide)
    grad_weights = jnp.einsum(
        "atxhd,auxhd->axhtu", grad_heads, value_heads, preferred_element_type=wide
    )
    grad_scores = weights * (grad_weights - rowdot[..., None])
    bias_terms = jnp.einsum("axhtu,tud->axhd", grad_scores, onehot, precision=lax.Precision.HIGHEST)
    grad_low = grad_scores.astype(jnp.bfloat16)
    grad_query = (
        jnp.einsum("axhtu,auxhd->atxhd", grad_low, key_heads, preferred_element_type=wide)
        * score_scale
    ).astype(jnp.bfloat16)
    grad_key = (
        jnp.einsum("axhtu,atxhd->auxhd", grad_low, query_heads, preferred_element_type=wide)
        * score_scale
    ).astype(jnp.bfloat16)
    grad_value = jnp.einsum(
        "axhtu,atxhd->auxhd", weights_low, grad_heads, preferred_element_type=wide
    ).astype(jnp.bfloat16)
    return (grad_query, grad_key, grad_value, bias_terms)


def sum_everywhere(value, sizes):
    for axis, size in sizes:
        if size & (size - 1):
            value = lax.psum(value, axis)
            continue
        step = 1
        while step < size:
            other = lax.ppermute(value, axis, [(i, i ^ step) for i in range(size)])
            value = value + other
            step *= 2
    return value


def by_heads(query_vectors, key_vectors, value_vectors, grad_output, time_bias, sizes):
    head_count = time_bias.shape[0]
    frames = time_bias.shape[1]
    head_dim = query_vectors.shape[3] // head_count
    split_shape = query_vectors.shape[:3] + (head_count, head_dim)
    local_heads = head_count // lax.axis_size("tm")
    first_head = lax.axis_index("tm") * local_heads
    bias_rows = lax.dynamic_slice_in_dim(time_bias, first_head, local_heads, 0)
    spread = [
        lax.all_to_all(item.reshape(split_shape), "tm", split_axis=3, concat_axis=1, tiled=True)
        for item in (query_vectors, key_vectors, value_vectors, grad_output)
    ]
    *grads, bias_terms = attend_back(*spread, bias_rows)
    grads = [
        lax.all_to_all(item, "tm", split_axis=1, concat_axis=3, tiled=True).reshape(
            query_vectors.shape
        )
        for item in grads
    ]
    partial = lax.dynamic_update_slice_in_dim(
        jnp.zeros((head_count, frames), jnp.float32),
        jnp.sum(bias_terms, axis=(0, 1)),
        first_head,
        0,
    )
    return (*grads, sum_everywhere(partial, sizes))


def pair_dots(queries, keys, grads, values, pairs, heads):
    place = lax.broadcasted_iota(jnp.int32, (TILE, LANES), 1)
    held = [jnp.zeros((TILE, LANES), jnp.float32)] * (2 * len(pairs))
    for head in range(heads):
        at = slice(head * LANES, (head + 1) * LANES)
        here = place == head
        load = lambda refs, used: {j: refs[j][at].astype(jnp.float32) for j in used}
        late, early = {t for t, _ in pairs}, {u for _, u in pairs}
        q, k = load(queries, sorted(late)), load(keys, sorted(early))
        o, v = load(grads, sorted(late)), load(values, sorted(early))
        for j, (t, u) in enumerate(pairs):
            score = jnp.sum(q[t] * k[u], axis=1, keepdims=True)
            held[j] = jnp.where(here, score, held[j])
            gain = jnp.sum(o[t] * v[u], axis=1, keepdims=True)
            held[len(pairs) + j] = jnp.where(here, gain, held[len(pairs) + j])
    return held


def over_tiles(rows, body):
    pl.loop(0, rows // TILE)(lambda i: body(i * TILE))


def tile_at(start):
    return pl.ds(pl.multiple_of(start, TILE), TILE)


class Shifted:
    def __init__(self, ref, start):
        self.ref, self.start = ref, start

    def at_rows(self, row):
        return View(self.ref, tile_at(self.start + row))


class View:
    def __init__(self, ref, rows):
        self.ref, self.rows = ref, rows

    def __getitem__(self, lanes):
        return self.ref[self.rows, lanes]

    def __setitem__(self, lanes, value):
        self.ref[self.rows, lanes] = value


def tiles_of(refs, row):
    return tuple(ref if ref is None else ref.at_rows(row) for ref in refs)


def shifted(refs, start):
    return tuple(ref if ref is None else Shifted(ref, start) for ref in refs)


def soft_row(scores, gains):
    top = functools.reduce(jnp.maximum, scores)
    expon = [jnp.exp(item - top) for item in scores]
    total = functools.reduce(jnp.add, expon)
    weights = [item / total for item in expon]
    low = [item.astype(jnp.bfloat16) for item in weights]
    rowdot = functools.reduce(
        jnp.add, [a.astype(jnp.float32) * g for a, g in zip(low, gains)]
    )
    grads = [w * (g - rowdot) for w, g in zip(weights, gains)]
    return low, grads


LOCAL = ((0, 0), (1, 0), (1, 1))
CROSS = ((0, 0), (0, 1), (1, 0), (1, 1))


def unpack(packed, heads, count=6):
    return [
        packed if j == 0 else pltpu.roll(packed, LANES - heads * j, axis=1) for j in range(count)
    ]


def bias_lines(terms):
    lines = []
    for items in terms:
        lines.append(
            jnp.sum(functools.reduce(jnp.add, items), axis=0, keepdims=True)
            if items
            else jnp.zeros((1, LANES), jnp.float32)
        )
    return jnp.concatenate(lines + [jnp.zeros((4, LANES), jnp.float32)], axis=0)


def early_rows(diag, scale, offset):
    score = lambda j, d: diag[j] * scale + offset[d]
    row0 = soft_row([score(0, 0)], [diag[3]])
    row1 = soft_row([score(1, 1), score(2, 0)], [diag[4], diag[5]])
    return row0, row1


def my_place():
    me = lax.axis_index("tm")
    return lax.rem(me, 2), lax.div(me, 2)


def with_frames(own, other, work):
    core, chip = my_place()
    for at_chip in range(2):
        pl.when((chip == at_chip) & (core == 0))(functools.partial(work, at_chip, own, other))
        pl.when((chip == at_chip) & (core == 1))(functools.partial(work, at_chip, other, own))


def chunk_start(chunk, size):
    return jnp.where(my_place()[1] == 0, chunk, CHUNKS - 1 - chunk) * size


def chunk_copies(sources, core, outs, sems, at=0):
    copies = []
    for c, out in enumerate(outs):
        if out is None:
            continue
        size = out.shape[1]
        start = pl.multiple_of(core * CHUNKS * size + chunk_start(c, size), ALIGN)
        for j, ref in enumerate(sources):
            copies.append(
                pltpu.make_async_copy(
                    ref.at[pl.ds(start, size)], out.at[j], sems.at[at + len(copies)]
                )
            )
    return copies


def copy_chunks(sources, core, outs, sems):
    copies = chunk_copies(sources, core, outs, sems)
    for copy in copies:
        copy.start()
    for copy in copies:
        copy.wait()


def take_far(refs, outs):
    chip = my_place()[1]

    def take(places):
        for out, place in zip(outs, places):
            for row in range(0, out.shape[0], TILE):
                rows = slice(row, row + TILE)
                out[rows, : refs[place].shape[1]] = refs[place][rows, :]

    pl.when(chip == 0)(lambda: take((1, 2)))
    pl.when(chip == 1)(lambda: take((0, 3)))


def fetch_other_kernel(q, k, v, o, other, got, sems):
    core, chip = my_place()

    def fetch(arrays):
        copy_chunks(arrays, 1 - core, (None,) * (CHUNKS - 1) + (got,), sems)
        for j in range(2):
            other[j, :, : got.shape[2]] = got[j]
            other[j, :, got.shape[2] :] = jnp.zeros((other.shape[1], LANES), jnp.bfloat16)

    pl.when(chip == 0)(lambda: fetch((k, v)))
    pl.when(chip == 1)(lambda: fetch((q, o)))


def forward_kernel(came, out):
    size, width = came.shape[1], out.shape[1]
    for j in range(2):
        out[j * size : (j + 1) * size, :] = came[j, :, :width]
    out[2 * size :, :] = jnp.zeros((out.shape[0] - 2 * size, width), jnp.bfloat16)


def fetch_theirs_kernel(q, k, v, o, after, *refs):
    *nears, sems = refs
    core = 1 - my_place()[0]
    copies = chunk_copies((q, k), core, nears[:CHUNKS], sems)
    copies += chunk_copies((v, o), core, nears[CHUNKS:], sems, len(copies))
    for copy in copies:
        copy.start()
    for copy in copies:
        copy.wait()


def fetch_mine_kernel(q, k, v, o, after, *refs):
    copy_chunks((q, k, v, o), my_place()[0], refs[:-1], refs[-1])


def packed_small(value, heads):
    used = 6 * heads
    place = lax.broadcasted_iota(jnp.int32, value.shape, 1)
    high = value.astype(jnp.bfloat16).astype(jnp.float32)
    middle = (value - high).astype(jnp.bfloat16).astype(jnp.float32)
    rest = (value - high) - middle
    first = jnp.where(place < used, high, pltpu.roll(rest, used, axis=1))
    second = jnp.where(place < used, middle, pltpu.roll(rest, 2 * used - LANES, axis=1))
    return first.astype(jnp.bfloat16), second.astype(jnp.bfloat16)


def unpacked_small(first, second, heads):
    used = 6 * heads
    first, second = first.astype(jnp.float32), second.astype(jnp.float32)
    place = lax.broadcasted_iota(jnp.int32, first.shape, 1)
    rest = jnp.where(
        place < LANES - used,
        pltpu.roll(first, LANES - used, axis=1),
        pltpu.roll(second, 2 * (LANES - used), axis=1),
    )
    return first + second + jnp.where(place < 3 * heads, rest, 0.0)


def local_kernel(heads, scale, table, *refs):
    mines, refs = refs[:2], refs[2:]
    nears = [planes(refs[0]) + planes(refs[2]), planes(refs[1]) + planes(refs[3])]
    theirs, refs = planes(refs[4]) + planes(refs[5]), refs[6:]
    smalls, out_bias, other, sames = refs[:2], refs[2], refs[3], [planes(x) for x in refs[4:]]
    core, chip = my_place()
    size, width = mines[0].shape[1:]
    offset = [table[d : d + 1, :] for d in range(4)]
    out_bias[...] = jnp.zeros_like(out_bias)

    def run(a, b, small):
        def tile(row):
            at, bt = tiles_of(a, row), tiles_of(b, row)
            held = pair_dots(
                (at[0], bt[0]), (at[1], bt[1]), (at[3], bt[3]), (at[2], bt[2]), LOCAL, heads
            )
            total = held[0]
            for j in range(1, 6):
                total = total + pltpu.roll(held[j], heads * j, axis=1)
            small[tile_at(row), :] = total
            (_, d0), (_, d1) = early_rows(held, scale, offset)
            lines = bias_lines([[d0[0], d1[1]], [d1[0]], [], []])
            out_bias[...] += jnp.where(chip == 0, lines, jnp.zeros_like(lines))

        over_tiles(size, tile)

    for mine, near, small in zip(mines, nears, smalls):
        own, neighbour = shifted(planes(mine), 0), shifted(near, 0)
        pl.when(core == 0)(functools.partial(run, own, neighbour, small))
        pl.when(core == 1)(functools.partial(run, neighbour, own, small))

    take_far(theirs, planes(other))
    for c, out in enumerate(sames):
        take_far(planes(mines[1 - c]), out)
        for row in range(0, size, TILE):
            rows = slice(row, row + TILE)
            parts = packed_small(smalls[1 - c][rows, :], heads)
            for ref, part in zip(sames[0], parts):
                ref[rows, width + c * LANES : width + (c + 1) * LANES] = part


EARLY, LATE = 14, 10


def cross_sides(chip, a, b):
    if chip == 0:
        return ((a[4], a[5]), (b[4], b[5])), ((a[1], a[2]), (b[1], b[2]))
    return ((a[0], a[3]), (b[0], b[3])), ((a[4], a[5]), (b[4], b[5]))


def far_pairs(chip, parity):
    return [pair for pair in CROSS if pair[chip] == parity]


def cross_dots(queries, keys, pairs, heads):
    return pair_dots(
        [x[0] for x in queries], [x[0] for x in keys],
        [x[1] for x in queries], [x[1] for x in keys], pairs, heads,
    )


def piece_kernel(heads, same, mine, near_first, near_second, *refs):
    far, out = refs[:-1], refs[-1]
    piece = pair_of(far)
    own, other = planes(mine), planes(near_first) + planes(near_second)
    if same:
        own, other = own + piece, other + (None, None)
    else:
        own, other = own + (None, None), other + piece
    own, other = shifted(own, 0), shifted(other, 0)

    def work(chip, a, b):
        parity = int((a is own) != same)

        def tile(row):
            queries, keys = cross_sides(chip, tiles_of(a, row), tiles_of(b, row))
            held = cross_dots(queries, keys, far_pairs(chip, parity), heads)
            total = held[0]
            for j in range(1, 4):
                total = total + pltpu.roll(held[j], heads * j, axis=1)
            out[tile_at(row), :] = total

        over_tiles(out.shape[0], tile)

    with_frames(own, other, work)


def score_tile(heads, scale, chip, a, b, table, small_own, small_far, known, parity):
    offset = [table[d : d + 1, :] for d in range(4)]
    queries, keys = cross_sides(chip, a, b)
    held = [None] * 8
    for pairs, values in (
        (far_pairs(chip, parity), known),
        (far_pairs(chip, 1 - parity), None),
    ):
        if values is None:
            values = cross_dots(queries, keys, pairs, heads)
        for j, pair in enumerate(pairs):
            held[CROSS.index(pair)] = values[j]
            held[4 + CROSS.index(pair)] = values[2 + j]
    diag = unpack(small_far if chip == 0 else small_own, heads)
    score = lambda j, d: held[j] * scale + offset[d]
    p2, d2 = soft_row(
        [score(0, 2), score(1, 1), diag[0] * scale + offset[0]], [held[4], held[5], diag[3]]
    )
    p3, d3 = soft_row(
        [score(2, 3), score(3, 2), diag[1] * scale + offset[1], diag[2] * scale + offset[0]],
        [held[6], held[7], diag[4], diag[5]],
    )
    lines = bias_lines([[d2[2], d3[3]], [d2[1], d3[2]], [d2[0], d3[1]], [d3[0]]])
    if chip == 1:
        items = [d2[2], d3[2], d3[3], d2[0], d2[1], d3[0], d3[1], p2[2], p3[2], p3[3]]
    else:
        (p0, d0), (p1, d1) = early_rows(unpack(small_own, heads), scale, offset)
        items = [d0[0], d1[0], d1[1], d2[0], d2[1], d3[0], d3[1]]
        items += [p0[0], p1[0], p1[1], p2[0], p2[1], p3[0], p3[1]]
    return [item.astype(jnp.bfloat16) for item in items], lines


def gradient_tile(heads, scale, chip, a, b, items, out_a, out_b):
    width = 2 * LANES
    lines = -(-heads // TILE) * TILE
    line = lax.broadcasted_iota(jnp.int32, (lines, width), 0)
    head = lax.broadcasted_iota(jnp.int32, (lines, width), 1) // LANES
    zeros = jnp.zeros((LANES - lines, width), jnp.bfloat16)
    spread = jnp.concatenate(items, axis=0)

    for pair in range(heads // 2):
        at = slice(pair * width, (pair + 1) * width)
        pick = jnp.where(line == 2 * pair + head, 1.0, 0.0).astype(jnp.bfloat16)
        flat = jnp.dot(
            spread, jnp.concatenate([pick, zeros], axis=0), preferred_element_type=jnp.float32
        )
        w = [flat[j * TILE : (j + 1) * TILE, :] for j in range(len(items))]

        def put(ref, value):
            ref[at] = value.astype(jnp.bfloat16)

        def wide(*refs):
            return [ref[at].astype(jnp.float32) for ref in refs]

        if chip == 0:
            ka, kb = wide(a[1], b[1])
            put(out_a[0], w[0] * ka * scale)
            put(out_b[0], (w[1] * ka + w[2] * kb) * scale)
            for to, x, g, rate in ((1, 0, 0, scale), (2, 3, 7, 1.0)):
                xa, xb, x2, x3 = wide(a[x], b[x], a[3 + to], b[3 + to])
                for_a = w[g] * xa + w[g + 1] * xb + w[g + 3] * x2 + w[g + 5] * x3
                for_b = w[g + 2] * xb + w[g + 4] * x2 + w[g + 6] * x3
                put(out_a[to], for_a * rate)
                put(out_b[to], for_b * rate)
        else:
            k2, k3, k0, k1 = wide(a[1], b[1], a[4], b[4])
            put(out_a[0], (w[0] * k2 + w[3] * k0 + w[4] * k1) * scale)
            put(out_b[0], (w[1] * k2 + w[2] * k3 + w[5] * k0 + w[6] * k1) * scale)
            q2, q3, o2, o3 = wide(a[0], b[0], a[3], b[3])
            put(out_a[1], (w[0] * q2 + w[1] * q3) * scale)
            put(out_b[1], w[2] * q3 * scale)
            put(out_a[2], w[7] * o2 + w[8] * o3)
            put(out_b[2], w[9] * o3)


def planes(ref):
    return tuple(ref.at[j] for j in range(ref.shape[0]))


def frames_of(mine, near, same, other):
    near_first, near_second = near
    return (
        shifted(planes(mine) + pair_of(same), 0),
        shifted(planes(near_first) + planes(near_second) + pair_of(other), 0),
    )


def pair_of(piece):
    (ref,) = piece
    if len(ref.shape) == 3:
        return planes(ref)
    return tuple(ref.at[j * TILE * (ref.shape[0] // 2 // TILE) :] for j in range(2))


def far_small(far, rows, width, heads, chunk):
    at = slice(width + chunk * LANES, width + (chunk + 1) * LANES)
    return unpacked_small(*(ref[rows, at] for ref in far), heads)


def score_kernel(heads, scale, known, table, small, bias, mine, *refs):
    near, same, other = refs[:2], refs[2:3], refs[3:4]
    far = pair_of(same)
    (out_items, out_shares, out_small), lines_ref = refs[4:7], refs[7]
    size, width = mine.shape[1:]
    lines_ref[...] = bias[...]
    own, neighbour = frames_of(mine, near, same, other)

    def work(chip, a, b):
        def tile(row):
            rows = tile_at(row)
            items, lines = score_tile(
                heads, scale, chip, tiles_of(a, row), tiles_of(b, row), table,
                small[rows, :], far_small(far, rows, width, heads, 0),
                unpack(known[rows, :], heads, 4), int(a is own),
            )
            out_small[rows, :] = far_small(far, rows, width, heads, 1)
            for j, item in enumerate(items):
                out_items[j, rows, :] = item
            lines_ref[...] += lines

        over_tiles(size, tile)

    with_frames(own, neighbour, work)
    for j in range(out_shares.shape[0]):
        out_shares[j] = lines_ref[: out_shares.shape[1], :]


def output_copies(which, piece, outs, chunk, sems, at, offset=0):
    half = outs[0].shape[0] // 2
    start = which * half + chunk_start(chunk, half // CHUNKS) + offset
    rows = pl.ds(pl.multiple_of(start, ALIGN), piece[0].shape[0])
    return [
        pltpu.make_async_copy(part, out.at[rows], sems.at[at + j])
        for j, (part, out) in enumerate(zip(piece, outs))
    ]


def gradient_kernel(heads, scale, items_ref, mine, *refs):
    near, same, other, refs = refs[:2], refs[2:3], refs[3:4], refs[4:]
    out_others, outs, kept, given, sems = refs[:2], refs[2:5], *refs[5:]
    own, neighbour = frames_of(mine, near, same, other)
    own_out, other_out = shifted(planes(kept), 0), shifted(planes(given), 0)

    def work(chip, a, b):
        out_a, out_b = (own_out, other_out) if a is own else (other_out, own_out)

        def tile(row):
            items = [items_ref[j, tile_at(row), :] for j in range(LATE if chip else EARLY)]
            gradient_tile(
                heads, scale, chip, tiles_of(a, row), tiles_of(b, row), items,
                tiles_of(out_a, row), tiles_of(out_b, row),
            )

        over_tiles(mine.shape[1], tile)

    with_frames(own, neighbour, work)
    copies = output_copies(my_place()[0], planes(kept), outs, 0, sems, 0)
    for copy in copies:
        copy.start()
    start = 0
    for out in out_others:
        for j in range(3):
            out[j] = given[j, start : start + out.shape[1], :]
        start += out.shape[1]
    for copy in copies:
        copy.wait()


def whole_kernel(heads, scale, known, table, small, small_far, mine, *refs):
    near, same, other, out_own, out_others = refs[:2], refs[2:3], refs[3:4], refs[4], refs[5:]
    own, neighbour = frames_of(mine, near, same, other)
    own_out, other_out = shifted(planes(out_own), 0), shifted(out_others, 0)

    def work(chip, a, b):
        out_a, out_b = (own_out, other_out) if a is own else (other_out, own_out)

        def tile(row):
            at, bt, rows = tiles_of(a, row), tiles_of(b, row), tile_at(row)
            items, _ = score_tile(
                heads, scale, chip, at, bt, table, small[rows, :], small_far[rows, :],
                unpack(known[rows, :], heads, 4), int(a is not own),
            )
            gradient_tile(
                heads, scale, chip, at, bt, items, tiles_of(out_a, row), tiles_of(out_b, row)
            )

        over_tiles(mine.shape[1], tile)

    with_frames(own, neighbour, work)


def early_output_kernel(*refs):
    first_backs, kept, outs, sems = refs[:2], planes(refs[2]), refs[6:9], refs[9]
    core = my_place()[0]
    copies = output_copies(core, kept, outs, 1, sems, 0)
    offset = 0
    for j, ref in enumerate(first_backs):
        copies += output_copies(1 - core, planes(ref), outs, 0, sems, 3 + 3 * j, offset)
        offset += ref.shape[1]
    for copy in copies:
        copy.start()
    for copy in copies:
        copy.wait()


def output_kernel(*refs):
    back, shares, outs, out_bias, total, sems = refs[:3], refs[3], refs[7:10], *refs[10:]
    copies = output_copies(1 - my_place()[0], back, outs, 1, sems, 0)
    for copy in copies:
        copy.start()
    parts = [shares[j] for j in range(shares.shape[0])]
    while len(parts) > 1:
        parts = [a + b for a, b in zip(parts[::2], parts[1::2])]
    total[...] = parts[0][: total.shape[0], : total.shape[1]]
    copies.append(pltpu.make_async_copy(total, out_bias, sems.at[len(copies)]))
    copies[-1].start()
    for copy in copies:
        copy.wait()


def by_chips(query_vectors, key_vectors, value_vectors, grad_output, time_bias, sizes):
    heads, frames = time_bias.shape
    clips, _, patches, width = query_vectors.shape
    rows = clips * patches
    half = rows // 2
    size = half // CHUNKS
    scale = 1.0 / math.sqrt(width // heads)
    own = [
        pltpu.with_memory_space_constraint(x.reshape(rows, width), pltpu.HBM)
        for x in (query_vectors, key_vectors, value_vectors, grad_output)
    ]
    vmem_spec = pl.BlockSpec(memory_space=pltpu.VMEM)
    any_spec = pl.BlockSpec(memory_space=pl.ANY)

    def swap(x, bits):
        return lax.ppermute(x, "tm", [(i, i ^ bits) for i in range(4)])

    def shape(*dims, dtype=jnp.bfloat16):
        return jax.ShapeDtypeStruct(dims, dtype)

    def call(kernel, name, out_shape, *args, scratch=(), hbm=(), hbm_out=(), aliases={}):
        return pl.pallas_call(
            kernel,
            in_specs=[any_spec if j in hbm else vmem_spec for j in range(len(args))],
            out_specs=[any_spec if j in hbm_out else vmem_spec for j in range(len(out_shape))],
            out_shape=out_shape,
            scratch_shapes=scratch,
            input_output_aliases=aliases,
            compiler_params=pltpu.CompilerParams(vmem_limit_bytes=16 * 2**20),
            cost_estimate=LITTLE,
            name=name,
        )(*args)

    wide = jnp.float32
    lines = shape(8, LANES, dtype=wide)
    chunk_shape, far_shape = shape(4, size, width), shape(2, size, width)
    copies = [pltpu.SemaphoreType.DMA((4 * CHUNKS,))]
    table = jnp.pad(time_bias.T, ((0, 8 - frames), (0, LANES - heads)))

    pair = shape(2, size, width)
    (other,) = call(
        fetch_other_kernel, "fetch_other", [shape(2, size, width + LANES)], *own,
        scratch=[pltpu.VMEM((2, size, width), jnp.bfloat16)] + copies, hbm=range(4),
    )
    came = swap(other, 2)
    theirs = call(
        fetch_theirs_kernel, "fetch_theirs", [pair] * (2 * CHUNKS), *own, other,
        scratch=copies, hbm=range(5),
    )
    nears = [swap(x, 1) for x in theirs]
    mines = call(
        fetch_mine_kernel, "fetch_mine", [chunk_shape] * CHUNKS, *own, theirs[0],
        scratch=copies, hbm=range(5),
    )
    (forward,) = call(forward_kernel, "forward", [shape(2 * size + FORWARD_MORE, width)], came)
    others = [[swap(forward, 1)]]

    *smalls, bias, other, same_first, same = call(
        functools.partial(local_kernel, heads, scale),
        "local_scores",
        [shape(size, LANES, dtype=wide)] * CHUNKS
        + [lines, far_shape]
        + [shape(2, size, width + CHUNKS * LANES), far_shape],
        table, *mines, *nears, theirs[0], theirs[CHUNKS],
    )
    sames = [[swap(same_first, 2)], [swap(same, 2)]]
    others.append([swap(other, 3)])

    whole = pltpu.HBM((rows, width), jnp.bfloat16)
    stack, piece = shape(3, size, width), shape(size, width)
    output_sems = pltpu.SemaphoreType.DMA((13,))
    first = (mines[0], nears[0], nears[CHUNKS], *sames[0], *others[0])
    (known,) = call(
        functools.partial(piece_kernel, heads, False),
        "first_dots",
        [shape(size, LANES, dtype=wide)],
        mines[0], nears[0], nears[CHUNKS], *others[0],
    )
    items, shares, small_far = call(
        functools.partial(score_kernel, heads, scale),
        "scores",
        [
            shape(EARLY, size, LANES),
            shape(math.prod(count for _, count in sizes), 8, LANES, dtype=wide),
            shape(size, LANES, dtype=wide),
        ],
        known, table, smalls[0], bias, *first,
        scratch=[pltpu.VMEM((8, LANES), wide)],
    )
    shares = lax.all_to_all(shares, tuple(axis for axis, _ in sizes), 0, 0, tiled=True)
    *back, grad_queries, grad_keys, grad_values = call(
        functools.partial(gradient_kernel, heads, scale),
        "gradients",
        [shape(3, size // 2, width)] * 2 + [whole] * 3,
        items, *first,
        scratch=[pltpu.VMEM((3, size, width), jnp.bfloat16)] * 2 + [output_sems],
        hbm_out=range(2, 5),
    )
    grads = (grad_queries, grad_keys, grad_values)
    first_backs = [swap(x, 1) for x in back]

    (known_last,) = call(
        functools.partial(piece_kernel, heads, True),
        "last_dots",
        [shape(size, LANES, dtype=wide)],
        mines[1], nears[1], nears[CHUNKS + 1], *sames[1],
    )
    kept, *back = call(
        functools.partial(whole_kernel, heads, scale),
        "scores_and_gradients",
        [stack] + [piece] * 3,
        known_last, table, smalls[1], small_far, mines[1], nears[1], nears[CHUNKS + 1],
        *sames[1], *others[1],
    )
    back = [swap(x, 1) for x in back]
    in_hbm = lambda arrays: [pltpu.with_memory_space_constraint(x, pltpu.HBM) for x in arrays]
    grads = call(
        early_output_kernel,
        "early_outputs",
        [whole] * 3,
        *first_backs, kept, *in_hbm(grads),
        scratch=[output_sems],
        hbm=range(3, 6),
        hbm_out=range(3),
        aliases={3 + j: j for j in range(3)},
    )
    *grads, bias = call(
        output_kernel,
        "outputs",
        [whole] * 3 + [shape(frames, heads, dtype=wide)],
        *back, shares, *in_hbm(grads),
        scratch=[pltpu.VMEM((frames, heads), wide), output_sems],
        hbm=range(4, 7),
        hbm_out=range(4),
        aliases={4 + j: j for j in range(3)},
    )
    return (*[x.reshape(query_vectors.shape) for x in grads], bias.T)


def solution(mesh):
    sizes = tuple((axis, mesh.shape[axis]) for axis in ("tm", "patch"))

    def per_device(*args):
        heads, frames = args[4].shape
        fits = (
            mesh.shape["tm"] == 4
            and frames == 4
            and args[0].shape[1] == 1
            and heads * LANES == args[0].shape[3]
            and 3 * heads <= 2 * (LANES - 6 * heads)
            and heads % 2 == 0
            and args[0].shape[0] * args[0].shape[2] % (2 * TILE * CHUNKS) == 0
            and mesh.shape["patch"].bit_count() == 1
        )
        return (by_chips if fits else by_heads)(*args, sizes)

    vectors = P(None, "tm", "patch", None)
    return jax.shard_map(
        per_device,
        mesh=mesh,
        in_specs=(vectors,) * 4 + (P(),),
        out_specs=(vectors,) * 3 + (P(),),
        check_vma=False,
    )
```

```python
import functools
import math

import jax
import jax.numpy as jnp
from jax import lax
from jax.experimental import pallas as pl
from jax.experimental.pallas import tpu as pltpu
from jax.sharding import PartitionSpec as P

LANES = 128
TILE = 32
ALIGN = 16
LITTLE = pl.CostEstimate(flops=1, bytes_accessed=1, transcendentals=0)
CHUNKS = 2


def score_table(bias_rows, frames):
    steps = jnp.arange(frames, dtype=jnp.int32)
    offsets = steps[:, None] - steps[None, :]
    onehot = (offsets[:, :, None] == steps[None, None, :]).astype(jnp.float32)
    table = jnp.einsum("hd,tud->htu", bias_rows, onehot, precision=lax.Precision.HIGHEST)
    return (table, offsets >= 0, onehot)


def attend_back(query_heads, key_heads, value_heads, grad_heads, bias_rows):
    frames = query_heads.shape[1]
    score_scale = 1.0 / math.sqrt(query_heads.shape[4])
    table, causal, onehot = score_table(bias_rows, frames)
    wide = jnp.float32
    scores = (
        jnp.einsum("atxhd,auxhd->axhtu", query_heads, key_heads, preferred_element_type=wide)
        * score_scale
        + table[None, None]
    )
    scores = jnp.where(causal, scores, -jnp.inf)
    row_max = jnp.max(scores, axis=-1, keepdims=True)
    expon = jnp.exp(scores - row_max)
    weights = expon / jnp.sum(expon, axis=-1, keepdims=True)
    weights_low = weights.astype(jnp.bfloat16)
    attended = jnp.einsum(
        "axhtu,auxhd->atxhd", weights_low, value_heads, preferred_element_type=wide
    )
    rowdot = jnp.einsum("atxhd,atxhd->axht", grad_heads, attended, preferred_element_type=wide)
    grad_weights = jnp.einsum(
        "atxhd,auxhd->axhtu", grad_heads, value_heads, preferred_element_type=wide
    )
    grad_scores = weights * (grad_weights - rowdot[..., None])
    bias_terms = jnp.einsum("axhtu,tud->axhd", grad_scores, onehot, precision=lax.Precision.HIGHEST)
    grad_low = grad_scores.astype(jnp.bfloat16)
    grad_query = (
        jnp.einsum("axhtu,auxhd->atxhd", grad_low, key_heads, preferred_element_type=wide)
        * score_scale
    ).astype(jnp.bfloat16)
    grad_key = (
        jnp.einsum("axhtu,atxhd->auxhd", grad_low, query_heads, preferred_element_type=wide)
        * score_scale
    ).astype(jnp.bfloat16)
    grad_value = jnp.einsum(
        "axhtu,atxhd->auxhd", weights_low, grad_heads, preferred_element_type=wide
    ).astype(jnp.bfloat16)
    return (grad_query, grad_key, grad_value, bias_terms)


def sum_everywhere(value, sizes):
    for axis, size in sizes:
        if size & (size - 1):
            value = lax.psum(value, axis)
            continue
        step = 1
        while step < size:
            other = lax.ppermute(value, axis, [(i, i ^ step) for i in range(size)])
            value = value + other
            step *= 2
    return value


def by_heads(query_vectors, key_vectors, value_vectors, grad_output, time_bias, sizes):
    head_count = time_bias.shape[0]
    frames = time_bias.shape[1]
    head_dim = query_vectors.shape[3] // head_count
    split_shape = query_vectors.shape[:3] + (head_count, head_dim)
    local_heads = head_count // lax.axis_size("tm")
    first_head = lax.axis_index("tm") * local_heads
    bias_rows = lax.dynamic_slice_in_dim(time_bias, first_head, local_heads, 0)
    spread = [
        lax.all_to_all(item.reshape(split_shape), "tm", split_axis=3, concat_axis=1, tiled=True)
        for item in (query_vectors, key_vectors, value_vectors, grad_output)
    ]
    *grads, bias_terms = attend_back(*spread, bias_rows)
    grads = [
        lax.all_to_all(item, "tm", split_axis=1, concat_axis=3, tiled=True).reshape(
            query_vectors.shape
        )
        for item in grads
    ]
    partial = lax.dynamic_update_slice_in_dim(
        jnp.zeros((head_count, frames), jnp.float32),
        jnp.sum(bias_terms, axis=(0, 1)),
        first_head,
        0,
    )
    return (*grads, sum_everywhere(partial, sizes))


def pair_dots(queries, keys, grads, values, pairs, heads):
    place = lax.broadcasted_iota(jnp.int32, (TILE, LANES), 1)
    held = [jnp.zeros((TILE, LANES), jnp.float32)] * (2 * len(pairs))
    for head in range(heads):
        at = slice(head * LANES, (head + 1) * LANES)
        here = place == head
        load = lambda refs, used: {j: refs[j][at].astype(jnp.float32) for j in used}
        late, early = {t for t, _ in pairs}, {u for _, u in pairs}
        q, k = load(queries, sorted(late)), load(keys, sorted(early))
        o, v = load(grads, sorted(late)), load(values, sorted(early))
        for j, (t, u) in enumerate(pairs):
            score = jnp.sum(q[t] * k[u], axis=1, keepdims=True)
            held[j] = jnp.where(here, score, held[j])
            gain = jnp.sum(o[t] * v[u], axis=1, keepdims=True)
            held[len(pairs) + j] = jnp.where(here, gain, held[len(pairs) + j])
    return held


def over_tiles(rows, body):
    pl.loop(0, rows // TILE)(lambda i: body(i * TILE))


def tile_at(start):
    return pl.ds(pl.multiple_of(start, TILE), TILE)


class Shifted:
    def __init__(self, ref, start):
        self.ref, self.start = ref, start

    def at_rows(self, row):
        return View(self.ref, tile_at(self.start + row))


class View:
    def __init__(self, ref, rows):
        self.ref, self.rows = ref, rows

    def __getitem__(self, lanes):
        return self.ref[self.rows, lanes]

    def __setitem__(self, lanes, value):
        self.ref[self.rows, lanes] = value


def tiles_of(refs, row):
    return tuple(ref if ref is None else ref.at_rows(row) for ref in refs)


def shifted(refs, start):
    return tuple(ref if ref is None else Shifted(ref, start) for ref in refs)


def soft_row(scores, gains):
    top = functools.reduce(jnp.maximum, scores)
    expon = [jnp.exp(item - top) for item in scores]
    total = functools.reduce(jnp.add, expon)
    weights = [item / total for item in expon]
    low = [item.astype(jnp.bfloat16) for item in weights]
    rowdot = functools.reduce(
        jnp.add, [a.astype(jnp.float32) * g for a, g in zip(low, gains)]
    )
    grads = [w * (g - rowdot) for w, g in zip(weights, gains)]
    return low, grads


LOCAL = ((0, 0), (1, 0), (1, 1))
CROSS = ((0, 0), (0, 1), (1, 0), (1, 1))


def unpack(packed, heads, count=6):
    return [
        packed if j == 0 else pltpu.roll(packed, LANES - heads * j, axis=1) for j in range(count)
    ]


def bias_lines(terms):
    lines = []
    for items in terms:
        lines.append(
            jnp.sum(functools.reduce(jnp.add, items), axis=0, keepdims=True)
            if items
            else jnp.zeros((1, LANES), jnp.float32)
        )
    return jnp.concatenate(lines + [jnp.zeros((4, LANES), jnp.float32)], axis=0)


def early_rows(diag, scale, offset):
    score = lambda j, d: diag[j] * scale + offset[d]
    row0 = soft_row([score(0, 0)], [diag[3]])
    row1 = soft_row([score(1, 1), score(2, 0)], [diag[4], diag[5]])
    return row0, row1


def my_place():
    me = lax.axis_index("tm")
    return lax.rem(me, 2), lax.div(me, 2)


def with_frames(own, other, work):
    core, chip = my_place()
    for at_chip in range(2):
        pl.when((chip == at_chip) & (core == 0))(functools.partial(work, at_chip, own, other))
        pl.when((chip == at_chip) & (core == 1))(functools.partial(work, at_chip, other, own))


def chunk_start(chunk, size):
    return jnp.where(my_place()[1] == 0, chunk, CHUNKS - 1 - chunk) * size


def copy_chunks(sources, core, outs, sems):
    size = outs[0].shape[1]
    copies = []
    for c, out in enumerate(outs):
        start = pl.multiple_of(core * CHUNKS * size + chunk_start(c, size), TILE)
        for j, ref in enumerate(sources):
            copies.append(
                pltpu.make_async_copy(
                    ref.at[pl.ds(start, size)], out.at[j], sems.at[len(copies)]
                )
            )
    for copy in copies:
        copy.start()
    for copy in copies:
        copy.wait()


def take_far(refs, outs):
    chip = my_place()[1]

    def take(places):
        for out, place in zip(outs, places):
            for row in range(0, out.shape[0], TILE):
                rows = slice(row, row + TILE)
                out[rows, : refs[place].shape[1]] = refs[place][rows, :]

    pl.when(chip == 0)(lambda: take((1, 2)))
    pl.when(chip == 1)(lambda: take((0, 3)))


def fetch_theirs_kernel(q, k, v, o, *refs):
    nears, other, sems = refs[:CHUNKS], refs[CHUNKS], refs[CHUNKS + 1]
    copy_chunks((q, k, v, o), 1 - my_place()[0], nears, sems)
    take_far(planes(nears[CHUNKS - 1]), planes(other))


def fetch_mine_kernel(q, k, v, o, after, *refs):
    copy_chunks((q, k, v, o), my_place()[0], refs[:-1], refs[-1])


def packed_small(value, heads):
    used = 6 * heads
    place = lax.broadcasted_iota(jnp.int32, value.shape, 1)
    high = value.astype(jnp.bfloat16).astype(jnp.float32)
    middle = (value - high).astype(jnp.bfloat16).astype(jnp.float32)
    rest = (value - high) - middle
    first = jnp.where(place < used, high, pltpu.roll(rest, used, axis=1))
    second = jnp.where(place < used, middle, pltpu.roll(rest, 2 * used - LANES, axis=1))
    return first.astype(jnp.bfloat16), second.astype(jnp.bfloat16)


def unpacked_small(first, second, heads):
    used = 6 * heads
    first, second = first.astype(jnp.float32), second.astype(jnp.float32)
    place = lax.broadcasted_iota(jnp.int32, first.shape, 1)
    rest = jnp.where(
        place < LANES - used,
        pltpu.roll(first, LANES - used, axis=1),
        pltpu.roll(second, 2 * (LANES - used), axis=1),
    )
    return first + second + jnp.where(place < 3 * heads, rest, 0.0)


def local_kernel(heads, scale, table, *refs):
    mines, nears, theirs, refs = refs[:2], refs[2:4], refs[4], refs[5:]
    smalls, out_bias, other, sames = refs[:2], refs[2], refs[3], (refs[4:6], planes(refs[6]))
    core, chip = my_place()
    size, width = mines[0].shape[1:]
    offset = [table[d : d + 1, :] for d in range(4)]
    out_bias[...] = jnp.zeros_like(out_bias)

    def run(a, b, small):
        def tile(row):
            at, bt = tiles_of(a, row), tiles_of(b, row)
            held = pair_dots(
                (at[0], bt[0]), (at[1], bt[1]), (at[3], bt[3]), (at[2], bt[2]), LOCAL, heads
            )
            total = held[0]
            for j in range(1, 6):
                total = total + pltpu.roll(held[j], heads * j, axis=1)
            small[tile_at(row), :] = total
            (_, d0), (_, d1) = early_rows(held, scale, offset)
            lines = bias_lines([[d0[0], d1[1]], [d1[0]], [], []])
            out_bias[...] += jnp.where(chip == 0, lines, jnp.zeros_like(lines))

        over_tiles(size, tile)

    for mine, near, small in zip(mines, nears, smalls):
        own, neighbour = shifted(planes(mine), 0), shifted(planes(near), 0)
        pl.when(core == 0)(functools.partial(run, own, neighbour, small))
        pl.when(core == 1)(functools.partial(run, neighbour, own, small))

    take_far(planes(theirs), planes(other))
    for c, out in enumerate(sames):
        take_far(planes(mines[1 - c]), out)
        for row in range(0, size, TILE):
            rows = slice(row, row + TILE)
            parts = packed_small(smalls[1 - c][rows, :], heads)
            for ref, part in zip(sames[0], parts):
                ref[rows, width + c * LANES : width + (c + 1) * LANES] = part


EARLY, LATE = 14, 10


def cross_sides(chip, a, b):
    if chip == 0:
        return ((a[4], a[5]), (b[4], b[5])), ((a[1], a[2]), (b[1], b[2]))
    return ((a[0], a[3]), (b[0], b[3])), ((a[4], a[5]), (b[4], b[5]))


def far_pairs(chip, parity):
    return [pair for pair in CROSS if pair[chip] == parity]


def cross_dots(queries, keys, pairs, heads):
    return pair_dots(
        [x[0] for x in queries], [x[0] for x in keys],
        [x[1] for x in queries], [x[1] for x in keys], pairs, heads,
    )


def piece_kernel(heads, same, mine, near, *refs):
    far, out = refs[:-1], refs[-1]
    piece = far if len(far) == 2 else planes(far[0])
    own, other = planes(mine), planes(near)
    if same:
        own, other = own + piece, other + (None, None)
    else:
        own, other = own + (None, None), other + piece
    own, other = shifted(own, 0), shifted(other, 0)

    def work(chip, a, b):
        parity = int((a is own) != same)

        def tile(row):
            queries, keys = cross_sides(chip, tiles_of(a, row), tiles_of(b, row))
            held = cross_dots(queries, keys, far_pairs(chip, parity), heads)
            total = held[0]
            for j in range(1, 4):
                total = total + pltpu.roll(held[j], heads * j, axis=1)
            out[tile_at(row), :] = total

        over_tiles(out.shape[0], tile)

    with_frames(own, other, work)


def score_tile(heads, scale, chip, a, b, table, small_own, small_far, known, parity):
    offset = [table[d : d + 1, :] for d in range(4)]
    queries, keys = cross_sides(chip, a, b)
    held = [None] * 8
    for pairs, values in (
        (far_pairs(chip, parity), known),
        (far_pairs(chip, 1 - parity), None),
    ):
        if values is None:
            values = cross_dots(queries, keys, pairs, heads)
        for j, pair in enumerate(pairs):
            held[CROSS.index(pair)] = values[j]
            held[4 + CROSS.index(pair)] = values[2 + j]
    diag = unpack(small_far if chip == 0 else small_own, heads)
    score = lambda j, d: held[j] * scale + offset[d]
    p2, d2 = soft_row(
        [score(0, 2), score(1, 1), diag[0] * scale + offset[0]], [held[4], held[5], diag[3]]
    )
    p3, d3 = soft_row(
        [score(2, 3), score(3, 2), diag[1] * scale + offset[1], diag[2] * scale + offset[0]],
        [held[6], held[7], diag[4], diag[5]],
    )
    lines = bias_lines([[d2[2], d3[3]], [d2[1], d3[2]], [d2[0], d3[1]], [d3[0]]])
    if chip == 1:
        items = [d2[2], d3[2], d3[3], d2[0], d2[1], d3[0], d3[1], p2[2], p3[2], p3[3]]
    else:
        (p0, d0), (p1, d1) = early_rows(unpack(small_own, heads), scale, offset)
        items = [d0[0], d1[0], d1[1], d2[0], d2[1], d3[0], d3[1]]
        items += [p0[0], p1[0], p1[1], p2[0], p2[1], p3[0], p3[1]]
    return [item.astype(jnp.bfloat16) for item in items], lines


def gradient_tile(heads, scale, chip, a, b, items, out_a, out_b):
    width = 2 * LANES
    lines = -(-heads // TILE) * TILE
    line = lax.broadcasted_iota(jnp.int32, (lines, width), 0)
    head = lax.broadcasted_iota(jnp.int32, (lines, width), 1) // LANES
    zeros = jnp.zeros((LANES - lines, width), jnp.bfloat16)
    spread = jnp.concatenate(items, axis=0)

    for pair in range(heads // 2):
        at = slice(pair * width, (pair + 1) * width)
        pick = jnp.where(line == 2 * pair + head, 1.0, 0.0).astype(jnp.bfloat16)
        flat = jnp.dot(
            spread, jnp.concatenate([pick, zeros], axis=0), preferred_element_type=jnp.float32
        )
        w = [flat[j * TILE : (j + 1) * TILE, :] for j in range(len(items))]

        def put(ref, value):
            ref[at] = value.astype(jnp.bfloat16)

        def wide(*refs):
            return [ref[at].astype(jnp.float32) for ref in refs]

        if chip == 0:
            ka, kb = wide(a[1], b[1])
            put(out_a[0], w[0] * ka * scale)
            put(out_b[0], (w[1] * ka + w[2] * kb) * scale)
            for to, x, g, rate in ((1, 0, 0, scale), (2, 3, 7, 1.0)):
                xa, xb, x2, x3 = wide(a[x], b[x], a[3 + to], b[3 + to])
                for_a = w[g] * xa + w[g + 1] * xb + w[g + 3] * x2 + w[g + 5] * x3
                for_b = w[g + 2] * xb + w[g + 4] * x2 + w[g + 6] * x3
                put(out_a[to], for_a * rate)
                put(out_b[to], for_b * rate)
        else:
            k2, k3, k0, k1 = wide(a[1], b[1], a[4], b[4])
            put(out_a[0], (w[0] * k2 + w[3] * k0 + w[4] * k1) * scale)
            put(out_b[0], (w[1] * k2 + w[2] * k3 + w[5] * k0 + w[6] * k1) * scale)
            q2, q3, o2, o3 = wide(a[0], b[0], a[3], b[3])
            put(out_a[1], (w[0] * q2 + w[1] * q3) * scale)
            put(out_b[1], w[2] * q3 * scale)
            put(out_a[2], w[7] * o2 + w[8] * o3)
            put(out_b[2], w[9] * o3)


def planes(ref):
    return tuple(ref.at[j] for j in range(ref.shape[0]))


def frames_of(mine, near, far):
    *same, other = far
    return (
        shifted(planes(mine) + pair_of(same), 0),
        shifted(planes(near) + planes(other), 0),
    )


def pair_of(same):
    return tuple(same) if len(same) == 2 else planes(same[0])


def far_small(far, rows, width, heads, chunk):
    at = slice(width + chunk * LANES, width + (chunk + 1) * LANES)
    return unpacked_small(*(ref[rows, at] for ref in pair_of(far[:-1])), heads)


def score_kernel(heads, scale, known, table, small, bias, mine, near, *refs):
    far, (out_items, out_shares, out_small), lines_ref = refs[:3], refs[3:6], refs[6]
    size, width = mine.shape[1:]
    lines_ref[...] = bias[...]
    own, neighbour = frames_of(mine, near, far)

    def work(chip, a, b):
        def tile(row):
            rows = tile_at(row)
            items, lines = score_tile(
                heads, scale, chip, tiles_of(a, row), tiles_of(b, row), table,
                small[rows, :], far_small(far, rows, width, heads, 0),
                unpack(known[rows, :], heads, 4), int(a is own),
            )
            out_small[rows, :] = far_small(far, rows, width, heads, 1)
            for j, item in enumerate(items):
                out_items[j, rows, :] = item
            lines_ref[...] += lines

        over_tiles(size, tile)

    with_frames(own, neighbour, work)
    for j in range(out_shares.shape[0]):
        out_shares[j] = lines_ref[: out_shares.shape[1], :]


def output_copies(which, piece, outs, chunk, sems, at, offset=0):
    half = outs[0].shape[0] // 2
    start = which * half + chunk_start(chunk, half // CHUNKS) + offset
    rows = pl.ds(pl.multiple_of(start, ALIGN), piece[0].shape[0])
    return [
        pltpu.make_async_copy(part, out.at[rows], sems.at[at + j])
        for j, (part, out) in enumerate(zip(piece, outs))
    ]


def gradient_kernel(heads, scale, items_ref, mine, near, *refs):
    far, out_others, outs, kept, given, sems = refs[:3], refs[3:5], refs[5:8], *refs[8:]
    own, neighbour = frames_of(mine, near, far)
    own_out, other_out = shifted(planes(kept), 0), shifted(planes(given), 0)

    def work(chip, a, b):
        out_a, out_b = (own_out, other_out) if a is own else (other_out, own_out)

        def tile(row):
            items = [items_ref[j, tile_at(row), :] for j in range(LATE if chip else EARLY)]
            gradient_tile(
                heads, scale, chip, tiles_of(a, row), tiles_of(b, row), items,
                tiles_of(out_a, row), tiles_of(out_b, row),
            )

        over_tiles(mine.shape[1], tile)

    with_frames(own, neighbour, work)
    copies = output_copies(my_place()[0], planes(kept), outs, 0, sems, 0)
    for copy in copies:
        copy.start()
    start = 0
    for out in out_others:
        for j in range(3):
            out[j] = given[j, start : start + out.shape[1], :]
        start += out.shape[1]
    for copy in copies:
        copy.wait()


def whole_kernel(heads, scale, known, table, small, small_far, mine, near, *refs):
    far, out_own, out_others = refs[:2], refs[2], refs[3:6]
    own, neighbour = frames_of(mine, near, far)
    own_out, other_out = shifted(planes(out_own), 0), shifted(out_others, 0)

    def work(chip, a, b):
        out_a, out_b = (own_out, other_out) if a is own else (other_out, own_out)

        def tile(row):
            at, bt, rows = tiles_of(a, row), tiles_of(b, row), tile_at(row)
            items, _ = score_tile(
                heads, scale, chip, at, bt, table, small[rows, :], small_far[rows, :],
                unpack(known[rows, :], heads, 4), int(a is not own),
            )
            gradient_tile(
                heads, scale, chip, at, bt, items, tiles_of(out_a, row), tiles_of(out_b, row)
            )

        over_tiles(mine.shape[1], tile)

    with_frames(own, neighbour, work)


def early_output_kernel(*refs):
    first_backs, kept, outs, sems = refs[:2], planes(refs[2]), refs[6:9], refs[9]
    core = my_place()[0]
    copies = output_copies(core, kept, outs, 1, sems, 0)
    offset = 0
    for j, ref in enumerate(first_backs):
        copies += output_copies(1 - core, planes(ref), outs, 0, sems, 3 + 3 * j, offset)
        offset += ref.shape[1]
    for copy in copies:
        copy.start()
    for copy in copies:
        copy.wait()


def output_kernel(*refs):
    back, shares, outs, out_bias, total, sems = refs[:3], refs[3], refs[7:10], *refs[10:]
    copies = output_copies(1 - my_place()[0], back, outs, 1, sems, 0)
    for copy in copies:
        copy.start()
    parts = [shares[j] for j in range(shares.shape[0])]
    while len(parts) > 1:
        parts = [a + b for a, b in zip(parts[::2], parts[1::2])]
    total[...] = parts[0][: total.shape[0], : total.shape[1]]
    copies.append(pltpu.make_async_copy(total, out_bias, sems.at[len(copies)]))
    copies[-1].start()
    for copy in copies:
        copy.wait()


def by_chips(query_vectors, key_vectors, value_vectors, grad_output, time_bias, sizes):
    heads, frames = time_bias.shape
    clips, _, patches, width = query_vectors.shape
    rows = clips * patches
    half = rows // 2
    size = half // CHUNKS
    scale = 1.0 / math.sqrt(width // heads)
    own = [
        pltpu.with_memory_space_constraint(x.reshape(rows, width), pltpu.HBM)
        for x in (query_vectors, key_vectors, value_vectors, grad_output)
    ]
    vmem_spec = pl.BlockSpec(memory_space=pltpu.VMEM)
    any_spec = pl.BlockSpec(memory_space=pl.ANY)

    def swap(x, bits):
        return lax.ppermute(x, "tm", [(i, i ^ bits) for i in range(4)])

    def shape(*dims, dtype=jnp.bfloat16):
        return jax.ShapeDtypeStruct(dims, dtype)

    def call(kernel, name, out_shape, *args, scratch=(), hbm=(), hbm_out=(), aliases={}):
        return pl.pallas_call(
            kernel,
            in_specs=[any_spec if j in hbm else vmem_spec for j in range(len(args))],
            out_specs=[any_spec if j in hbm_out else vmem_spec for j in range(len(out_shape))],
            out_shape=out_shape,
            scratch_shapes=scratch,
            input_output_aliases=aliases,
            compiler_params=pltpu.CompilerParams(vmem_limit_bytes=16 * 2**20),
            cost_estimate=LITTLE,
            name=name,
        )(*args)

    wide = jnp.float32
    lines = shape(8, LANES, dtype=wide)
    chunk_shape, far_shape = shape(4, size, width), shape(2, size, width)
    copies = [pltpu.SemaphoreType.DMA((4 * CHUNKS,))]
    table = jnp.pad(time_bias.T, ((0, 8 - frames), (0, LANES - heads)))

    *theirs, other = call(
        fetch_theirs_kernel, "fetch_theirs", [chunk_shape] * CHUNKS + [far_shape], *own,
        scratch=copies, hbm=range(4),
    )
    nears = [swap(x, 1) for x in theirs]
    others = [swap(other, 3)]
    mines = call(
        fetch_mine_kernel, "fetch_mine", [chunk_shape] * CHUNKS, *own, other,
        scratch=copies, hbm=range(5),
    )

    *smalls, bias, other, same_first, same_second, same = call(
        functools.partial(local_kernel, heads, scale),
        "local_scores",
        [shape(size, LANES, dtype=wide)] * CHUNKS
        + [lines, far_shape]
        + [shape(size, width + CHUNKS * LANES)] * 2
        + [far_shape],
        table, *mines, *nears, theirs[0],
    )
    sames = [[swap(same_first, 2), swap(same_second, 2)], [swap(same, 2)]]
    others.append(swap(other, 3))

    whole = pltpu.HBM((rows, width), jnp.bfloat16)
    stack, piece = shape(3, size, width), shape(size, width)
    output_sems = pltpu.SemaphoreType.DMA((13,))
    first = (mines[0], nears[0], *sames[0], others[0])
    (known,) = call(
        functools.partial(piece_kernel, heads, False),
        "first_dots",
        [shape(size, LANES, dtype=wide)],
        mines[0], nears[0], others[0],
    )
    items, shares, small_far = call(
        functools.partial(score_kernel, heads, scale),
        "scores",
        [
            shape(EARLY, size, LANES),
            shape(math.prod(count for _, count in sizes), 8, LANES, dtype=wide),
            shape(size, LANES, dtype=wide),
        ],
        known, table, smalls[0], bias, *first,
        scratch=[pltpu.VMEM((8, LANES), wide)],
    )
    shares = lax.all_to_all(shares, tuple(axis for axis, _ in sizes[::-1]), 0, 0, tiled=True)
    *back, grad_queries, grad_keys, grad_values = call(
        functools.partial(gradient_kernel, heads, scale),
        "gradients",
        [shape(3, size // 2, width)] * 2 + [whole] * 3,
        items, *first,
        scratch=[pltpu.VMEM((3, size, width), jnp.bfloat16)] * 2 + [output_sems],
        hbm_out=range(2, 5),
    )
    grads = (grad_queries, grad_keys, grad_values)
    first_backs = [swap(x, 1) for x in back]

    (known_last,) = call(
        functools.partial(piece_kernel, heads, True),
        "last_dots",
        [shape(size, LANES, dtype=wide)],
        mines[1], nears[1], *sames[1],
    )
    kept, *back = call(
        functools.partial(whole_kernel, heads, scale),
        "scores_and_gradients",
        [stack] + [piece] * 3,
        known_last, table, smalls[1], small_far, mines[1], nears[1], *sames[1], others[1],
    )
    back = [swap(x, 1) for x in back]
    in_hbm = lambda arrays: [pltpu.with_memory_space_constraint(x, pltpu.HBM) for x in arrays]
    grads = call(
        early_output_kernel,
        "early_outputs",
        [whole] * 3,
        *first_backs, kept, *in_hbm(grads),
        scratch=[output_sems],
        hbm=range(3, 6),
        hbm_out=range(3),
        aliases={3 + j: j for j in range(3)},
    )
    *grads, bias = call(
        output_kernel,
        "outputs",
        [whole] * 3 + [shape(frames, heads, dtype=wide)],
        *back, shares, *in_hbm(grads),
        scratch=[pltpu.VMEM((frames, heads), wide), output_sems],
        hbm=range(4, 7),
        hbm_out=range(4),
        aliases={4 + j: j for j in range(3)},
    )
    return (*[x.reshape(query_vectors.shape) for x in grads], bias.T)


def solution(mesh):
    sizes = tuple((axis, mesh.shape[axis]) for axis in ("tm", "patch"))

    def per_device(*args):
        heads, frames = args[4].shape
        fits = (
            mesh.shape["tm"] == 4
            and frames == 4
            and args[0].shape[1] == 1
            and heads * LANES == args[0].shape[3]
            and 3 * heads <= 2 * (LANES - 6 * heads)
            and heads % 2 == 0
            and args[0].shape[0] * args[0].shape[2] % (2 * TILE * CHUNKS) == 0
            and mesh.shape["patch"].bit_count() == 1
        )
        return (by_chips if fits else by_heads)(*args, sizes)

    vectors = P(None, "tm", "patch", None)
    return jax.shard_map(
        per_device,
        mesh=mesh,
        in_specs=(vectors,) * 4 + (P(),),
        out_specs=(vectors,) * 3 + (P(),),
        check_vma=False,
    )
```

```python
import functools
import math

import jax
import jax.numpy as jnp
from jax import lax
from jax.experimental import pallas as pl
from jax.experimental.pallas import tpu as pltpu
from jax.sharding import PartitionSpec as P

LANES = 128
TILE = 32
ALIGN = 16
LITTLE = pl.CostEstimate(flops=1, bytes_accessed=1, transcendentals=0)
CHUNKS = 2


def score_table(bias_rows, frames):
    steps = jnp.arange(frames, dtype=jnp.int32)
    offsets = steps[:, None] - steps[None, :]
    onehot = (offsets[:, :, None] == steps[None, None, :]).astype(jnp.float32)
    table = jnp.einsum("hd,tud->htu", bias_rows, onehot, precision=lax.Precision.HIGHEST)
    return (table, offsets >= 0, onehot)


def attend_back(query_heads, key_heads, value_heads, grad_heads, bias_rows):
    frames = query_heads.shape[1]
    score_scale = 1.0 / math.sqrt(query_heads.shape[4])
    table, causal, onehot = score_table(bias_rows, frames)
    wide = jnp.float32
    scores = (
        jnp.einsum("atxhd,auxhd->axhtu", query_heads, key_heads, preferred_element_type=wide)
        * score_scale
        + table[None, None]
    )
    scores = jnp.where(causal, scores, -jnp.inf)
    row_max = jnp.max(scores, axis=-1, keepdims=True)
    expon = jnp.exp(scores - row_max)
    weights = expon / jnp.sum(expon, axis=-1, keepdims=True)
    weights_low = weights.astype(jnp.bfloat16)
    attended = jnp.einsum(
        "axhtu,auxhd->atxhd", weights_low, value_heads, preferred_element_type=wide
    )
    rowdot = jnp.einsum("atxhd,atxhd->axht", grad_heads, attended, preferred_element_type=wide)
    grad_weights = jnp.einsum(
        "atxhd,auxhd->axhtu", grad_heads, value_heads, preferred_element_type=wide
    )
    grad_scores = weights * (grad_weights - rowdot[..., None])
    bias_terms = jnp.einsum("axhtu,tud->axhd", grad_scores, onehot, precision=lax.Precision.HIGHEST)
    grad_low = grad_scores.astype(jnp.bfloat16)
    grad_query = (
        jnp.einsum("axhtu,auxhd->atxhd", grad_low, key_heads, preferred_element_type=wide)
        * score_scale
    ).astype(jnp.bfloat16)
    grad_key = (
        jnp.einsum("axhtu,atxhd->auxhd", grad_low, query_heads, preferred_element_type=wide)
        * score_scale
    ).astype(jnp.bfloat16)
    grad_value = jnp.einsum(
        "axhtu,atxhd->auxhd", weights_low, grad_heads, preferred_element_type=wide
    ).astype(jnp.bfloat16)
    return (grad_query, grad_key, grad_value, bias_terms)


def sum_everywhere(value, sizes):
    for axis, size in sizes:
        if size & (size - 1):
            value = lax.psum(value, axis)
            continue
        step = 1
        while step < size:
            other = lax.ppermute(value, axis, [(i, i ^ step) for i in range(size)])
            value = value + other
            step *= 2
    return value


def by_heads(query_vectors, key_vectors, value_vectors, grad_output, time_bias, sizes):
    head_count = time_bias.shape[0]
    frames = time_bias.shape[1]
    head_dim = query_vectors.shape[3] // head_count
    split_shape = query_vectors.shape[:3] + (head_count, head_dim)
    local_heads = head_count // lax.axis_size("tm")
    first_head = lax.axis_index("tm") * local_heads
    bias_rows = lax.dynamic_slice_in_dim(time_bias, first_head, local_heads, 0)
    spread = [
        lax.all_to_all(item.reshape(split_shape), "tm", split_axis=3, concat_axis=1, tiled=True)
        for item in (query_vectors, key_vectors, value_vectors, grad_output)
    ]
    *grads, bias_terms = attend_back(*spread, bias_rows)
    grads = [
        lax.all_to_all(item, "tm", split_axis=1, concat_axis=3, tiled=True).reshape(
            query_vectors.shape
        )
        for item in grads
    ]
    partial = lax.dynamic_update_slice_in_dim(
        jnp.zeros((head_count, frames), jnp.float32),
        jnp.sum(bias_terms, axis=(0, 1)),
        first_head,
        0,
    )
    return (*grads, sum_everywhere(partial, sizes))


def pair_dots(queries, keys, grads, values, pairs, heads):
    place = lax.broadcasted_iota(jnp.int32, (TILE, LANES), 1)
    held = [jnp.zeros((TILE, LANES), jnp.float32)] * (2 * len(pairs))
    for head in range(heads):
        at = slice(head * LANES, (head + 1) * LANES)
        here = place == head
        load = lambda refs, used: {j: refs[j][at].astype(jnp.float32) for j in used}
        late, early = {t for t, _ in pairs}, {u for _, u in pairs}
        q, k = load(queries, sorted(late)), load(keys, sorted(early))
        o, v = load(grads, sorted(late)), load(values, sorted(early))
        for j, (t, u) in enumerate(pairs):
            score = jnp.sum(q[t] * k[u], axis=1, keepdims=True)
            held[j] = jnp.where(here, score, held[j])
            gain = jnp.sum(o[t] * v[u], axis=1, keepdims=True)
            held[len(pairs) + j] = jnp.where(here, gain, held[len(pairs) + j])
    return held


def over_tiles(rows, body):
    pl.loop(0, rows // TILE)(lambda i: body(i * TILE))


def tile_at(start):
    return pl.ds(pl.multiple_of(start, TILE), TILE)


class Shifted:
    def __init__(self, ref, start):
        self.ref, self.start = ref, start

    def at_rows(self, row):
        return View(self.ref, tile_at(self.start + row))


class View:
    def __init__(self, ref, rows):
        self.ref, self.rows = ref, rows

    def __getitem__(self, lanes):
        return self.ref[self.rows, lanes]

    def __setitem__(self, lanes, value):
        self.ref[self.rows, lanes] = value


def tiles_of(refs, row):
    return tuple(ref if ref is None else ref.at_rows(row) for ref in refs)


def shifted(refs, start):
    return tuple(ref if ref is None else Shifted(ref, start) for ref in refs)


def soft_row(scores, gains):
    top = functools.reduce(jnp.maximum, scores)
    expon = [jnp.exp(item - top) for item in scores]
    total = functools.reduce(jnp.add, expon)
    weights = [item / total for item in expon]
    low = [item.astype(jnp.bfloat16) for item in weights]
    rowdot = functools.reduce(
        jnp.add, [a.astype(jnp.float32) * g for a, g in zip(low, gains)]
    )
    grads = [w * (g - rowdot) for w, g in zip(weights, gains)]
    return low, grads


LOCAL = ((0, 0), (1, 0), (1, 1))
CROSS = ((0, 0), (0, 1), (1, 0), (1, 1))


def unpack(packed, heads, count=6):
    return [
        packed if j == 0 else pltpu.roll(packed, LANES - heads * j, axis=1) for j in range(count)
    ]


def bias_lines(terms):
    lines = []
    for items in terms:
        lines.append(
            jnp.sum(functools.reduce(jnp.add, items), axis=0, keepdims=True)
            if items
            else jnp.zeros((1, LANES), jnp.float32)
        )
    return jnp.concatenate(lines + [jnp.zeros((4, LANES), jnp.float32)], axis=0)


def early_rows(diag, scale, offset):
    score = lambda j, d: diag[j] * scale + offset[d]
    row0 = soft_row([score(0, 0)], [diag[3]])
    row1 = soft_row([score(1, 1), score(2, 0)], [diag[4], diag[5]])
    return row0, row1


def my_place():
    me = lax.axis_index("tm")
    return lax.rem(me, 2), lax.div(me, 2)


def with_frames(own, other, work):
    core, chip = my_place()
    for at_chip in range(2):
        pl.when((chip == at_chip) & (core == 0))(functools.partial(work, at_chip, own, other))
        pl.when((chip == at_chip) & (core == 1))(functools.partial(work, at_chip, other, own))


def chunk_start(chunk, size):
    return jnp.where(my_place()[1] == 0, chunk, CHUNKS - 1 - chunk) * size


def copy_chunks(sources, core, outs, sems):
    size = outs[0].shape[1]
    copies = []
    for c, out in enumerate(outs):
        start = pl.multiple_of(core * CHUNKS * size + chunk_start(c, size), TILE)
        for j, ref in enumerate(sources):
            copies.append(
                pltpu.make_async_copy(
                    ref.at[pl.ds(start, size)], out.at[j], sems.at[len(copies)]
                )
            )
    for copy in copies:
        copy.start()
    for copy in copies:
        copy.wait()


def take_far(refs, outs):
    chip = my_place()[1]

    def take(places):
        for out, place in zip(outs, places):
            for row in range(0, out.shape[0], TILE):
                rows = slice(row, row + TILE)
                out[rows, : refs[place].shape[1]] = refs[place][rows, :]

    pl.when(chip == 0)(lambda: take((1, 2)))
    pl.when(chip == 1)(lambda: take((0, 3)))


def fetch_theirs_kernel(q, k, v, o, *refs):
    nears, other, sems = refs[:CHUNKS], refs[CHUNKS], refs[CHUNKS + 1]
    copy_chunks((q, k, v, o), 1 - my_place()[0], nears, sems)
    take_far(planes(nears[CHUNKS - 1]), planes(other))


def fetch_mine_kernel(q, k, v, o, after, *refs):
    copy_chunks((q, k, v, o), my_place()[0], refs[:-1], refs[-1])


def packed_small(value, heads):
    used = 6 * heads
    place = lax.broadcasted_iota(jnp.int32, value.shape, 1)
    high = value.astype(jnp.bfloat16).astype(jnp.float32)
    middle = (value - high).astype(jnp.bfloat16).astype(jnp.float32)
    rest = (value - high) - middle
    first = jnp.where(place < used, high, pltpu.roll(rest, used, axis=1))
    second = jnp.where(place < used, middle, pltpu.roll(rest, 2 * used - LANES, axis=1))
    return first.astype(jnp.bfloat16), second.astype(jnp.bfloat16)


def unpacked_small(first, second, heads):
    used = 6 * heads
    first, second = first.astype(jnp.float32), second.astype(jnp.float32)
    place = lax.broadcasted_iota(jnp.int32, first.shape, 1)
    rest = jnp.where(
        place < LANES - used,
        pltpu.roll(first, LANES - used, axis=1),
        pltpu.roll(second, 2 * (LANES - used), axis=1),
    )
    return first + second + jnp.where(place < 3 * heads, rest, 0.0)


def local_kernel(heads, scale, table, *refs):
    mines, nears, smalls, out_bias, same = refs[:2], refs[2:4], refs[4:6], refs[6], refs[7:]
    core, chip = my_place()
    size, width = mines[0].shape[1:]
    offset = [table[d : d + 1, :] for d in range(4)]
    out_bias[...] = jnp.zeros_like(out_bias)

    def run(a, b, small):
        def tile(row):
            at, bt = tiles_of(a, row), tiles_of(b, row)
            held = pair_dots(
                (at[0], bt[0]), (at[1], bt[1]), (at[3], bt[3]), (at[2], bt[2]), LOCAL, heads
            )
            total = held[0]
            for j in range(1, 6):
                total = total + pltpu.roll(held[j], heads * j, axis=1)
            small[tile_at(row), :] = total
            (_, d0), (_, d1) = early_rows(held, scale, offset)
            lines = bias_lines([[d0[0], d1[1]], [d1[0]], [], []])
            out_bias[...] += jnp.where(chip == 0, lines, jnp.zeros_like(lines))

        over_tiles(size, tile)

    for mine, near, small in zip(mines, nears, smalls):
        own, neighbour = shifted(planes(mine), 0), shifted(planes(near), 0)
        pl.when(core == 0)(functools.partial(run, own, neighbour, small))
        pl.when(core == 1)(functools.partial(run, neighbour, own, small))

    take_far(planes(mines[1]), same)
    for c in range(CHUNKS):
        for row in range(0, size, TILE):
            rows = slice(row, row + TILE)
            parts = packed_small(smalls[1 - c][rows, :], heads)
            for ref, part in zip(same, parts):
                ref[rows, width + c * LANES : width + (c + 1) * LANES] = part


def pack_kernel(after, mine, theirs, same, other):
    take_far(planes(mine), planes(same))
    take_far(planes(theirs), planes(other))


EARLY, LATE = 14, 10


def cross_sides(chip, a, b):
    if chip == 0:
        return ((a[4], a[5]), (b[4], b[5])), ((a[1], a[2]), (b[1], b[2]))
    return ((a[0], a[3]), (b[0], b[3])), ((a[4], a[5]), (b[4], b[5]))


def far_pairs(chip, parity):
    return [pair for pair in CROSS if pair[chip] == parity]


def cross_dots(queries, keys, pairs, heads):
    return pair_dots(
        [x[0] for x in queries], [x[0] for x in keys],
        [x[1] for x in queries], [x[1] for x in keys], pairs, heads,
    )


def piece_kernel(heads, same, mine, near, *refs):
    far, out = refs[:-1], refs[-1]
    piece = far if len(far) == 2 else planes(far[0])
    own, other = planes(mine), planes(near)
    if same:
        own, other = own + piece, other + (None, None)
    else:
        own, other = own + (None, None), other + piece
    own, other = shifted(own, 0), shifted(other, 0)

    def work(chip, a, b):
        parity = int((a is own) != same)

        def tile(row):
            queries, keys = cross_sides(chip, tiles_of(a, row), tiles_of(b, row))
            held = cross_dots(queries, keys, far_pairs(chip, parity), heads)
            total = held[0]
            for j in range(1, 4):
                total = total + pltpu.roll(held[j], heads * j, axis=1)
            out[tile_at(row), :] = total

        over_tiles(out.shape[0], tile)

    with_frames(own, other, work)


def score_tile(heads, scale, chip, a, b, table, small_own, small_far, known, parity):
    offset = [table[d : d + 1, :] for d in range(4)]
    queries, keys = cross_sides(chip, a, b)
    held = [None] * 8
    for pairs, values in (
        (far_pairs(chip, parity), known),
        (far_pairs(chip, 1 - parity), None),
    ):
        if values is None:
            values = cross_dots(queries, keys, pairs, heads)
        for j, pair in enumerate(pairs):
            held[CROSS.index(pair)] = values[j]
            held[4 + CROSS.index(pair)] = values[2 + j]
    diag = unpack(small_far if chip == 0 else small_own, heads)
    score = lambda j, d: held[j] * scale + offset[d]
    p2, d2 = soft_row(
        [score(0, 2), score(1, 1), diag[0] * scale + offset[0]], [held[4], held[5], diag[3]]
    )
    p3, d3 = soft_row(
        [score(2, 3), score(3, 2), diag[1] * scale + offset[1], diag[2] * scale + offset[0]],
        [held[6], held[7], diag[4], diag[5]],
    )
    lines = bias_lines([[d2[2], d3[3]], [d2[1], d3[2]], [d2[0], d3[1]], [d3[0]]])
    if chip == 1:
        items = [d2[2], d3[2], d3[3], d2[0], d2[1], d3[0], d3[1], p2[2], p3[2], p3[3]]
    else:
        (p0, d0), (p1, d1) = early_rows(unpack(small_own, heads), scale, offset)
        items = [d0[0], d1[0], d1[1], d2[0], d2[1], d3[0], d3[1]]
        items += [p0[0], p1[0], p1[1], p2[0], p2[1], p3[0], p3[1]]
    return [item.astype(jnp.bfloat16) for item in items], lines


def gradient_tile(heads, scale, chip, a, b, items, out_a, out_b):
    width = 2 * LANES
    lines = -(-heads // TILE) * TILE
    line = lax.broadcasted_iota(jnp.int32, (lines, width), 0)
    head = lax.broadcasted_iota(jnp.int32, (lines, width), 1) // LANES
    zeros = jnp.zeros((LANES - lines, width), jnp.bfloat16)
    spread = jnp.concatenate(items, axis=0)

    for pair in range(heads // 2):
        at = slice(pair * width, (pair + 1) * width)
        pick = jnp.where(line == 2 * pair + head, 1.0, 0.0).astype(jnp.bfloat16)
        flat = jnp.dot(
            spread, jnp.concatenate([pick, zeros], axis=0), preferred_element_type=jnp.float32
        )
        w = [flat[j * TILE : (j + 1) * TILE, :] for j in range(len(items))]

        def put(ref, value):
            ref[at] = value.astype(jnp.bfloat16)

        def wide(*refs):
            return [ref[at].astype(jnp.float32) for ref in refs]

        if chip == 0:
            ka, kb = wide(a[1], b[1])
            put(out_a[0], w[0] * ka * scale)
            put(out_b[0], (w[1] * ka + w[2] * kb) * scale)
            for to, x, g, rate in ((1, 0, 0, scale), (2, 3, 7, 1.0)):
                xa, xb, x2, x3 = wide(a[x], b[x], a[3 + to], b[3 + to])
                for_a = w[g] * xa + w[g + 1] * xb + w[g + 3] * x2 + w[g + 5] * x3
                for_b = w[g + 2] * xb + w[g + 4] * x2 + w[g + 6] * x3
                put(out_a[to], for_a * rate)
                put(out_b[to], for_b * rate)
        else:
            k2, k3, k0, k1 = wide(a[1], b[1], a[4], b[4])
            put(out_a[0], (w[0] * k2 + w[3] * k0 + w[4] * k1) * scale)
            put(out_b[0], (w[1] * k2 + w[2] * k3 + w[5] * k0 + w[6] * k1) * scale)
            q2, q3, o2, o3 = wide(a[0], b[0], a[3], b[3])
            put(out_a[1], (w[0] * q2 + w[1] * q3) * scale)
            put(out_b[1], w[2] * q3 * scale)
            put(out_a[2], w[7] * o2 + w[8] * o3)
            put(out_b[2], w[9] * o3)


def planes(ref):
    return tuple(ref.at[j] for j in range(ref.shape[0]))


def frames_of(mine, near, far):
    *same, other = far
    return (
        shifted(planes(mine) + pair_of(same), 0),
        shifted(planes(near) + planes(other), 0),
    )


def pair_of(same):
    return tuple(same) if len(same) == 2 else planes(same[0])


def far_small(far, rows, width, heads, chunk):
    at = slice(width + chunk * LANES, width + (chunk + 1) * LANES)
    return unpacked_small(*(ref[rows, at] for ref in pair_of(far[:-1])), heads)


def score_kernel(heads, scale, known, table, small, bias, mine, near, *refs):
    far, (out_items, out_shares, out_small), lines_ref = refs[:3], refs[3:6], refs[6]
    size, width = mine.shape[1:]
    lines_ref[...] = bias[...]
    own, neighbour = frames_of(mine, near, far)

    def work(chip, a, b):
        def tile(row):
            rows = tile_at(row)
            items, lines = score_tile(
                heads, scale, chip, tiles_of(a, row), tiles_of(b, row), table,
                small[rows, :], far_small(far, rows, width, heads, 0),
                unpack(known[rows, :], heads, 4), int(a is own),
            )
            out_small[rows, :] = far_small(far, rows, width, heads, 1)
            for j, item in enumerate(items):
                out_items[j, rows, :] = item
            lines_ref[...] += lines

        over_tiles(size, tile)

    with_frames(own, neighbour, work)
    for j in range(out_shares.shape[0]):
        out_shares[j] = lines_ref[: out_shares.shape[1], :]


def output_copies(which, piece, outs, chunk, sems, at, offset=0):
    half = outs[0].shape[0] // 2
    start = which * half + chunk_start(chunk, half // CHUNKS) + offset
    rows = pl.ds(pl.multiple_of(start, ALIGN), piece[0].shape[0])
    return [
        pltpu.make_async_copy(part, out.at[rows], sems.at[at + j])
        for j, (part, out) in enumerate(zip(piece, outs))
    ]


def gradient_kernel(heads, scale, items_ref, mine, near, *refs):
    far, out_others, outs, kept, given, sems = refs[:3], refs[3:5], refs[5:8], *refs[8:]
    own, neighbour = frames_of(mine, near, far)
    own_out, other_out = shifted(planes(kept), 0), shifted(planes(given), 0)

    def work(chip, a, b):
        out_a, out_b = (own_out, other_out) if a is own else (other_out, own_out)

        def tile(row):
            items = [items_ref[j, tile_at(row), :] for j in range(LATE if chip else EARLY)]
            gradient_tile(
                heads, scale, chip, tiles_of(a, row), tiles_of(b, row), items,
                tiles_of(out_a, row), tiles_of(out_b, row),
            )

        over_tiles(mine.shape[1], tile)

    with_frames(own, neighbour, work)
    copies = output_copies(my_place()[0], planes(kept), outs, 0, sems, 0)
    for copy in copies:
        copy.start()
    start = 0
    for out in out_others:
        for j in range(3):
            out[j] = given[j, start : start + out.shape[1], :]
        start += out.shape[1]
    for copy in copies:
        copy.wait()


def whole_kernel(heads, scale, known, table, small, small_far, mine, near, *refs):
    far, out_own, out_others = refs[:2], refs[2], refs[3:6]
    own, neighbour = frames_of(mine, near, far)
    own_out, other_out = shifted(planes(out_own), 0), shifted(out_others, 0)

    def work(chip, a, b):
        out_a, out_b = (own_out, other_out) if a is own else (other_out, own_out)

        def tile(row):
            at, bt, rows = tiles_of(a, row), tiles_of(b, row), tile_at(row)
            items, _ = score_tile(
                heads, scale, chip, at, bt, table, small[rows, :], small_far[rows, :],
                unpack(known[rows, :], heads, 4), int(a is not own),
            )
            gradient_tile(
                heads, scale, chip, at, bt, items, tiles_of(out_a, row), tiles_of(out_b, row)
            )

        over_tiles(mine.shape[1], tile)

    with_frames(own, neighbour, work)


def early_output_kernel(*refs):
    first_backs, kept, outs, sems = refs[:2], planes(refs[2]), refs[6:9], refs[9]
    core = my_place()[0]
    copies = output_copies(core, kept, outs, 1, sems, 0)
    offset = 0
    for j, ref in enumerate(first_backs):
        copies += output_copies(1 - core, planes(ref), outs, 0, sems, 3 + 3 * j, offset)
        offset += ref.shape[1]
    for copy in copies:
        copy.start()
    for copy in copies:
        copy.wait()


def output_kernel(*refs):
    back, shares, outs, out_bias, total, sems = refs[:3], refs[3], refs[7:10], *refs[10:]
    copies = output_copies(1 - my_place()[0], back, outs, 1, sems, 0)
    for copy in copies:
        copy.start()
    parts = [shares[j] for j in range(shares.shape[0])]
    while len(parts) > 1:
        parts = [a + b for a, b in zip(parts[::2], parts[1::2])]
    total[...] = parts[0][: total.shape[0], : total.shape[1]]
    copies.append(pltpu.make_async_copy(total, out_bias, sems.at[len(copies)]))
    copies[-1].start()
    for copy in copies:
        copy.wait()


def by_chips(query_vectors, key_vectors, value_vectors, grad_output, time_bias, sizes):
    heads, frames = time_bias.shape
    clips, _, patches, width = query_vectors.shape
    rows = clips * patches
    half = rows // 2
    size = half // CHUNKS
    scale = 1.0 / math.sqrt(width // heads)
    own = [
        pltpu.with_memory_space_constraint(x.reshape(rows, width), pltpu.HBM)
        for x in (query_vectors, key_vectors, value_vectors, grad_output)
    ]
    vmem_spec = pl.BlockSpec(memory_space=pltpu.VMEM)
    any_spec = pl.BlockSpec(memory_space=pl.ANY)

    def swap(x, bits):
        return lax.ppermute(x, "tm", [(i, i ^ bits) for i in range(4)])

    def shape(*dims, dtype=jnp.bfloat16):
        return jax.ShapeDtypeStruct(dims, dtype)

    def call(kernel, name, out_shape, *args, scratch=(), hbm=(), hbm_out=(), aliases={}):
        return pl.pallas_call(
            kernel,
            in_specs=[any_spec if j in hbm else vmem_spec for j in range(len(args))],
            out_specs=[any_spec if j in hbm_out else vmem_spec for j in range(len(out_shape))],
            out_shape=out_shape,
            scratch_shapes=scratch,
            input_output_aliases=aliases,
            compiler_params=pltpu.CompilerParams(vmem_limit_bytes=16 * 2**20),
            cost_estimate=LITTLE,
            name=name,
        )(*args)

    wide = jnp.float32
    lines = shape(8, LANES, dtype=wide)
    chunk_shape, far_shape = shape(4, size, width), shape(2, size, width)
    copies = [pltpu.SemaphoreType.DMA((4 * CHUNKS,))]
    table = jnp.pad(time_bias.T, ((0, 8 - frames), (0, LANES - heads)))

    *theirs, other = call(
        fetch_theirs_kernel, "fetch_theirs", [chunk_shape] * CHUNKS + [far_shape], *own,
        scratch=copies, hbm=range(4),
    )
    nears = [swap(x, 1) for x in theirs]
    others = [swap(other, 3)]
    mines = call(
        fetch_mine_kernel, "fetch_mine", [chunk_shape] * CHUNKS, *own, other,
        scratch=copies, hbm=range(5),
    )

    *smalls, bias, same_first, same_second = call(
        functools.partial(local_kernel, heads, scale),
        "local_scores",
        [shape(size, LANES, dtype=wide)] * CHUNKS
        + [lines]
        + [shape(size, width + CHUNKS * LANES)] * 2,
        table, *mines, *nears,
    )
    sames = [[swap(same_first, 2), swap(same_second, 2)]]

    whole = pltpu.HBM((rows, width), jnp.bfloat16)
    stack, piece = shape(3, size, width), shape(size, width)
    output_sems = pltpu.SemaphoreType.DMA((13,))
    first = (mines[0], nears[0], *sames[0], others[0])
    (known,) = call(
        functools.partial(piece_kernel, heads, False),
        "first_dots",
        [shape(size, LANES, dtype=wide)],
        mines[0], nears[0], others[0],
    )
    same, other = call(pack_kernel, "pack", [far_shape] * 2, known, mines[0], theirs[0])
    sames.append([swap(same, 2)])
    others.append(swap(other, 3))
    items, shares, small_far = call(
        functools.partial(score_kernel, heads, scale),
        "scores",
        [
            shape(EARLY, size, LANES),
            shape(math.prod(count for _, count in sizes), 8, LANES, dtype=wide),
            shape(size, LANES, dtype=wide),
        ],
        known, table, smalls[0], bias, *first,
        scratch=[pltpu.VMEM((8, LANES), wide)],
    )
    shares = lax.all_to_all(shares, tuple(axis for axis, _ in sizes), 0, 0, tiled=True)
    *back, grad_queries, grad_keys, grad_values = call(
        functools.partial(gradient_kernel, heads, scale),
        "gradients",
        [shape(3, size // 2, width)] * 2 + [whole] * 3,
        items, *first,
        scratch=[pltpu.VMEM((3, size, width), jnp.bfloat16)] * 2 + [output_sems],
        hbm_out=range(2, 5),
    )
    grads = (grad_queries, grad_keys, grad_values)
    first_backs = [swap(x, 1) for x in back]

    (known_last,) = call(
        functools.partial(piece_kernel, heads, True),
        "last_dots",
        [shape(size, LANES, dtype=wide)],
        mines[1], nears[1], *sames[1],
    )
    kept, *back = call(
        functools.partial(whole_kernel, heads, scale),
        "scores_and_gradients",
        [stack] + [piece] * 3,
        known_last, table, smalls[1], small_far, mines[1], nears[1], *sames[1], others[1],
    )
    back = [swap(x, 1) for x in back]
    in_hbm = lambda arrays: [pltpu.with_memory_space_constraint(x, pltpu.HBM) for x in arrays]
    grads = call(
        early_output_kernel,
        "early_outputs",
        [whole] * 3,
        *first_backs, kept, *in_hbm(grads),
        scratch=[output_sems],
        hbm=range(3, 6),
        hbm_out=range(3),
        aliases={3 + j: j for j in range(3)},
    )
    *grads, bias = call(
        output_kernel,
        "outputs",
        [whole] * 3 + [shape(frames, heads, dtype=wide)],
        *back, shares, *in_hbm(grads),
        scratch=[pltpu.VMEM((frames, heads), wide), output_sems],
        hbm=range(4, 7),
        hbm_out=range(4),
        aliases={4 + j: j for j in range(3)},
    )
    return (*[x.reshape(query_vectors.shape) for x in grads], bias.T)


def solution(mesh):
    sizes = tuple((axis, mesh.shape[axis]) for axis in ("tm", "patch"))

    def per_device(*args):
        heads, frames = args[4].shape
        fits = (
            mesh.shape["tm"] == 4
            and frames == 4
            and args[0].shape[1] == 1
            and heads * LANES == args[0].shape[3]
            and 3 * heads <= 2 * (LANES - 6 * heads)
            and heads % 2 == 0
            and args[0].shape[0] * args[0].shape[2] % (2 * TILE * CHUNKS) == 0
            and mesh.shape["patch"].bit_count() == 1
        )
        return (by_chips if fits else by_heads)(*args, sizes)

    vectors = P(None, "tm", "patch", None)
    return jax.shard_map(
        per_device,
        mesh=mesh,
        in_specs=(vectors,) * 4 + (P(),),
        out_specs=(vectors,) * 3 + (P(),),
        check_vma=False,
    )
```
